512 devices in a mesh: gx: 16 (over x, y), gy: 16 (over z), ens: 2 (over core).
Axes of the slice: x: 4, y: 4, z: 16, core: 2. Of those that a mesh axis runs over, the one named last changes fastest.
Arguments:
- concentration: float32 [2, 4, 512, 2048], P('ens', None, 'gx', 'gy'), may hold values from 0 to 2
- cotangent: float32 [2, 4, 512, 2048], P('ens', None, 'gx', 'gy'), may hold values from -6 to 6
- vel_x: float32 [512, 2048], P('gx', 'gy'), may hold values from -2 to 2
- vel_y: float32 [512, 2048], P('gx', 'gy'), may hold values from -2 to 2
- dispersion: float32 [512, 2048], P('gx', 'gy'), may hold values from 1 to 10000
- wet_cells: int32 [512, 2048], P('gx', 'gy'), may hold values from 0 to 1
- decay_rate: float32 [4], replicated, may hold values from 0.05 to 1
- emission: float32 [4, 8192], replicated, may hold values from 2 to 40
- source_cell: int32 [8192], replicated, may hold values from 0 to 1048575
Outputs:
- state_next: float32 [2, 4, 512, 2048], P('ens', None, 'gx', 'gy')
- adjoint_state: float32 [2, 4, 512, 2048], P('ens', None, 'gx', 'gy')
- emission_grad: float32 [4, 8192], replicated
The draws below stay inside these ranges and needn't reach their ends.
Inputs may be any that keep to these rules, and one draw needn't show every extreme that they name: `source_cell`: flat cell index, row * 2048 + column; several sources may share a cell.
All inputs are finite; a program needn't handle non-finite values.
Results may differ from the reference program's by a relative error of at most 0.0003.
Values sent between devices are 32-bit elements; how exact they have to be, the bound alone decides.
A program may use at most 64 MiB of HBM per device.

```python
import math
import jax
import jax.numpy as jnp
from jax import lax

TR = 4
NSRC = 8192
MEMBERS = 2
NX = 512
NY = 2048


def draw_wet_cells(key, part):
    key = jax.random.fold_in(key, 7)
    rows = jax.lax.broadcasted_iota(jnp.int32, (NX, NY), 0)
    cols = jax.lax.broadcasted_iota(jnp.int32, (NX, NY), 1)
    land = jnp.zeros((NX, NY), jnp.bool_)
    tall_most = max(2, NX // 16)
    wide_most = max(2, NY // 16)
    for block_index in range(16):
        block_key = jax.random.fold_in(key, block_index)
        keys_four = jax.random.split(block_key, 4)
        row_first = jax.random.randint(keys_four[0], (), 0, NX)
        col_first = jax.random.randint(keys_four[1], (), 0, NY)
        tall = jax.random.randint(keys_four[2], (), 1, tall_most + 1)
        wide = jax.random.randint(keys_four[3], (), 1, wide_most + 1)
        inside = (rows >= row_first) & (rows < row_first + tall) & (cols >= col_first) & (cols < col_first + wide)
        land = land | inside
    spot_key = jax.random.fold_in(key, 100)
    spot_rows = jax.random.randint(jax.random.fold_in(spot_key, 1), (8,), 0, NX)
    spot_cols = jax.random.randint(jax.random.fold_in(spot_key, 2), (8,), 0, NY)
    for spot_index in range(8):
        land = land | (rows == spot_rows[spot_index]) & (cols == spot_cols[spot_index])
    return jnp.where(land, 0, 1).astype(jnp.int32)


def place_ends(drawn, rng, least, largest):
    longest = drawn.shape.index(max(drawn.shape))
    spots = []
    for shift in (0, 1):
        where = [jax.random.randint(jax.random.fold_in(rng, axis), (), 0, length) for axis, length in enumerate(drawn.shape)]
        where[longest] = (where[longest] + shift) % drawn.shape[longest]
        spots.append(tuple(where))
    return drawn.at[spots[0]].set(least).at[spots[1]].set(largest)


def steps_of(stream_key, dims, cuts, least, top_value):
    factor_of, own = 1.0, jax.random.fold_in(stream_key, 6)
    for dim, shards_of in cuts:
        steps = jnp.exp(jax.random.uniform(jax.random.fold_in(own, dim), (shards_of,), jnp.float32, least / len(cuts), top_value / len(cuts)))
        factor_of = factor_of * jnp.repeat(steps, dims[dim] // shards_of).reshape([-1 if axis == dim else 1 for axis in range(len(dims))])
    return factor_of


def scatter_about(rng, dims, spread, limit, pieces=(), dtype=jnp.bfloat16):
    entries = jax.random.normal(rng, dims, jnp.float32) * spread
    if len(pieces) > 0:
        entries = steps_of(rng, dims, pieces, -0.22, 0.18) * entries
    return jnp.clip(entries, min=-limit, max=limit).astype(dtype)


def setup_inputs(seed: int = 0) -> dict:
    streams_of = jax.random.split(jax.random.key(seed), 10)
    return {
        "concentration": jnp.clip(2.0 * jax.random.uniform(streams_of[0], (MEMBERS, TR, NX, NY), jnp.float32) ** steps_of(streams_of[0], (MEMBERS, TR, NX, NY), ((0, 2), (2, 16), (3, 16)), -0.2, 0.2), 0.0, 2.0),
        "cotangent": scatter_about(streams_of[1], (MEMBERS, TR, NX, NY), 1.0, 6.0, ((0, 2), (2, 16), (3, 16)), jnp.float32),
        "vel_x": jnp.clip(jax.random.uniform(streams_of[2], (NX, NY), jnp.float32, -2.0, 2.0) * steps_of(streams_of[2], (NX, NY), ((0, 16), (1, 16)), -0.4, 0.0), -2.0, 2.0),
        "vel_y": jnp.clip(jax.random.uniform(streams_of[3], (NX, NY), jnp.float32, -2.0, 2.0) * steps_of(streams_of[3], (NX, NY), ((0, 16), (1, 16)), -0.4, 0.0), -2.0, 2.0),
        "dispersion": jnp.clip(jnp.exp(math.log(10000.0) - 9.2103404 * jax.random.uniform(streams_of[4], (NX, NY), jnp.float32) ** steps_of(streams_of[4], (NX, NY), ((0, 16), (1, 16)), -0.2, 0.2)), 1.0, 10000.0),
        "wet_cells": draw_wet_cells(jax.random.fold_in(streams_of[9], 71), 0),
        "decay_rate": jnp.clip(jnp.exp(jax.random.uniform(streams_of[6], (TR,), jnp.float32, math.log(0.05), math.log(1.0))), 0.05, 1.0),
        "emission": jnp.clip(jnp.exp(jax.random.uniform(streams_of[7], (TR, NSRC), jnp.float32, math.log(2.0), math.log(40.0))), 2.0, 40.0),
        "source_cell": place_ends(jax.random.randint(streams_of[8], (NSRC,), 0, NX * NY), jax.random.fold_in(streams_of[8], 1), 0, (NX * NY) - 1).astype(jnp.int32),
    }


def neighbours(values, line_axis):
    extent = values.shape[line_axis]
    widths = [(1, 1) if dim_index == line_axis else (0, 0) for dim_index in range(values.ndim)]
    padded = jnp.pad(values, widths)
    before = lax.slice_in_dim(padded, 0, extent, axis=line_axis)
    after = lax.slice_in_dim(padded, 2, extent + 2, axis=line_axis)
    return (before, after)

def tracer_copies(band, shape_like):
    return jnp.broadcast_to(band[None], shape_like.shape)

def band_pairs(velocity, disp_here, wet_here, vel_before, vel_after, disp_before, disp_after, wet_before, wet_after, decay_rate):
    open_before = wet_here * wet_before
    open_after = wet_here * wet_after
    flux_before = 0.5 * (disp_here + disp_before) * open_before
    flux_after = 0.5 * (disp_here + disp_after) * open_after
    inflow = jnp.maximum(velocity, 0.0)
    outflow = jnp.maximum(-velocity, 0.0)
    diagonal_base = 1.0 + flux_before + flux_after + inflow * open_before + outflow * open_after
    center = diagonal_base[None] + 0.5 * decay_rate[:, None, None]
    fwd_below = -(flux_before + inflow * open_before)
    fwd_above = -(flux_after + outflow * open_after)
    adj_below = -(flux_before + jnp.maximum(-vel_before, 0.0) * open_before)
    adj_above = -(flux_after + jnp.maximum(vel_after, 0.0) * open_after)
    forward = (tracer_copies(fwd_below, center), center, tracer_copies(fwd_above, center))
    adjoint = (tracer_copies(adj_below, center), center, tracer_copies(adj_above, center))
    return (forward, adjoint)

def direction_bands(velocity, dispersion, wet_float, decay_rate, line_axis):
    vel_before, vel_after = neighbours(velocity, line_axis)
    disp_before, disp_after = neighbours(dispersion, line_axis)
    wet_before, wet_after = neighbours(wet_float, line_axis)
    return band_pairs(velocity, dispersion, wet_float, vel_before, vel_after, disp_before, disp_after, wet_before, wet_after, decay_rate)

def solve_lines(field_in, bands, line_axis):
    moved_bands = [jnp.moveaxis(band, line_axis - 1, -1) for band in bands]

    def one_member(member_field):
        moved = jnp.moveaxis(member_field, line_axis - 1, -1)[..., None]
        solved = lax.linalg.tridiagonal_solve(moved_bands[0], moved_bands[1], moved_bands[2], moved)
        return jnp.moveaxis(solved[..., 0], -1, line_axis - 1)
    return lax.map(one_member, field_in)

def reference(concentration, cotangent, vel_x, vel_y, dispersion, wet_cells, decay_rate, emission, source_cell):
    wet_float = wet_cells.astype(jnp.float32)
    forward_x, adjoint_x = direction_bands(vel_x, dispersion, wet_float, decay_rate, 0)
    forward_y, adjoint_y = direction_bands(vel_y, dispersion, wet_float, decay_rate, 1)
    source = jnp.zeros((TR, NX * NY), jnp.float32).at[:, source_cell].add(emission).reshape(TR, NX, NY)
    start_field = concentration + source[None]
    half_step = solve_lines(start_field, forward_x, 2)
    state_next = solve_lines(half_step, forward_y, 3)
    middle = solve_lines(cotangent, adjoint_y, 3)
    adjoint_state = solve_lines(middle, adjoint_x, 2)
    gradient = jnp.sum(adjoint_state.reshape(MEMBERS, TR, NX * NY)[:, :, source_cell], axis=0)
    return (state_next, adjoint_state, gradient)
```

```python
import functools

import jax
import jax.numpy as jnp
from jax import lax
from jax.experimental import pallas as pl
from jax.experimental.pallas import tpu as pltpu
from jax.sharding import PartitionSpec as P

MESH = pl.DeviceIdType.MESH
TR, ROWS, COLS, LANES, Q = 4, 32, 128, 128, 16
F32, BF16 = jnp.float32, jnp.bfloat16
TILES = 8


def rolled(x, shift):
    n = x.shape[0]
    shift = shift % n
    if shift == 0:
        return x
    if shift % 8 == 0:
        return jnp.concatenate([x[n - shift :], x[: n - shift]], axis=0)
    return pltpu.roll(x, shift, 0)


def pcr_factor(below, center, above, count, unit):
    steps, stride = [], 1
    while stride < count:
        k = stride * unit
        inverse = 1.0 / center
        alpha = -below * rolled(inverse, k)
        gamma = -above * rolled(inverse, -k)
        center = center + alpha * rolled(above, k) + gamma * rolled(below, -k)
        below, above = alpha * rolled(below, k), gamma * rolled(above, -k)
        steps.append((k, alpha, gamma))
        stride *= 2
    return steps, 1.0 / center


def pcr_apply(factors, side):
    steps, inverse = factors
    for k, alpha, gamma in steps:
        side = side + alpha * rolled(side, k) + gamma * rolled(side, -k)
    return side * inverse


class Line:
    def __init__(self, size):
        self.size = size
        sub = lax.broadcasted_iota(jnp.int32, (8, LANES), 0) % size
        self.first = sub == 0
        self.last = sub == size - 1

    def extended(self, cells, before, after):
        head = jnp.where(self.first, before, rolled(cells[-1], 1))
        tail = jnp.where(self.last, after, rolled(cells[0], -1))
        return [head] + cells + [tail]

    def bands(self, vel, disp, wet, half_decay, before, after):
        vel = self.extended(vel, before[0], after[0])
        disp = self.extended(disp, before[1], after[1])
        wet = self.extended(wet, before[2], after[2])
        gate = [wet[k] * wet[k + 1] for k in range(Q + 1)]
        flux = [0.5 * (disp[k] + disp[k + 1]) * gate[k] for k in range(Q + 1)]
        plus = [jnp.maximum(v, 0.0) for v in vel]
        minus = [jnp.maximum(-v, 0.0) for v in vel]
        fwd_below = [-(flux[q] + plus[q + 1] * gate[q]) for q in range(Q)]
        fwd_above = [-(flux[q + 1] + minus[q + 1] * gate[q + 1]) for q in range(Q)]
        adj_below = [-(flux[q] + minus[q] * gate[q]) for q in range(Q)]
        adj_above = [-(flux[q + 1] + plus[q + 2] * gate[q + 1]) for q in range(Q)]
        center = [
            (1.0 + flux[q] + flux[q + 1] + plus[q + 1] * gate[q] + minus[q + 1] * gate[q + 1])
            + half_decay
            for q in range(Q)
        ]
        inverse = [1.0 / center[0]]
        for q in range(1, Q - 1):
            pivot = center[q] - fwd_below[q] * fwd_above[q - 1] * inverse[q - 1]
            inverse.append(1.0 / pivot)
        forward = self.factor(fwd_below, center, fwd_above, inverse, adj_below[0])
        adjoint = self.factor(adj_below, center, adj_above, inverse, fwd_below[0])
        return forward, adjoint

    def factor(self, below, center, above, inverse, above_prev):
        e = Q - 1
        mult = [None] + [below[q] * inverse[q - 1] for q in range(1, e)]
        up = [above[q] * inverse[q] for q in range(e)]
        start = [-below[0]]
        for q in range(1, e):
            start.append(-mult[q] * start[q - 1])
        v, w = [None] * e, [None] * e
        v[e - 1] = start[e - 1] * inverse[e - 1]
        w[e - 1] = -up[e - 1]
        for q in range(e - 2, -1, -1):
            v[q] = start[q] * inverse[q] - up[q] * v[q + 1]
            w[q] = -up[q] * w[q + 1]
        zero = jnp.zeros((8, LANES), F32)
        coef = below[e] * v[e - 1]
        center_local = center[e] + below[e] * w[e - 1]
        reduced = pcr_factor(
            jnp.where(self.first | self.last, zero, coef),
            jnp.where(self.last, 1.0, center_local + above[e] * rolled(v[0], -1)),
            jnp.where(self.last, zero, above[e] * rolled(w[0], -1)),
            self.size,
            1,
        )
        outer_v = pcr_apply(reduced, jnp.where(self.first, -coef, zero))
        outer_w = pcr_apply(reduced, jnp.where(self.last, 1.0, zero))
        fa = dict(
            mult=mult, up=up, inverse=inverse, v=v, w=w, below_end=below[e], above_end=above[e],
            coef=coef, reduced=reduced, outer_v=outer_v, outer_w=outer_w, above_prev=above_prev,
        )
        fa["center_terms"] = jnp.where(
            self.last,
            center_local + coef * rolled(outer_w, 1),
            above_prev * (v[0] + w[0] * outer_v),
        )
        fa["side_coefs"] = jnp.where(
            self.last, coef * rolled(outer_v, 1), above_prev * (w[0] * outer_w)
        )
        return fa

    def local(self, fa, field):
        e = Q - 1
        g = [field[0]]
        for q in range(1, e):
            g.append(field[q] - fa["mult"][q] * g[q - 1])
        part = [None] * e
        part[e - 1] = g[e - 1] * fa["inverse"][e - 1]
        for q in range(e - 2, -1, -1):
            part[q] = g[q] * fa["inverse"][q] - fa["up"][q] * part[q + 1]
        own = field[e] - fa["below_end"] * part[e - 1]
        inner = jnp.where(self.last, 0.0, own - fa["above_end"] * rolled(part[0], -1))
        outer = pcr_apply(fa["reduced"], inner)
        message = jnp.where(
            self.last,
            own - fa["coef"] * rolled(outer, 1),
            fa["above_prev"] * (part[0] + fa["w"][0] * outer),
        )
        return part, outer, message

    def finish(self, fa, part, outer, left, own):
        ends = outer + fa["outer_v"] * left + fa["outer_w"] * own
        before = jnp.where(self.first, left, rolled(ends, 1))
        cells = [part[q] + fa["v"][q] * before + fa["w"][q] * ends for q in range(Q - 1)]
        return cells + [ends]


def split(n):
    inner = 1
    while inner * inner < n:
        inner *= 2
    return n // inner, inner


def kernel(
    nx, ny, ne, nsrc,
    decay, conc, cot, vel_x, vel_y, disp, wet_cells, emission, cells,
    state_out, adjoint_out, grad_out,
    f_vx, f_vy, f_disp, f_wet, f_conc, f_cot, f_emis, f_cells,
    vel_t, disp_t, wet_t, work, work_t, state_v, adjoint_v,
    halo_send, halo_recv, onehot, rows_v, cols_v,
    y_send, y_recv, x_send, x_recv, xb_send, xb_recv, yb_send, yb_recv, ends_x, ends_y,
    picked, rs_recv, r1_send, r1_recv, r2_send, r2_recv, total, grad_v,
    in_sem, out_sem, halo_ssem, halo_rsem, ssem, rsem,
):
    gx, gy, en = lax.axis_index("gx"), lax.axis_index("gy"), lax.axis_index("ens")
    group = nx * ne
    me = gx * ne + en
    chunk = nsrc // group

    loads = [
        pltpu.make_async_copy(src, dst, in_sem.at[i])
        for i, (src, dst) in enumerate(
            [
                (vel_x, f_vx), (vel_y, f_vy), (disp, f_disp), (wet_cells, f_wet),
                (cells, f_cells), (cot.at[0], f_cot), (emission, f_emis), (conc.at[0], f_conc),
            ]
        )
    ]
    for load in loads:
        load.start()

    barrier = pltpu.get_barrier_semaphore()

    def greet_plane(o, _):
        peer = lax.rem(me + o, group)
        pl.semaphore_signal(
            barrier, inc=1, device_id=(peer // ne, gy, lax.rem(peer, ne)), device_id_type=MESH
        )
        return 0

    def greet_line(o, _):
        pl.semaphore_signal(
            barrier, inc=1, device_id=(gx, lax.rem(gy + o, ny), en), device_id_type=MESH
        )
        return 0

    lax.fori_loop(1, group, greet_plane, 0)
    lax.fori_loop(1, ny, greet_line, 0)

    def strided(ref, q):
        return ref[pl.ds(q, 8, stride=Q), :]

    def column(ref):
        return [strided(ref, q) for q in range(Q)]

    def put(ref, cells_):
        for q in range(Q):
            ref[pl.ds(q, 8, stride=Q), :] = cells_[q]

    for i in range(4):
        loads[i].wait()
    wet_f = f_wet[...].astype(F32)
    for field, ref in ((f_vy[...], vel_t), (f_disp[...], disp_t), (wet_f, wet_t)):
        ref[...] = jnp.transpose(jnp.concatenate([field] * TR, axis=0))
    zero8 = jnp.zeros((8, LANES), F32)
    for i in range(4):
        halo_send[i] = zero8
    halo_send[0, 0:1, :] = f_vx[ROWS - 1 : ROWS, :]
    halo_send[0, 1:2, :] = f_disp[ROWS - 1 : ROWS, :]
    halo_send[0, 2:3, :] = wet_f[ROWS - 1 : ROWS, :]
    halo_send[1, 0:1, :] = f_vx[0:1, :]
    halo_send[1, 1:2, :] = f_disp[0:1, :]
    halo_send[1, 2:3, :] = wet_f[0:1, :]
    for i, ref in enumerate((vel_t, disp_t, wet_t)):
        halo_send[2, i : i + 1, :] = ref[COLS - 1 : COLS, :]
        halo_send[3, i : i + 1, :] = ref[0:1, :]
    ends_x[0:8, :] = zero8
    ends_y[0:8, :] = zero8

    pl.semaphore_wait(barrier, group - 1 + ny - 1)

    halos = []
    for i, device in enumerate(
        (
            (lax.rem(gx + 1, nx), gy, en),
            (lax.rem(gx + nx - 1, nx), gy, en),
            (gx, lax.rem(gy + 1, ny), en),
            (gx, lax.rem(gy + ny - 1, ny), en),
        )
    ):
        halos.append(
            pltpu.make_async_remote_copy(
                src_ref=halo_send.at[i], dst_ref=halo_recv.at[i],
                send_sem=halo_ssem.at[i], recv_sem=halo_rsem.at[i],
                device_id=device, device_id_type=MESH,
            )
        )
    halos[2].start()
    halos[3].start()
    halos[0].start()
    halos[1].start()

    def along_line(send, recv, slot):
        def go(o, _):
            pltpu.make_async_remote_copy(
                src_ref=send, dst_ref=recv.at[gy], send_sem=ssem.at[slot],
                recv_sem=rsem.at[slot],
                device_id=(gx, lax.rem(gy + o, ny), en), device_id_type=MESH,
            ).start()
            return 0

        lax.fori_loop(1, ny, go, 0)
        recv[gy] = send[...]

    def along_x(send, recv, slot):
        def go(o, _):
            pltpu.make_async_remote_copy(
                src_ref=send, dst_ref=recv.at[gx], send_sem=ssem.at[slot],
                recv_sem=rsem.at[slot],
                device_id=(lax.rem(gx + o, nx), gy, en), device_id_type=MESH,
            ).start()
            return 0

        lax.fori_loop(1, nx, go, 0)
        recv[gx] = send[...]

    def arrived(recv, count, slot):
        pltpu.make_async_copy(
            recv.at[pl.ds(0, count)], recv.at[pl.ds(0, count)], rsem.at[slot]
        ).wait()

    def sent(recv, count, slot):
        pltpu.make_async_copy(
            recv.at[pl.ds(0, count)], recv.at[pl.ds(0, count)], ssem.at[slot]
        ).wait()

    loads[4].wait()
    shift = (ny * COLS).bit_length() - 1
    source = f_cells[...]
    rows_v[...] = lax.shift_right_logical(source, shift) - gx * ROWS
    cols_v[...] = (source & (ny * COLS - 1)) - gy * COLS
    row_iota = lax.broadcasted_iota(jnp.int32, (ROWS, LANES), 0)
    col_iota = lax.broadcasted_iota(jnp.int32, (COLS, LANES), 0)
    steps = nsrc // LANES // TILES

    def hot_columns(step, _):
        base = pl.multiple_of(step * TILES, TILES)
        tile = cols_v[pl.ds(base, TILES), :]
        for i in range(TILES):
            hot = jnp.where(col_iota == tile[i : i + 1, :], 1.0, 0.0).astype(BF16)
            onehot[:, pl.ds(pl.multiple_of((base + i) * LANES, LANES), LANES)] = hot
        return 0

    lax.fori_loop(0, steps, hot_columns, 0)

    loads[5].wait()
    work_t[...] = jnp.transpose(f_cot[...].reshape(TR * ROWS, COLS))

    y_line, x_line = Line(8), Line(2)
    halos[2].wait_recv()
    halos[3].wait_recv()
    lane_tracer = lax.broadcasted_iota(jnp.int32, (8, LANES), 1) // ROWS
    sub_tracer = lax.broadcasted_iota(jnp.int32, (8, LANES), 0) // 2

    def half_decay(tracer):
        value = jnp.full((8, LANES), decay[TR - 1], F32)
        for t in range(TR - 1):
            value = jnp.where(tracer == t, decay[t], value)
        return 0.5 * value

    def halo(i, keep):
        block = jnp.where(keep, halo_recv[i], 0.0)
        return [block[k : k + 1, :] for k in range(3)]

    y_fwd, y_adj = y_line.bands(
        column(vel_t), column(disp_t), column(wet_t), half_decay(lane_tracer),
        halo(2, gy > 0), halo(3, gy < ny - 1),
    )
    y_part, y_outer, message = y_line.local(y_adj, column(work_t))
    y_send[...] = zero8
    for i, term in enumerate((message, y_adj["center_terms"], y_adj["side_coefs"])):
        y_send[2 * i : 2 * i + 1, :] = term[0:1, :]
        y_send[2 * i + 1 : 2 * i + 2, :] = term[7:8, :]
    along_line(y_send, y_recv, 0)

    loads[6].wait()
    loads[7].wait()

    def scatter(step, acc):
        base = pl.multiple_of(step * TILES, TILES)
        tile = rows_v[pl.ds(base, TILES), :]
        start = pl.multiple_of(base * LANES, TILES * LANES)
        values = f_emis[:, pl.ds(start, TILES * LANES)]
        high = values.astype(BF16).astype(F32)
        low = values - high
        left = []
        for i in range(TILES):
            mask = row_iota == tile[i : i + 1, :]
            part = slice(i * LANES, (i + 1) * LANES)
            left.append(
                jnp.concatenate(
                    [
                        jnp.where(mask, half[t : t + 1, part], 0.0).astype(BF16)
                        for half in (high, low)
                        for t in range(TR)
                    ],
                    axis=0,
                )
            )
        return acc + lax.dot_general(
            jnp.concatenate(left, axis=1),
            onehot[:, pl.ds(start, TILES * LANES)],
            (((1,), (1,)), ((), ())),
            preferred_element_type=F32,
        )

    placed = lax.fori_loop(0, steps, scatter, jnp.zeros((2 * TR * ROWS, COLS), F32))
    work[...] = f_conc[...].reshape(TR * ROWS, COLS) + (placed[: TR * ROWS] + placed[TR * ROWS :])

    halos[0].wait_recv()
    halos[1].wait_recv()

    def spread(ref, as_float):
        upper = x_line.first
        out = []
        for q in range(Q):
            value = jnp.where(upper, ref[q : q + 1, :], ref[q + Q : q + Q + 1, :])
            out.append(value.astype(F32) if as_float else value)
        return out

    x_fwd, x_adj = x_line.bands(
        spread(f_vx, False), spread(f_disp, False), spread(f_wet, True), half_decay(sub_tracer),
        halo(0, gx > 0), halo(1, gx < nx - 1),
    )
    fx_part, fx_outer, message = x_line.local(x_fwd, column(work))
    x_send[0:8, :] = message
    x_send[8:16, :] = x_fwd["center_terms"]
    x_send[16:24, :] = x_fwd["side_coefs"]
    along_x(x_send, x_recv, 1)

    def y_piece(ref, k):
        return jnp.concatenate([ref[d, k : k + 1, :] for d in range(ny)], axis=0)

    def y_ends(factors, side):
        ends_y[8 : 8 + ny, :] = pcr_apply(factors, side)
        left = ends_y[pl.ds(7 + gy, 1), :]
        own = ends_y[pl.ds(8 + gy, 1), :]
        return left, own

    arrived(y_recv, ny - 1, 0)
    y_center = y_piece(y_recv, 3) + rolled(y_piece(y_recv, 2), -1)
    y_below, y_above = y_piece(y_recv, 5), rolled(y_piece(y_recv, 4), -1)
    factors = pcr_factor(y_below, y_center, y_above, ny, 1)
    left, own = y_ends(factors, y_piece(y_recv, 1) - rolled(y_piece(y_recv, 0), -1))
    put(work_t, y_line.finish(y_adj, y_part, y_outer, left, own))
    work[...] = jnp.transpose(work_t[...])
    ax_part, ax_outer, message = x_line.local(x_adj, column(work))
    xb_send[...] = message
    along_x(xb_send, xb_recv, 2)

    def x_piece(ref, k):
        return jnp.concatenate([ref[d, 8 * k : 8 * k + 8, :] for d in range(nx)], axis=0)

    def from_next(value):
        later = rolled(value, -8)
        return jnp.concatenate(
            [rolled(later[8 * d : 8 * d + 8], 1) for d in range(nx)], axis=0
        )

    def x_ends(factors, side):
        ends_x[8 : 8 + 8 * nx, :] = pcr_apply(factors, side)
        out = []
        for start in (gx, gx + 1):
            block = ends_x[pl.ds(pl.multiple_of(8 * start, 8), 8), :]
            out.append(jnp.where(x_line.last, block, rolled(block, -1)))
        return out

    arrived(x_recv, nx - 1, 1)
    terms = x_piece(x_recv, 1)
    x_center = terms + from_next(terms)
    terms = x_piece(x_recv, 2)
    x_below, x_above = terms, from_next(terms)
    factors = pcr_factor(x_below, x_center, x_above, nx, 8)
    terms = x_piece(x_recv, 0)
    left, own = x_ends(factors, terms - from_next(terms))
    put(work, x_line.finish(x_fwd, fx_part, fx_outer, left, own))
    work_t[...] = jnp.transpose(work[...])
    y_part, y_outer, message = y_line.local(y_fwd, column(work_t))
    yb_send[...] = zero8
    yb_send[0:1, :] = message[0:1, :]
    yb_send[1:2, :] = message[7:8, :]
    along_line(yb_send, yb_recv, 3)

    x_factors = pcr_factor(rolled(x_above, 8), x_center, rolled(x_below, -8), nx, 8)
    arrived(xb_recv, nx - 1, 2)
    terms = x_piece(xb_recv, 0)
    left, own = x_ends(x_factors, terms - from_next(terms))
    put(adjoint_v, x_line.finish(x_adj, ax_part, ax_outer, left, own))
    adjoint_store = pltpu.make_async_copy(
        adjoint_v, adjoint_out, out_sem.at[0]
    )
    adjoint_store.start()

    values = adjoint_v[...]
    high = values.astype(BF16)
    low = (values - high.astype(F32)).astype(BF16)
    both = jnp.concatenate([high, low], axis=1)

    def pick(step, _):
        base = pl.multiple_of(step * TILES, TILES)
        tile = rows_v[pl.ds(base, TILES), :]
        start = pl.multiple_of(base * LANES, TILES * LANES)
        hot = onehot[:, pl.ds(start, TILES * LANES)]
        found = jnp.dot(both, jnp.concatenate([hot, hot], axis=0), preferred_element_type=F32)
        for i in range(TILES):
            mask = row_iota == tile[i : i + 1, :]
            part = found[:, i * LANES : (i + 1) * LANES]
            lines = [
                jnp.sum(
                    jnp.where(mask, part[t * ROWS : (t + 1) * ROWS], 0.0), axis=0, keepdims=True
                )
                for t in range(TR)
            ]
            picked[:, pl.ds(pl.multiple_of((base + i) * LANES, LANES), LANES)] = jnp.concatenate(
                lines, axis=0
            )
        return 0

    lax.fori_loop(0, steps, pick, 0)

    def own_part(ref, j):
        return ref.at[:, pl.ds(pl.multiple_of(j * chunk, chunk), chunk)]

    def reduce_out(o, _):
        peer = lax.rem(me + o, group)
        pltpu.make_async_remote_copy(
            src_ref=own_part(picked, peer), dst_ref=rs_recv.at[me],
            send_sem=ssem.at[4], recv_sem=rsem.at[4],
            device_id=(peer // ne, gy, lax.rem(peer, ne)), device_id_type=MESH,
        ).start()
        return 0

    lax.fori_loop(1, group, reduce_out, 0)
    rs_recv[me] = picked[:, pl.ds(pl.multiple_of(me * chunk, chunk), chunk)]

    arrived(yb_recv, ny - 1, 3)
    y_factors = pcr_factor(rolled(y_above, 1), y_center, rolled(y_below, -1), ny, 1)
    left, own = y_ends(y_factors, y_piece(yb_recv, 1) - rolled(y_piece(yb_recv, 0), -1))
    put(work_t, y_line.finish(y_fwd, y_part, y_outer, left, own))
    state_v[...] = jnp.transpose(work_t[...])
    state_store = pltpu.make_async_copy(state_v, state_out, out_sem.at[1])
    state_store.start()

    arrived(rs_recv, group - 1, 4)

    def summed(ref, n):
        value = ref[0]
        for i in range(1, n):
            value = value + ref[i]
        return value

    outer, inner = split(ny)
    r1_send[...] = summed(rs_recv, group)
    for k in range(1, outer):
        pltpu.make_async_remote_copy(
            src_ref=r1_send, dst_ref=r1_recv.at[gy // inner],
            send_sem=ssem.at[5], recv_sem=rsem.at[5],
            device_id=(gx, lax.rem(gy + k * inner, ny), en), device_id_type=MESH,
        ).start()
    r1_recv[gy // inner] = r1_send[...]
    if outer > 1:
        arrived(r1_recv, outer - 1, 5)
    r2_send[...] = summed(r1_recv, outer)
    place = lax.rem(gy, inner)
    for k in range(1, inner):
        pltpu.make_async_remote_copy(
            src_ref=r2_send, dst_ref=r2_recv.at[place],
            send_sem=ssem.at[6], recv_sem=rsem.at[6],
            device_id=(gx, gy - place + lax.rem(place + k, inner), en), device_id_type=MESH,
        ).start()
    r2_recv[place] = r2_send[...]
    arrived(r2_recv, inner - 1, 6)
    total[...] = summed(r2_recv, inner)

    def spread_out(o, _):
        peer = lax.rem(me + o, group)
        pltpu.make_async_remote_copy(
            src_ref=total, dst_ref=own_part(grad_v, me),
            send_sem=ssem.at[7], recv_sem=rsem.at[7],
            device_id=(peer // ne, gy, lax.rem(peer, ne)), device_id_type=MESH,
        ).start()
        return 0

    lax.fori_loop(1, group, spread_out, 0)
    grad_v[:, pl.ds(pl.multiple_of(me * chunk, chunk), chunk)] = total[...]

    for copy in halos:
        copy.wait_send()
    sent(y_recv, ny - 1, 0)
    sent(x_recv, nx - 1, 1)
    sent(xb_recv, nx - 1, 2)
    sent(yb_recv, ny - 1, 3)
    sent(rs_recv, group - 1, 4)
    if outer > 1:
        sent(r1_recv, outer - 1, 5)
    sent(r2_recv, inner - 1, 6)
    adjoint_store.wait()
    state_store.wait()
    rest = grad_v.at[:, pl.ds(0, (group - 1) * chunk)]
    pltpu.make_async_copy(rest, rest, rsem.at[7]).wait()
    grad_store = pltpu.make_async_copy(grad_v, grad_out, out_sem.at[2])
    grad_store.start()
    pltpu.make_async_copy(rest, rest, ssem.at[7]).wait()
    grad_store.wait()


def per_device(
    nx, ny, ne, concentration, cotangent, vel_x, vel_y, dispersion, wet_cells, decay_rate, emission,
    source_cell,
):
    nsrc = source_cell.shape[0]
    group = nx * ne
    chunk = nsrc // group
    outer, inner = split(ny)
    square = pltpu.VMEM((TR * ROWS, COLS), F32)
    block = pltpu.VMEM((ROWS, COLS), F32)

    def vmem(*shape, dtype=F32):
        return pltpu.VMEM(shape, dtype)

    scratch = [
        block, block, block, vmem(ROWS, COLS, dtype=jnp.int32),
        vmem(TR, ROWS, COLS), vmem(TR, ROWS, COLS), vmem(TR, nsrc),
        vmem(nsrc // LANES, LANES, dtype=jnp.int32),
        square, square, square, square, square, square, square,
        vmem(4, 8, LANES), vmem(4, 8, LANES), vmem(COLS, nsrc, dtype=BF16),
        vmem(nsrc // LANES, LANES, dtype=jnp.int32), vmem(nsrc // LANES, LANES, dtype=jnp.int32),
        vmem(8, LANES), vmem(ny, 8, LANES), vmem(24, LANES), vmem(nx, 24, LANES),
        vmem(8, LANES), vmem(nx, 8, LANES), vmem(8, LANES), vmem(ny, 8, LANES),
        vmem(8 + 8 * nx, LANES), vmem(8 + max(8, ny), LANES),
        vmem(TR, nsrc), vmem(group, TR, chunk),
        vmem(TR, chunk), vmem(outer, TR, chunk), vmem(TR, chunk), vmem(inner, TR, chunk),
        vmem(TR, chunk), vmem(TR, nsrc),
        pltpu.SemaphoreType.DMA((8,)), pltpu.SemaphoreType.DMA((3,)),
        pltpu.SemaphoreType.DMA((4,)), pltpu.SemaphoreType.DMA((4,)),
        pltpu.SemaphoreType.DMA((8,)), pltpu.SemaphoreType.DMA((8,)),
    ]
    hbm = pl.BlockSpec(memory_space=pl.ANY)
    state, adjoint, gradient = pl.pallas_call(
        functools.partial(kernel, nx, ny, ne, nsrc),
        out_shape=(
            jax.ShapeDtypeStruct((TR * ROWS, COLS), F32),
            jax.ShapeDtypeStruct((TR * ROWS, COLS), F32),
            jax.ShapeDtypeStruct(emission.shape, F32),
        ),
        in_specs=[pl.BlockSpec(memory_space=pltpu.SMEM)] + [hbm] * 8,
        out_specs=(hbm, hbm, hbm),
        scratch_shapes=scratch,
        compiler_params=pltpu.CompilerParams(
            collective_id=0, has_side_effects=True, vmem_limit_bytes=32 * 1024 * 1024
        ),
        name="adi_step",
    )(
        decay_rate, concentration, cotangent, vel_x, vel_y, dispersion, wet_cells, emission,
        source_cell.reshape(nsrc // LANES, LANES),
    )
    shape = concentration.shape
    return (state.reshape(shape), adjoint.reshape(shape), gradient)


def solution(mesh):
    nx, ny, ne = (mesh.shape[a] for a in ("gx", "gy", "ens"))
    field = P("ens", None, "gx", "gy")
    plane = P("gx", "gy")
    return jax.shard_map(
        functools.partial(per_device, nx, ny, ne),
        mesh=mesh,
        in_specs=(field, field, plane, plane, plane, plane, P(), P(), P()),
        out_specs=(field, field, P()),
        check_vma=False,
    )
```

```python
import functools

import jax
import jax.numpy as jnp
from jax import lax
from jax.experimental import pallas as pl
from jax.experimental.pallas import tpu as pltpu
from jax.sharding import PartitionSpec as P

MESH = pl.DeviceIdType.MESH
TR, ROWS, COLS, LANES, Q = 4, 32, 128, 128, 16
CELLS = TR * ROWS
F32, BF16 = jnp.float32, jnp.bfloat16
TILES = 8


def rolled(x, shift):
    n = x.shape[0]
    shift = shift % n
    if shift == 0:
        return x
    if shift % 8 == 0:
        return jnp.concatenate([x[n - shift :], x[: n - shift]], axis=0)
    return pltpu.roll(x, shift, 0)


def wrapped(i, n):
    return i & (n - 1) if n & (n - 1) == 0 else lax.rem(i, n)


def farthest_first(n):
    return sorted(range(1, n), key=lambda o: (-min(o, n - o), o))


def pcr_factor(below, center, above, count, unit):
    steps, stride = [], 1
    while stride < count:
        k = stride * unit
        inverse = 1.0 / center
        alpha = -below * rolled(inverse, k)
        gamma = -above * rolled(inverse, -k)
        center = center + alpha * rolled(above, k) + gamma * rolled(below, -k)
        below, above = alpha * rolled(below, k), gamma * rolled(above, -k)
        steps.append((k, alpha, gamma))
        stride *= 2
    return steps, 1.0 / center


def pcr_apply(factors, side):
    steps, inverse = factors
    for k, alpha, gamma in steps:
        side = side + alpha * rolled(side, k) + gamma * rolled(side, -k)
    return side * inverse


class Line:
    def __init__(self, size):
        self.size = size
        sub = lax.broadcasted_iota(jnp.int32, (8, LANES), 0) % size
        self.first = sub == 0
        self.last = sub == size - 1

    def extended(self, cells):
        head = jnp.where(self.first, 0.0, rolled(cells[-1], 1))
        tail = jnp.where(self.last, 0.0, rolled(cells[0], -1))
        return [head] + cells + [tail]

    def bands(self, vel, disp, wet, half_decay):
        vel, disp, wet = (self.extended(cells) for cells in (vel, disp, wet))
        gate = [wet[k] * wet[k + 1] for k in range(Q + 1)]
        flux = [0.5 * (disp[k] + disp[k + 1]) * gate[k] for k in range(Q + 1)]
        plus = [jnp.maximum(v, 0.0) for v in vel]
        minus = [jnp.maximum(-v, 0.0) for v in vel]
        fwd_below = [-(flux[q] + plus[q + 1] * gate[q]) for q in range(Q)]
        fwd_above = [-(flux[q + 1] + minus[q + 1] * gate[q + 1]) for q in range(Q)]
        adj_below = [-(flux[q] + minus[q] * gate[q]) for q in range(Q)]
        adj_above = [-(flux[q + 1] + plus[q + 2] * gate[q + 1]) for q in range(Q)]
        center = [
            (1.0 + flux[q] + flux[q + 1] + plus[q + 1] * gate[q] + minus[q + 1] * gate[q + 1])
            + half_decay
            for q in range(Q)
        ]
        inverse = [1.0 / center[0]]
        for q in range(1, Q - 1):
            pivot = center[q] - fwd_below[q] * fwd_above[q - 1] * inverse[q - 1]
            inverse.append(1.0 / pivot)
        forward = self.factor(fwd_below, center, fwd_above, inverse)
        adjoint = self.factor(adj_below, center, adj_above, inverse)
        return forward, adjoint

    def factor(self, below, center, above, inverse):
        e = Q - 1
        fa = dict(inverse=inverse, below_end=below[e], above_end=above[e])
        fa["mult"] = mult = [None] + [below[q] * inverse[q - 1] for q in range(1, e)]
        fa["up"] = up = [above[q] * inverse[q] for q in range(e)]
        start = [-below[0]]
        for q in range(1, e):
            start.append(-mult[q] * start[q - 1])
        v, w = [None] * e, [None] * e
        v[e - 1] = start[e - 1] * inverse[e - 1]
        w[e - 1] = -up[e - 1]
        for q in range(e - 2, -1, -1):
            v[q] = start[q] * inverse[q] - up[q] * v[q + 1]
            w[q] = -up[q] * w[q + 1]
        fa["v"], fa["w"] = v, w
        fa["reduced"] = pcr_factor(
            below[e] * v[e - 1],
            center[e] + below[e] * w[e - 1] + above[e] * rolled(v[0], -1),
            above[e] * rolled(w[0], -1),
            self.size,
            1,
        )
        head = jnp.where(self.first, 1.0, 0.0)
        fa["from_first"] = self.solve(fa, [head] + [None] * e)
        fa["from_last"] = self.solve(fa, [None] * e + [jnp.where(self.last, 1.0, 0.0)])
        return fa

    def solve(self, fa, field):
        def plus(a, b):
            return b if a is None else a if b is None else a + b

        def times(a, b):
            return None if b is None else a * b

        e = Q - 1
        g = [field[0]]
        for q in range(1, e):
            g.append(plus(field[q], times(-fa["mult"][q], g[q - 1])))
        part = [None] * e
        part[e - 1] = times(fa["inverse"][e - 1], g[e - 1])
        for q in range(e - 2, -1, -1):
            part[q] = plus(times(fa["inverse"][q], g[q]), times(-fa["up"][q], part[q + 1]))
        side = plus(field[e], times(-fa["below_end"], part[e - 1]))
        if part[0] is not None:
            side = side - fa["above_end"] * rolled(part[0], -1)
        ends = pcr_apply(fa["reduced"], side)
        before = rolled(ends, 1)
        return [
            plus(part[q], fa["v"][q] * before + fa["w"][q] * ends) for q in range(e)
        ] + [ends]

    def finish(self, fa, part, head, tail):
        first, last = fa["from_first"], fa["from_last"]
        return [part[q] + first[q] * head + last[q] * tail for q in range(Q)]

    def edges(self, cells):
        return jnp.where(self.last, cells[Q - 1], cells[0])


def faces(plus_first, disp_first, minus_last, disp_last, index, count):
    disp_next = rolled(disp_first, -1)
    shut = (index == count - 1) | (disp_last <= 0.0) | (disp_next <= 0.0)
    flux = 0.5 * (disp_last + disp_next)
    return (
        jnp.where(shut, 0.0, flux + minus_last),
        jnp.where(shut, 0.0, flux + rolled(plus_first, -1)),
    )


def kernel(
    nx, ny, ne, nsrc,
    decay, conc, cot, vel_x, vel_y, disp, wet_cells, emission, cells,
    state_out, adjoint_out, grad_out,
    f_vx, f_vy, f_disp, f_wet, f_conc, f_cot, f_emis, f_cells,
    vel_t, disp_t, wet_t, work, work_t, state_v, adjoint_v, mate_v, first_v, last_v,
    onehot, rows_v, cols_v, owner_v,
    y_send, y_recv, x_send, x_recv, xb_send, xb_recv, yb_send, yb_recv, ends_a, ends_b,
    z_send, z_recv, p_send, p_recv, g_send, g_recv, total, grad_v,
    in_sem, out_sem, mate_ssem, mate_rsem, ssem, rsem,
):
    gx, gy, en = lax.axis_index("gx"), lax.axis_index("gy"), lax.axis_index("ens")
    half = nsrc // ne
    chunk = half // nx
    tiles = chunk // LANES
    half_tiles = half // LANES
    mate = (gx, gy, wrapped(en + 1, ne))

    loads = [
        pltpu.make_async_copy(src, dst, in_sem.at[i])
        for i, (src, dst) in enumerate(
            [
                (vel_y, f_vy), (disp, f_disp), (wet_cells, f_wet), (cot.at[0], f_cot),
                (vel_x, f_vx), (cells, f_cells), (emission, f_emis), (conc.at[0], f_conc),
            ]
        )
    ]

    def line_peer(o):
        return (gx, wrapped(gy + o, ny), en)

    def x_peer(o):
        return (wrapped(gx + o, nx), gy, en)

    barrier = pltpu.get_barrier_semaphore()
    for o in farthest_first(ny):
        pl.semaphore_signal(barrier, inc=1, device_id=line_peer(o), device_id_type=MESH)
    for load in loads:
        load.start()
    for o in farthest_first(nx):
        pl.semaphore_signal(barrier, inc=1, device_id=x_peer(o), device_id_type=MESH)
    pl.semaphore_signal(barrier, inc=1, device_id=mate, device_id_type=MESH)

    def to_line(send, recv, slot):
        for o in farthest_first(ny):
            pltpu.make_async_remote_copy(
                src_ref=send, dst_ref=recv.at[gy], send_sem=ssem.at[slot],
                recv_sem=rsem.at[slot], device_id=line_peer(o), device_id_type=MESH,
            ).start()
        recv[gy] = send[...]

    def to_x(send, recv, slot):
        for o in farthest_first(nx):
            pltpu.make_async_remote_copy(
                src_ref=send, dst_ref=recv.at[gx], send_sem=ssem.at[slot],
                recv_sem=rsem.at[slot], device_id=x_peer(o), device_id_type=MESH,
            ).start()
        recv[gx] = send[...]

    def to_each_x(send, recv, slot):
        for o in farthest_first(nx):
            peer = wrapped(gx + o, nx)
            pltpu.make_async_remote_copy(
                src_ref=send.at[peer], dst_ref=recv.at[gx], send_sem=ssem.at[slot],
                recv_sem=rsem.at[slot], device_id=x_peer(o), device_id_type=MESH,
            ).start()
        recv[gx] = send[gx]

    def arrived(recv, count, slot):
        part = recv.at[pl.ds(0, count)]
        pltpu.make_async_copy(part, part, rsem.at[slot]).wait()

    def sent(recv, count, slot):
        part = recv.at[pl.ds(0, count)]
        pltpu.make_async_copy(part, part, ssem.at[slot]).wait()

    def strided(ref, q):
        return ref[pl.ds(q, 8, stride=Q), :]

    def column(ref):
        return [strided(ref, q) for q in range(Q)]

    def put(ref, cells_):
        for q in range(Q):
            ref[pl.ds(q, 8, stride=Q), :] = cells_[q]

    y_line, x_line = Line(8), Line(2)
    zero8 = jnp.zeros((8, LANES), F32)
    lane_tracer = lax.broadcasted_iota(jnp.int32, (8, LANES), 1) // ROWS
    sub_tracer = lax.broadcasted_iota(jnp.int32, (8, LANES), 0) // 2

    def half_decay(tracer):
        value = jnp.full((8, LANES), decay[TR - 1], F32)
        for t in range(TR - 1):
            value = jnp.where(tracer == t, decay[t], value)
        return 0.5 * value

    for i in range(4):
        loads[i].wait()
    wet_f = f_wet[...].astype(F32)
    for field, ref in ((f_vy[...], vel_t), (f_disp[...], disp_t), (wet_f, wet_t)):
        ref[...] = jnp.transpose(jnp.concatenate([field] * TR, axis=0))
    work_t[...] = jnp.transpose(f_cot[...].reshape(CELLS, COLS))
    y_fwd, y_adj = y_line.bands(
        column(vel_t), column(disp_t), column(wet_t), half_decay(lane_tracer)
    )
    y_part = y_line.solve(y_adj, column(work_t))
    end = COLS - 1
    tracer_row = lane_tracer[0:1]
    packed = jnp.where(
        tracer_row == 0,
        jnp.maximum(vel_t[0:1, :], 0.0),
        jnp.where(
            tracer_row == 1,
            disp_t[0:1, :] * wet_t[0:1, :],
            jnp.where(
                tracer_row == 2,
                jnp.maximum(-vel_t[end : end + 1, :], 0.0),
                disp_t[end : end + 1, :] * wet_t[end : end + 1, :],
            ),
        ),
    )
    e = Q - 1
    for i, row in enumerate(
        (
            y_part[0][0:1], y_part[e][7:8], y_fwd["from_first"][0][0:1],
            y_fwd["from_last"][e][7:8], y_fwd["from_last"][0][0:1],
            y_fwd["from_first"][e][7:8], packed, zero8[0:1],
        )
    ):
        y_send[i : i + 1, :] = row

    loads[4].wait()

    def spread(ref, as_float):
        out = []
        for q in range(Q):
            value = jnp.where(x_line.first, ref[q : q + 1, :], ref[q + Q : q + Q + 1, :])
            out.append(value.astype(F32) if as_float else value)
        return out

    x_fwd, x_adj = x_line.bands(
        spread(f_vx, False), spread(f_disp, False), spread(f_wet, True), half_decay(sub_tracer)
    )
    put(first_v, x_adj["from_first"])
    put(last_v, x_adj["from_last"])

    loads[5].wait()
    shift = (ny * COLS).bit_length() - 1
    source = f_cells[...]
    row = lax.shift_right_logical(source, shift)
    owner_v[...] = lax.shift_right_logical(row, ROWS.bit_length() - 1)
    rows_v[...] = row - gx * ROWS
    cols_v[...] = (source & (ny * COLS - 1)) - gy * COLS
    row_iota = lax.broadcasted_iota(jnp.int32, (ROWS, LANES), 0)
    col_iota = lax.broadcasted_iota(jnp.int32, (COLS, LANES), 0)

    def lanes(tile, count):
        return pl.ds(pl.multiple_of(tile * LANES, LANES), count * LANES)

    loads[6].wait()

    def scatter(step, acc):
        base = pl.multiple_of(step * TILES, TILES)
        row_tile = rows_v[pl.ds(base, TILES), :]
        col_tile = cols_v[pl.ds(base, TILES), :]
        values = f_emis[:, lanes(base, TILES)]
        high = values.astype(BF16).astype(F32)
        low = values - high
        left, hots = [], []
        for i in range(TILES):
            mask = row_iota == row_tile[i : i + 1, :]
            part = slice(i * LANES, (i + 1) * LANES)
            left.append(
                jnp.concatenate(
                    [
                        jnp.where(mask, piece[t : t + 1, part], 0.0).astype(BF16)
                        for piece in (high, low)
                        for t in range(TR)
                    ],
                    axis=0,
                )
            )
            hots.append(jnp.where(col_iota == col_tile[i : i + 1, :], 1.0, 0.0).astype(BF16))
        hot = jnp.concatenate(hots, axis=1)
        onehot[:, lanes(base, TILES)] = hot
        return acc + lax.dot_general(
            jnp.concatenate(left, axis=1),
            hot,
            (((1,), (1,)), ((), ())),
            preferred_element_type=F32,
        )

    placed = lax.fori_loop(
        0, nsrc // LANES // TILES, scatter, jnp.zeros((2 * CELLS, COLS), F32)
    )
    loads[7].wait()
    work[...] = f_conc[...].reshape(CELLS, COLS) + (placed[:CELLS] + placed[CELLS:])
    fx_part = x_line.solve(x_fwd, column(work))
    x_send[0:8, :] = x_line.edges(fx_part)
    x_send[8:16, :] = jnp.where(x_line.last, x_fwd["from_last"][e], x_fwd["from_first"][0])
    x_send[16:24, :] = jnp.where(x_line.last, x_fwd["from_first"][e], x_fwd["from_last"][0])
    x_send[24:25, :] = jnp.maximum(f_vx[0:1, :], 0.0)
    x_send[25:26, :] = f_disp[0:1, :] * wet_f[0:1, :]
    x_send[26:27, :] = jnp.maximum(-f_vx[ROWS - 1 : ROWS, :], 0.0)
    x_send[27:28, :] = f_disp[ROWS - 1 : ROWS, :] * wet_f[ROWS - 1 : ROWS, :]
    x_send[28:32, :] = zero8[0:4]
    ends_a[0:8, :] = zero8
    ends_b[0:8, :] = zero8

    pl.semaphore_wait(barrier, ny - 1 + nx - 1 + 1)
    to_line(y_send, y_recv, 0)
    to_x(x_send, x_recv, 1)

    def split_bf16(values):
        high = values.astype(BF16)
        return jnp.concatenate([high, (values - high.astype(F32)).astype(BF16)], axis=1)

    def pick(fields, send, at):
        left = jnp.concatenate([split_bf16(field) for field in fields], axis=0)
        per_step = max(TILES, tiles)

        def go(step, _):
            base = pl.multiple_of(en * half_tiles + step * per_step, per_step)
            row_tile = rows_v[pl.ds(base, per_step), :]
            hot = onehot[:, lanes(base, per_step)]
            found = jnp.dot(left, jnp.concatenate([hot, hot], axis=0), preferred_element_type=F32)
            for i in range(per_step):
                mask = row_iota == row_tile[i : i + 1, :]
                block = step * (per_step // tiles) + i // tiles
                for k, first in enumerate(at):
                    for t in range(TR):
                        start = (k * TR + t) * ROWS
                        line = found[start : start + ROWS, i * LANES : (i + 1) * LANES]
                        line = jnp.sum(jnp.where(mask, line, 0.0), axis=0, keepdims=True)
                        spot = first + tiles * t + i % tiles
                        send[block, spot : spot + 1, :] = line
            return 0

        lax.fori_loop(0, half_tiles // per_step, go, 0)

    pick((first_v[...], last_v[...]), z_send, (0, TR * tiles))
    to_each_x(z_send, z_recv, 2)

    def x_piece(ref, k):
        return jnp.concatenate([ref[d, 8 * k : 8 * k + 8, :] for d in range(nx)], axis=0)

    def single(ref, k, n):
        return jnp.concatenate([ref[d, k : k + 1, :] for d in range(n)], axis=0)

    def expanded(rows):
        return jnp.concatenate(
            [jnp.broadcast_to(rows[d : d + 1], (8, LANES)) for d in range(nx)], axis=0
        )

    def from_next(value):
        later = rolled(value, -8)
        return jnp.concatenate([rolled(later[8 * d : 8 * d + 8], 1) for d in range(nx)], axis=0)

    def own_x(ref, at):
        block = ref[pl.ds(pl.multiple_of(8 * at, 8), 8), :]
        return jnp.where(x_line.last, block, rolled(block, -1))

    arrived(x_recv, nx - 1, 1)
    index = lax.broadcasted_iota(jnp.int32, (nx, LANES), 0)
    x_before, x_after = (
        expanded(face) for face in faces(*[single(x_recv, 24 + k, nx) for k in range(4)], index, nx)
    )
    diagonal, corner = x_piece(x_recv, 1), x_piece(x_recv, 2)
    x_below = -corner * rolled(x_after, 8)
    x_center = 1.0 + diagonal * x_before + from_next(diagonal) * x_after
    block_index = lax.broadcasted_iota(jnp.int32, (8 * nx, LANES), 0) // 8
    x_above = jnp.where(
        block_index == nx - 1, 0.0, -from_next(corner) * rolled(x_before, -8)
    )
    terms = x_piece(x_recv, 0)
    jump = pcr_apply(pcr_factor(x_below, x_center, x_above, nx, 8), terms - from_next(terms))
    ends_a[8 : 8 + 8 * nx, :] = x_after * jump
    ends_b[8 : 8 + 8 * nx, :] = x_before * jump
    put(work, x_line.finish(x_fwd, fx_part, own_x(ends_a, gx), -own_x(ends_b, gx + 1)))
    work_t[...] = jnp.transpose(work[...])
    fy_part = y_line.solve(y_fwd, column(work_t))
    yb_send[0:1, :] = fy_part[0][0:1]
    yb_send[1:2, :] = fy_part[e][7:8]
    yb_send[2:8, :] = zero8[0:6]
    to_line(yb_send, yb_recv, 3)
    x_factors = pcr_factor(rolled(x_above, 8), x_center, rolled(x_below, -8), nx, 8)

    arrived(y_recv, ny - 1, 0)
    raw = single(y_recv, 6, ny)
    tracer_n = jnp.broadcast_to(tracer_row, (ny, LANES))
    quantities = []
    for k in range(4):
        value = jnp.where(tracer_n == k, raw, 0.0)
        value = value + pltpu.roll(value, ROWS, 1)
        quantities.append(value + pltpu.roll(value, 2 * ROWS, 1))
    index = lax.broadcasted_iota(jnp.int32, (ny, LANES), 0)
    y_before, y_after = faces(*quantities, index, ny)
    g00, gnn, g0n, gn0 = (single(y_recv, k, ny) for k in (2, 3, 4, 5))
    y_below = -gn0 * rolled(y_after, 1)
    y_center = 1.0 + gnn * y_before + rolled(g00, -1) * y_after
    y_above = jnp.where(index == ny - 1, 0.0, -rolled(g0n * y_before, -1))
    y_factors = pcr_factor(rolled(y_above, 1), y_center, rolled(y_below, -1), ny, 1)
    ends_a[8 : 8 + ny, :] = pcr_apply(
        y_factors, y_before * single(y_recv, 1, ny) - y_after * rolled(single(y_recv, 0, ny), -1)
    )
    head, tail = ends_a[pl.ds(7 + gy, 1), :], -ends_a[pl.ds(8 + gy, 1), :]
    put(work_t, y_line.finish(y_adj, y_part, head, tail))
    work[...] = jnp.transpose(work_t[...])
    ax_part = x_line.solve(x_adj, column(work))
    put(adjoint_v, ax_part)
    to_mate = pltpu.make_async_remote_copy(
        src_ref=adjoint_v, dst_ref=mate_v, send_sem=mate_ssem.at[0], recv_sem=mate_rsem.at[0],
        device_id=mate, device_id_type=MESH,
    )
    to_mate.start()
    xb_send[...] = x_line.edges(ax_part)
    to_x(xb_send, xb_recv, 4)

    to_mate.wait_recv()
    both = adjoint_v[...] + mate_v[...]
    work[...] = both
    both_edges = x_line.edges([strided(work, q) if q in (0, e) else None for q in range(Q)])
    for d in range(nx):
        p_send[d, 0:8, :] = both_edges
    pick((both,), p_send, (8,))
    to_each_x(p_send, p_recv, 5)

    y_fwd_factors = pcr_factor(y_below, y_center, y_above, ny, 1)
    arrived(z_recv, nx - 1, 2)

    def summed(ref, first, count, n):
        value = ref[0, first : first + count, :]
        for i in range(1, n):
            value = value + ref[i, first : first + count, :]
        return value

    width = TR * tiles
    z_first, z_last = summed(z_recv, 0, width, nx), summed(z_recv, width, width, nx)

    arrived(p_recv, nx - 1, 5)

    def flux_of(ref):
        terms = x_piece(ref, 0)
        return pcr_apply(x_factors, x_before * terms - x_after * from_next(terms))

    flux = flux_of(p_recv)
    mine = pl.multiple_of(en * half_tiles + gx * tiles, tiles)
    hot = onehot[:, lanes(mine, tiles)]
    found = jnp.dot(
        split_bf16(flux), jnp.concatenate([hot, hot], axis=0), preferred_element_type=F32
    )
    owner = owner_v[pl.ds(mine, tiles), :]
    for i in range(tiles):
        into, out = zero8, zero8
        for d in range(nx):
            value = found[8 * d : 8 * d + 8, i * LANES : (i + 1) * LANES]
            into = into + jnp.where(owner[i : i + 1, :] == d + 1, value, 0.0)
            out = out + jnp.where(owner[i : i + 1, :] == d, value, 0.0)
        for t in range(TR):
            spot = slice(tiles * t + i, tiles * t + i + 1)
            at = slice(2 * t + 1, 2 * t + 2)
            g_send[spot, :] = z_first[spot] * into[at] - z_last[spot] * out[at]
    g_send[...] = g_send[...] + summed(p_recv, 8, width, nx)
    to_line(g_send, g_recv, 6)

    arrived(xb_recv, nx - 1, 4)
    ends_a[8 : 8 + 8 * nx, :] = flux_of(xb_recv)
    put(
        work,
        x_line.finish(x_adj, column(adjoint_v), own_x(ends_a, gx), -own_x(ends_a, gx + 1)),
    )
    adjoint_store = pltpu.make_async_copy(work, adjoint_out, out_sem.at[0])
    adjoint_store.start()

    arrived(yb_recv, ny - 1, 3)
    jump = pcr_apply(
        y_fwd_factors, single(yb_recv, 1, ny) - rolled(single(yb_recv, 0, ny), -1)
    )
    ends_a[8 : 8 + ny, :] = y_after * jump
    ends_b[8 : 8 + ny, :] = y_before * jump
    head, tail = ends_a[pl.ds(7 + gy, 1), :], -ends_b[pl.ds(8 + gy, 1), :]
    put(work_t, y_line.finish(y_fwd, fy_part, head, tail))
    state_v[...] = jnp.transpose(work_t[...])
    state_store = pltpu.make_async_copy(state_v, state_out, out_sem.at[1])
    state_store.start()

    arrived(g_recv, ny - 1, 6)
    sums = summed(g_recv, 0, width, ny)
    for t in range(TR):
        for i in range(tiles):
            total[t : t + 1, i * LANES : (i + 1) * LANES] = sums[tiles * t + i : tiles * t + i + 1]

    def span(start, size):
        return grad_v.at[:, pl.ds(pl.multiple_of(start, LANES), size)]

    here = en * half + gx * chunk
    for o in farthest_first(nx):
        pltpu.make_async_remote_copy(
            src_ref=total, dst_ref=span(here, chunk), send_sem=ssem.at[7], recv_sem=rsem.at[7],
            device_id=x_peer(o), device_id_type=MESH,
        ).start()
    grad_v[:, pl.ds(pl.multiple_of(here, LANES), chunk)] = total[...]

    sent(y_recv, ny - 1, 0)
    sent(x_recv, nx - 1, 1)
    sent(z_recv, nx - 1, 2)
    sent(yb_recv, ny - 1, 3)
    sent(xb_recv, nx - 1, 4)
    sent(p_recv, nx - 1, 5)
    sent(g_recv, ny - 1, 6)
    to_mate.wait_send()
    adjoint_store.wait()
    state_store.wait()

    rest = span(0, (nx - 1) * chunk)
    pltpu.make_async_copy(rest, rest, rsem.at[7]).wait()
    own_half = span(en * half, half)
    swap = pltpu.make_async_remote_copy(
        src_ref=own_half, dst_ref=own_half, send_sem=mate_ssem.at[1], recv_sem=mate_rsem.at[1],
        device_id=mate, device_id_type=MESH,
    )
    swap.start()
    pltpu.make_async_copy(rest, rest, ssem.at[7]).wait()
    swap.wait()
    grad_store = pltpu.make_async_copy(grad_v, grad_out, out_sem.at[2])
    grad_store.start()
    grad_store.wait()


def per_device(
    nx, ny, ne, concentration, cotangent, vel_x, vel_y, dispersion, wet_cells, decay_rate, emission,
    source_cell,
):
    nsrc = source_cell.shape[0]
    chunk = nsrc // (nx * ne)
    width = TR * chunk // LANES
    square = pltpu.VMEM((CELLS, COLS), F32)
    block = pltpu.VMEM((ROWS, COLS), F32)

    def vmem(*shape, dtype=F32):
        return pltpu.VMEM(shape, dtype)

    index = vmem(nsrc // LANES, LANES, dtype=jnp.int32)
    ends = vmem(8 + 8 * max(nx, ny), LANES)
    scratch = [
        block, block, block, vmem(ROWS, COLS, dtype=jnp.int32),
        vmem(TR, ROWS, COLS), vmem(TR, ROWS, COLS), vmem(TR, nsrc), index,
        square, square, square, square, square, square, square, square, square, square,
        vmem(COLS, nsrc, dtype=BF16), index, index, index,
        vmem(8, LANES), vmem(ny, 8, LANES), vmem(32, LANES), vmem(nx, 32, LANES),
        vmem(8, LANES), vmem(nx, 8, LANES), vmem(8, LANES), vmem(ny, 8, LANES), ends, ends,
        vmem(nx, 2 * width, LANES), vmem(nx, 2 * width, LANES),
        vmem(nx, 8 + width, LANES), vmem(nx, 8 + width, LANES),
        vmem(width, LANES), vmem(ny, width, LANES), vmem(TR, chunk), vmem(TR, nsrc),
        pltpu.SemaphoreType.DMA((8,)), pltpu.SemaphoreType.DMA((3,)),
        pltpu.SemaphoreType.DMA((2,)), pltpu.SemaphoreType.DMA((2,)),
        pltpu.SemaphoreType.DMA((8,)), pltpu.SemaphoreType.DMA((8,)),
    ]
    hbm = pl.BlockSpec(memory_space=pl.ANY)
    state, adjoint, gradient = pl.pallas_call(
        functools.partial(kernel, nx, ny, ne, nsrc),
        out_shape=(
            jax.ShapeDtypeStruct((CELLS, COLS), F32),
            jax.ShapeDtypeStruct((CELLS, COLS), F32),
            jax.ShapeDtypeStruct(emission.shape, F32),
        ),
        in_specs=[pl.BlockSpec(memory_space=pltpu.SMEM)] + [hbm] * 8,
        out_specs=(hbm, hbm, hbm),
        scratch_shapes=scratch,
        compiler_params=pltpu.CompilerParams(
            collective_id=0, has_side_effects=True, vmem_limit_bytes=VMEM_BYTES
        ),
        name="adi_step",
    )(
        decay_rate, concentration, cotangent, vel_x, vel_y, dispersion, wet_cells, emission,
        source_cell.reshape(nsrc // LANES, LANES),
    )
    shape = concentration.shape
    return (state.reshape(shape), adjoint.reshape(shape), gradient)


VMEM_BYTES = 60 * 1024 * 1024


def solution(mesh):
    nx, ny, ne = (mesh.shape[a] for a in ("gx", "gy", "ens"))
    field = P("ens", None, "gx", "gy")
    plane = P("gx", "gy")
    return jax.shard_map(
        functools.partial(per_device, nx, ny, ne),
        mesh=mesh,
        in_specs=(field, field, plane, plane, plane, plane, P(), P(), P()),
        out_specs=(field, field, P()),
        check_vma=False,
    )
```

```python
import functools

import jax
import jax.numpy as jnp
from jax import lax
from jax.experimental import pallas as pl
from jax.experimental.pallas import tpu as pltpu
from jax.sharding import PartitionSpec as P

MESH = pl.DeviceIdType.MESH
TR, ROWS, COLS, LANES, Q = 4, 32, 128, 128, 16
CELLS = TR * ROWS
F32, BF16 = jnp.float32, jnp.bfloat16
TILES = 8


def rolled(x, shift):
    n = x.shape[0]
    shift = shift % n
    if shift == 0:
        return x
    if shift % 8 == 0:
        return jnp.concatenate([x[n - shift :], x[: n - shift]], axis=0)
    return pltpu.roll(x, shift, 0)


def wrapped(i, n):
    return i & (n - 1) if n & (n - 1) == 0 else lax.rem(i, n)


def farthest_first(n):
    return sorted(range(1, n), key=lambda o: (-min(o, n - o), o))


def plane_order(n):
    far = (0, 1, 2, 1)
    return sorted(range(1, n), key=lambda o: -(far[o % 4] + far[o // 4 % 4]))


def pcr_factor(below, center, above, count, unit):
    steps, stride = [], 1
    while stride < count:
        k = stride * unit
        inverse = 1.0 / center
        alpha = -below * rolled(inverse, k)
        gamma = -above * rolled(inverse, -k)
        center = center + alpha * rolled(above, k) + gamma * rolled(below, -k)
        below, above = alpha * rolled(below, k), gamma * rolled(above, -k)
        steps.append((k, alpha, gamma))
        stride *= 2
    return steps, 1.0 / center


def pcr_apply(factors, side):
    steps, inverse = factors
    for k, alpha, gamma in steps:
        side = side + alpha * rolled(side, k) + gamma * rolled(side, -k)
    return side * inverse


class Line:
    def __init__(self, size):
        self.size = size
        sub = lax.broadcasted_iota(jnp.int32, (8, LANES), 0) % size
        self.first = sub == 0
        self.last = sub == size - 1

    def extended(self, cells):
        head = jnp.where(self.first, 0.0, rolled(cells[-1], 1))
        tail = jnp.where(self.last, 0.0, rolled(cells[0], -1))
        return [head] + cells + [tail]

    def bands(self, vel, disp, wet, half_decay):
        vel, disp, wet = (self.extended(cells) for cells in (vel, disp, wet))
        gate = [wet[k] * wet[k + 1] for k in range(Q + 1)]
        flux = [0.5 * (disp[k] + disp[k + 1]) * gate[k] for k in range(Q + 1)]
        plus = [jnp.maximum(v, 0.0) for v in vel]
        minus = [jnp.maximum(-v, 0.0) for v in vel]
        fwd_below = [-(flux[q] + plus[q + 1] * gate[q]) for q in range(Q)]
        fwd_above = [-(flux[q + 1] + minus[q + 1] * gate[q + 1]) for q in range(Q)]
        adj_below = [-(flux[q] + minus[q] * gate[q]) for q in range(Q)]
        adj_above = [-(flux[q + 1] + plus[q + 2] * gate[q + 1]) for q in range(Q)]
        center = [
            (1.0 + flux[q] + flux[q + 1] + plus[q + 1] * gate[q] + minus[q + 1] * gate[q + 1])
            + half_decay
            for q in range(Q)
        ]
        inverse = [1.0 / center[0]]
        for q in range(1, Q - 1):
            pivot = center[q] - fwd_below[q] * fwd_above[q - 1] * inverse[q - 1]
            inverse.append(1.0 / pivot)
        forward = self.factor(fwd_below, center, fwd_above, inverse)
        adjoint = self.factor(adj_below, center, adj_above, inverse)
        return forward, adjoint

    def factor(self, below, center, above, inverse):
        e = Q - 1
        fa = dict(inverse=inverse, below_end=below[e], above_end=above[e])
        fa["mult"] = mult = [None] + [below[q] * inverse[q - 1] for q in range(1, e)]
        fa["up"] = up = [above[q] * inverse[q] for q in range(e)]
        start = [-below[0]]
        for q in range(1, e):
            start.append(-mult[q] * start[q - 1])
        v, w = [None] * e, [None] * e
        v[e - 1] = start[e - 1] * inverse[e - 1]
        w[e - 1] = -up[e - 1]
        for q in range(e - 2, -1, -1):
            v[q] = start[q] * inverse[q] - up[q] * v[q + 1]
            w[q] = -up[q] * w[q + 1]
        fa["v"], fa["w"] = v, w
        fa["reduced"] = pcr_factor(
            below[e] * v[e - 1],
            center[e] + below[e] * w[e - 1] + above[e] * rolled(v[0], -1),
            above[e] * rolled(w[0], -1),
            self.size,
            1,
        )
        head = jnp.where(self.first, 1.0, 0.0)
        fa["from_first"] = self.solve(fa, [head] + [None] * e)
        fa["from_last"] = self.solve(fa, [None] * e + [jnp.where(self.last, 1.0, 0.0)])
        return fa

    def solve(self, fa, field):
        def plus(a, b):
            return b if a is None else a if b is None else a + b

        def times(a, b):
            return None if b is None else a * b

        e = Q - 1
        g = [field[0]]
        for q in range(1, e):
            g.append(plus(field[q], times(-fa["mult"][q], g[q - 1])))
        part = [None] * e
        part[e - 1] = times(fa["inverse"][e - 1], g[e - 1])
        for q in range(e - 2, -1, -1):
            part[q] = plus(times(fa["inverse"][q], g[q]), times(-fa["up"][q], part[q + 1]))
        side = plus(field[e], times(-fa["below_end"], part[e - 1]))
        if part[0] is not None:
            side = side - fa["above_end"] * rolled(part[0], -1)
        ends = pcr_apply(fa["reduced"], side)
        before = rolled(ends, 1)
        return [
            plus(part[q], fa["v"][q] * before + fa["w"][q] * ends) for q in range(e)
        ] + [ends]

    def finish(self, fa, part, head, tail):
        first, last = fa["from_first"], fa["from_last"]
        return [part[q] + first[q] * head + last[q] * tail for q in range(Q)]

    def edges(self, cells):
        return jnp.where(self.last, cells[Q - 1], cells[0])


def faces(plus_first, disp_first, minus_last, disp_last, index, count):
    disp_next = rolled(disp_first, -1)
    shut = (index == count - 1) | (disp_last <= 0.0) | (disp_next <= 0.0)
    flux = 0.5 * (disp_last + disp_next)
    return (
        jnp.where(shut, 0.0, flux + minus_last),
        jnp.where(shut, 0.0, flux + rolled(plus_first, -1)),
    )


def kernel(
    nx, ny, ne, nsrc,
    decay_in, conc, cot, vel_x, vel_y, disp, wet_cells, emission, cells,
    state_out, adjoint_out, grad_out,
    decay, f_vx, f_vy, f_disp, f_wet, f_conc, f_cot, f_emis, f_cells,
    vel_t, disp_t, wet_t, work, work_t, adjoint_v, mate_v, first_v, last_v,
    onehot, rows_v, cols_v, owner_v,
    y_send, y_recv, x_send, x_recv, xb_send, xb_recv, yb_send, yb_recv, ends_a, ends_b,
    z_send, z_recv, p_send, p_recv, g_send, g_recv, total,
    in_sem, mate_ssem, mate_rsem, ssem, rsem,
):
    gx, gy, en = lax.axis_index("gx"), lax.axis_index("gy"), lax.axis_index("ens")
    half = nsrc // ne
    chunk = half // nx
    tiles = chunk // LANES
    half_tiles = half // LANES
    mate = (gx, gy, wrapped(en + 1, ne))

    loads = [
        pltpu.make_async_copy(src, dst, in_sem.at[i])
        for i, (src, dst) in enumerate(
            [
                (vel_y, f_vy), (disp, f_disp), (wet_cells, f_wet), (cot.at[0], f_cot),
                (vel_x, f_vx), (cells, f_cells), (emission, f_emis), (conc.at[0], f_conc),
                (decay_in, decay),
            ]
        )
    ]

    def line_peer(o):
        return (gx, wrapped(gy + o, ny), en)

    def x_peer(o):
        return (gx ^ o, gy, en)

    def mate_peer(o):
        return (gx ^ o, gy, mate[2])

    barrier = pltpu.get_barrier_semaphore()
    greeted = [line_peer(o) for o in farthest_first(ny)]
    greeted += [peer(o) for o in plane_order(nx) for peer in (x_peer, mate_peer)] + [mate]
    for load in loads[:5]:
        load.start()
    for peer in greeted:
        pl.semaphore_signal(barrier, inc=1, device_id=peer, device_id_type=MESH)
    for load in loads[5:]:
        load.start()

    def to_line(send, recv, slot):
        for o in farthest_first(ny):
            pltpu.make_async_remote_copy(
                src_ref=send, dst_ref=recv.at[gy], send_sem=ssem.at[slot],
                recv_sem=rsem.at[slot], device_id=line_peer(o), device_id_type=MESH,
            ).start()
        recv[gy] = send[...]

    def to_x(send, recv, slot):
        for o in plane_order(nx):
            pltpu.make_async_remote_copy(
                src_ref=send, dst_ref=recv.at[gx], send_sem=ssem.at[slot],
                recv_sem=rsem.at[slot], device_id=x_peer(o), device_id_type=MESH,
            ).start()
        recv[gx] = send[...]

    def to_each_x(send, recv, slot):
        for o in plane_order(nx):
            peer = gx ^ o
            pltpu.make_async_remote_copy(
                src_ref=send.at[peer], dst_ref=recv.at[gx], send_sem=ssem.at[slot],
                recv_sem=rsem.at[slot], device_id=x_peer(o), device_id_type=MESH,
            ).start()
        recv[gx] = send[gx]

    def arrived(recv, count, slot):
        part = recv.at[pl.ds(0, count)]
        pltpu.make_async_copy(part, part, rsem.at[slot]).wait()

    def sent(recv, count, slot):
        part = recv.at[pl.ds(0, count)]
        pltpu.make_async_copy(part, part, ssem.at[slot]).wait()

    def strided(ref, q):
        return ref[pl.ds(q, 8, stride=Q), :]

    def column(ref):
        return [strided(ref, q) for q in range(Q)]

    def put(ref, cells_):
        for q in range(Q):
            ref[pl.ds(q, 8, stride=Q), :] = cells_[q]

    y_line, x_line = Line(8), Line(2)
    zero8 = jnp.zeros((8, LANES), F32)
    lane_tracer = lax.broadcasted_iota(jnp.int32, (8, LANES), 1) // ROWS
    sub_tracer = lax.broadcasted_iota(jnp.int32, (8, LANES), 0) // 2

    def half_decay(tracer):
        value = jnp.full((8, LANES), decay[TR - 1], F32)
        for t in range(TR - 1):
            value = jnp.where(tracer == t, decay[t], value)
        return 0.5 * value

    for i in (8, 0, 1, 2, 3):
        loads[i].wait()
    wet_f = f_wet[...].astype(F32)
    for field, ref in ((f_vy[...], vel_t), (f_disp[...], disp_t), (wet_f, wet_t)):
        ref[...] = jnp.transpose(jnp.concatenate([field] * TR, axis=0))
    work_t[...] = jnp.transpose(f_cot[...].reshape(CELLS, COLS))
    y_fwd, y_adj = y_line.bands(
        column(vel_t), column(disp_t), column(wet_t), half_decay(lane_tracer)
    )
    y_part = y_line.solve(y_adj, column(work_t))
    end = COLS - 1
    tracer_row = lane_tracer[0:1]
    packed = jnp.where(
        tracer_row == 0,
        jnp.maximum(vel_t[0:1, :], 0.0),
        jnp.where(
            tracer_row == 1,
            disp_t[0:1, :] * wet_t[0:1, :],
            jnp.where(
                tracer_row == 2,
                jnp.maximum(-vel_t[end : end + 1, :], 0.0),
                disp_t[end : end + 1, :] * wet_t[end : end + 1, :],
            ),
        ),
    )
    e = Q - 1
    for i, row in enumerate(
        (
            y_part[0][0:1], y_part[e][7:8], y_fwd["from_first"][0][0:1],
            y_fwd["from_last"][e][7:8], y_fwd["from_last"][0][0:1],
            y_fwd["from_first"][e][7:8], packed, zero8[0:1],
        )
    ):
        y_send[i : i + 1, :] = row

    loads[4].wait()

    def spread(ref, as_float):
        out = []
        for q in range(Q):
            value = jnp.where(x_line.first, ref[q : q + 1, :], ref[q + Q : q + Q + 1, :])
            out.append(value.astype(F32) if as_float else value)
        return out

    x_fwd, x_adj = x_line.bands(
        spread(f_vx, False), spread(f_disp, False), spread(f_wet, True), half_decay(sub_tracer)
    )
    put(first_v, x_adj["from_first"])
    put(last_v, x_adj["from_last"])

    loads[5].wait()
    shift = (ny * COLS).bit_length() - 1
    source = f_cells[...]
    row = lax.shift_right_logical(source, shift)
    owner_v[...] = lax.shift_right_logical(row, ROWS.bit_length() - 1)
    rows_v[...] = row - gx * ROWS
    cols_v[...] = (source & (ny * COLS - 1)) - gy * COLS
    row_iota = lax.broadcasted_iota(jnp.int32, (ROWS, LANES), 0)
    col_iota = lax.broadcasted_iota(jnp.int32, (COLS, LANES), 0)

    def lanes(tile, count):
        return pl.ds(pl.multiple_of(tile * LANES, LANES), count * LANES)

    loads[6].wait()

    def scatter(step, acc):
        base = pl.multiple_of(step * TILES, TILES)
        row_tile = rows_v[pl.ds(base, TILES), :]
        col_tile = cols_v[pl.ds(base, TILES), :]
        values = f_emis[:, lanes(base, TILES)]
        high = values.astype(BF16).astype(F32)
        low = values - high
        left, hots = [], []
        for i in range(TILES):
            mask = row_iota == row_tile[i : i + 1, :]
            part = slice(i * LANES, (i + 1) * LANES)
            left.append(
                jnp.concatenate(
                    [
                        jnp.where(mask, piece[t : t + 1, part], 0.0).astype(BF16)
                        for piece in (high, low)
                        for t in range(TR)
                    ],
                    axis=0,
                )
            )
            hots.append(jnp.where(col_iota == col_tile[i : i + 1, :], 1.0, 0.0).astype(BF16))
        hot = jnp.concatenate(hots, axis=1)
        onehot[:, lanes(base, TILES)] = hot
        return acc + lax.dot_general(
            jnp.concatenate(left, axis=1),
            hot,
            (((1,), (1,)), ((), ())),
            preferred_element_type=F32,
        )

    placed = lax.fori_loop(
        0, nsrc // LANES // TILES, scatter, jnp.zeros((2 * CELLS, COLS), F32)
    )
    loads[7].wait()
    work[...] = f_conc[...].reshape(CELLS, COLS) + (placed[:CELLS] + placed[CELLS:])
    fx_part = x_line.solve(x_fwd, column(work))
    x_send[0:8, :] = x_line.edges(fx_part)
    x_send[8:16, :] = jnp.where(x_line.last, x_fwd["from_last"][e], x_fwd["from_first"][0])
    x_send[16:24, :] = jnp.where(x_line.last, x_fwd["from_first"][e], x_fwd["from_last"][0])
    x_send[24:25, :] = jnp.maximum(f_vx[0:1, :], 0.0)
    x_send[25:26, :] = f_disp[0:1, :] * wet_f[0:1, :]
    x_send[26:27, :] = jnp.maximum(-f_vx[ROWS - 1 : ROWS, :], 0.0)
    x_send[27:28, :] = f_disp[ROWS - 1 : ROWS, :] * wet_f[ROWS - 1 : ROWS, :]
    x_send[28:32, :] = zero8[0:4]
    ends_a[0:8, :] = zero8
    ends_b[0:8, :] = zero8

    pl.semaphore_wait(barrier, len(greeted))
    to_line(y_send, y_recv, 0)
    to_x(x_send, x_recv, 1)

    def split_bf16(values):
        high = values.astype(BF16)
        return jnp.concatenate([high, (values - high.astype(F32)).astype(BF16)], axis=1)

    def pick(fields, send, at):
        left = jnp.concatenate([split_bf16(field) for field in fields], axis=0)
        per_step = max(TILES, tiles)

        def go(step, _):
            base = pl.multiple_of(en * half_tiles + step * per_step, per_step)
            row_tile = rows_v[pl.ds(base, per_step), :]
            hot = onehot[:, lanes(base, per_step)]
            found = jnp.dot(left, jnp.concatenate([hot, hot], axis=0), preferred_element_type=F32)
            for i in range(per_step):
                mask = row_iota == row_tile[i : i + 1, :]
                block = step * (per_step // tiles) + i // tiles
                for k, first in enumerate(at):
                    for t in range(TR):
                        start = (k * TR + t) * ROWS
                        line = found[start : start + ROWS, i * LANES : (i + 1) * LANES]
                        line = jnp.sum(jnp.where(mask, line, 0.0), axis=0, keepdims=True)
                        spot = first + tiles * t + i % tiles
                        send[block, spot : spot + 1, :] = line
            return 0

        lax.fori_loop(0, half_tiles // per_step, go, 0)

    pick((first_v[...], last_v[...]), z_send, (0, TR * tiles))
    to_each_x(z_send, z_recv, 2)

    def x_piece(ref, k):
        return jnp.concatenate([ref[d, 8 * k : 8 * k + 8, :] for d in range(nx)], axis=0)

    def single(ref, k, n):
        return jnp.concatenate([ref[d, k : k + 1, :] for d in range(n)], axis=0)

    def expanded(rows):
        return jnp.concatenate(
            [jnp.broadcast_to(rows[d : d + 1], (8, LANES)) for d in range(nx)], axis=0
        )

    def from_next(value):
        later = rolled(value, -8)
        return jnp.concatenate([rolled(later[8 * d : 8 * d + 8], 1) for d in range(nx)], axis=0)

    def own_x(ref, at):
        block = ref[pl.ds(pl.multiple_of(8 * at, 8), 8), :]
        return jnp.where(x_line.last, block, rolled(block, -1))

    arrived(x_recv, nx - 1, 1)
    index = lax.broadcasted_iota(jnp.int32, (nx, LANES), 0)
    x_before, x_after = (
        expanded(face) for face in faces(*[single(x_recv, 24 + k, nx) for k in range(4)], index, nx)
    )
    diagonal, corner = x_piece(x_recv, 1), x_piece(x_recv, 2)
    x_below = -corner * rolled(x_after, 8)
    x_center = 1.0 + diagonal * x_before + from_next(diagonal) * x_after
    block_index = lax.broadcasted_iota(jnp.int32, (8 * nx, LANES), 0) // 8
    x_above = jnp.where(
        block_index == nx - 1, 0.0, -from_next(corner) * rolled(x_before, -8)
    )
    terms = x_piece(x_recv, 0)
    jump = pcr_apply(pcr_factor(x_below, x_center, x_above, nx, 8), terms - from_next(terms))
    ends_a[8 : 8 + 8 * nx, :] = x_after * jump
    ends_b[8 : 8 + 8 * nx, :] = x_before * jump
    put(work, x_line.finish(x_fwd, fx_part, own_x(ends_a, gx), -own_x(ends_b, gx + 1)))
    work_t[...] = jnp.transpose(work[...])
    fy_part = y_line.solve(y_fwd, column(work_t))
    yb_send[0:1, :] = fy_part[0][0:1]
    yb_send[1:2, :] = fy_part[e][7:8]
    yb_send[2:8, :] = zero8[0:6]
    to_line(yb_send, yb_recv, 3)
    x_factors = pcr_factor(rolled(x_above, 8), x_center, rolled(x_below, -8), nx, 8)

    arrived(y_recv, ny - 1, 0)
    raw = single(y_recv, 6, ny)
    tracer_n = jnp.broadcast_to(tracer_row, (ny, LANES))
    quantities = []
    for k in range(4):
        value = jnp.where(tracer_n == k, raw, 0.0)
        value = value + pltpu.roll(value, ROWS, 1)
        quantities.append(value + pltpu.roll(value, 2 * ROWS, 1))
    index = lax.broadcasted_iota(jnp.int32, (ny, LANES), 0)
    y_before, y_after = faces(*quantities, index, ny)
    g00, gnn, g0n, gn0 = (single(y_recv, k, ny) for k in (2, 3, 4, 5))
    y_below = -gn0 * rolled(y_after, 1)
    y_center = 1.0 + gnn * y_before + rolled(g00, -1) * y_after
    y_above = jnp.where(index == ny - 1, 0.0, -rolled(g0n * y_before, -1))
    y_factors = pcr_factor(rolled(y_above, 1), y_center, rolled(y_below, -1), ny, 1)
    ends_a[8 : 8 + ny, :] = pcr_apply(
        y_factors, y_before * single(y_recv, 1, ny) - y_after * rolled(single(y_recv, 0, ny), -1)
    )
    head, tail = ends_a[pl.ds(7 + gy, 1), :], -ends_a[pl.ds(8 + gy, 1), :]
    put(work_t, y_line.finish(y_adj, y_part, head, tail))
    work[...] = jnp.transpose(work_t[...])
    ax_part = x_line.solve(x_adj, column(work))
    put(adjoint_v, ax_part)
    to_mate = pltpu.make_async_remote_copy(
        src_ref=adjoint_v, dst_ref=mate_v, send_sem=mate_ssem.at[0], recv_sem=mate_rsem.at[0],
        device_id=mate, device_id_type=MESH,
    )
    to_mate.start()
    xb_send[...] = x_line.edges(ax_part)
    to_x(xb_send, xb_recv, 4)

    to_mate.wait_recv()
    both = adjoint_v[...] + mate_v[...]
    work[...] = both
    both_edges = x_line.edges([strided(work, q) if q in (0, e) else None for q in range(Q)])
    for d in range(nx):
        p_send[d, 0:8, :] = both_edges
    pick((both,), p_send, (8,))
    to_each_x(p_send, p_recv, 5)

    y_fwd_factors = pcr_factor(y_below, y_center, y_above, ny, 1)
    arrived(z_recv, nx - 1, 2)

    def summed(ref, first, count, n):
        value = ref[0, first : first + count, :]
        for i in range(1, n):
            value = value + ref[i, first : first + count, :]
        return value

    width = TR * tiles
    z_first, z_last = summed(z_recv, 0, width, nx), summed(z_recv, width, width, nx)

    arrived(p_recv, nx - 1, 5)

    def flux_of(ref):
        terms = x_piece(ref, 0)
        return pcr_apply(x_factors, x_before * terms - x_after * from_next(terms))

    flux = flux_of(p_recv)
    mine = pl.multiple_of(en * half_tiles + gx * tiles, tiles)
    hot = onehot[:, lanes(mine, tiles)]
    found = jnp.dot(
        split_bf16(flux), jnp.concatenate([hot, hot], axis=0), preferred_element_type=F32
    )
    owner = owner_v[pl.ds(mine, tiles), :]
    for i in range(tiles):
        into, out = zero8, zero8
        for d in range(nx):
            value = found[8 * d : 8 * d + 8, i * LANES : (i + 1) * LANES]
            into = into + jnp.where(owner[i : i + 1, :] == d + 1, value, 0.0)
            out = out + jnp.where(owner[i : i + 1, :] == d, value, 0.0)
        for t in range(TR):
            spot = slice(tiles * t + i, tiles * t + i + 1)
            at = slice(2 * t + 1, 2 * t + 2)
            g_send[spot, :] = z_first[spot] * into[at] - z_last[spot] * out[at]
    g_send[...] = g_send[...] + summed(p_recv, 8, width, nx)
    to_line(g_send, g_recv, 6)

    arrived(xb_recv, nx - 1, 4)
    ends_a[8 : 8 + 8 * nx, :] = flux_of(xb_recv)
    put(
        adjoint_out,
        x_line.finish(x_adj, column(adjoint_v), own_x(ends_a, gx), -own_x(ends_a, gx + 1)),
    )

    arrived(yb_recv, ny - 1, 3)
    jump = pcr_apply(
        y_fwd_factors, single(yb_recv, 1, ny) - rolled(single(yb_recv, 0, ny), -1)
    )
    ends_a[8 : 8 + ny, :] = y_after * jump
    ends_b[8 : 8 + ny, :] = y_before * jump
    head, tail = ends_a[pl.ds(7 + gy, 1), :], -ends_b[pl.ds(8 + gy, 1), :]
    put(work_t, y_line.finish(y_fwd, fy_part, head, tail))
    state_out[...] = jnp.transpose(work_t[...])

    arrived(g_recv, ny - 1, 6)
    sums = summed(g_recv, 0, width, ny)
    for t in range(TR):
        for i in range(tiles):
            total[t : t + 1, i * LANES : (i + 1) * LANES] = sums[tiles * t + i : tiles * t + i + 1]

    here = grad_out.at[:, pl.ds(pl.multiple_of(en * half + gx * chunk, LANES), chunk)]
    peers = [peer(o) for o in plane_order(nx) for peer in (x_peer, mate_peer)] + [mate]
    for peer in peers:
        pltpu.make_async_remote_copy(
            src_ref=total, dst_ref=here, send_sem=ssem.at[7], recv_sem=rsem.at[7],
            device_id=peer, device_id_type=MESH,
        ).start()
    grad_out[:, pl.ds(pl.multiple_of(en * half + gx * chunk, LANES), chunk)] = total[...]

    sent(y_recv, ny - 1, 0)
    sent(x_recv, nx - 1, 1)
    sent(z_recv, nx - 1, 2)
    sent(yb_recv, ny - 1, 3)
    sent(xb_recv, nx - 1, 4)
    sent(p_recv, nx - 1, 5)
    sent(g_recv, ny - 1, 6)
    to_mate.wait_send()

    rest = grad_out.at[:, pl.ds(0, len(peers) * chunk)]
    pltpu.make_async_copy(rest, rest, ssem.at[7]).wait()
    pltpu.make_async_copy(rest, rest, rsem.at[7]).wait()


def store(state, adjoint, gradient, state_out, adjoint_out, grad_out, sem):
    moves = ((gradient, grad_out), (state, state_out), (adjoint, adjoint_out))
    copies = [pltpu.make_async_copy(m[0], m[1], sem.at[i]) for i, m in enumerate(moves)]
    for copy in copies:
        copy.start()
    for copy in copies:
        copy.wait()


def per_device(
    nx, ny, ne, concentration, cotangent, vel_x, vel_y, dispersion, wet_cells, decay_rate, emission,
    source_cell,
):
    nsrc = source_cell.shape[0]
    chunk = nsrc // (nx * ne)
    operands = [
        pltpu.with_memory_space_constraint(x, pltpu.HBM)
        for x in (
            decay_rate, concentration, cotangent, vel_x, vel_y, dispersion, wet_cells, emission,
            source_cell.reshape(nsrc // LANES, LANES),
        )
    ]
    width = TR * chunk // LANES
    square = pltpu.VMEM((CELLS, COLS), F32)
    block = pltpu.VMEM((ROWS, COLS), F32)

    def vmem(*shape, dtype=F32):
        return pltpu.VMEM(shape, dtype)

    index = vmem(nsrc // LANES, LANES, dtype=jnp.int32)
    ends = vmem(8 + 8 * max(nx, ny), LANES)
    scratch = [
        pltpu.SMEM((TR,), F32), block, block, block, vmem(ROWS, COLS, dtype=jnp.int32),
        vmem(TR, ROWS, COLS), vmem(TR, ROWS, COLS), vmem(TR, nsrc), index,
        square, square, square, square, square, square, square, square, square,
        vmem(COLS, nsrc, dtype=BF16), index, index, index,
        vmem(8, LANES), vmem(ny, 8, LANES), vmem(32, LANES), vmem(nx, 32, LANES),
        vmem(8, LANES), vmem(nx, 8, LANES), vmem(8, LANES), vmem(ny, 8, LANES), ends, ends,
        vmem(nx, 2 * width, LANES), vmem(nx, 2 * width, LANES),
        vmem(nx, 8 + width, LANES), vmem(nx, 8 + width, LANES),
        vmem(width, LANES), vmem(ny, width, LANES), vmem(TR, chunk),
        pltpu.SemaphoreType.DMA((9,)),
        pltpu.SemaphoreType.DMA((1,)), pltpu.SemaphoreType.DMA((1,)),
        pltpu.SemaphoreType.DMA((8,)), pltpu.SemaphoreType.DMA((8,)),
    ]
    hbm = pl.BlockSpec(memory_space=pl.ANY)
    on_chip = pl.BlockSpec(memory_space=pltpu.VMEM)
    state, adjoint, gradient = pl.pallas_call(
        functools.partial(kernel, nx, ny, ne, nsrc),
        out_shape=(
            jax.ShapeDtypeStruct((CELLS, COLS), F32),
            jax.ShapeDtypeStruct((CELLS, COLS), F32),
            jax.ShapeDtypeStruct(emission.shape, F32),
        ),
        in_specs=[hbm] * 9,
        out_specs=(on_chip, on_chip, on_chip),
        scratch_shapes=scratch,
        compiler_params=pltpu.CompilerParams(
            collective_id=0, has_side_effects=True, vmem_limit_bytes=VMEM_BYTES
        ),
        name="adi_step",
    )(*operands)
    shape = concentration.shape
    return pl.pallas_call(
        store,
        out_shape=(
            jax.ShapeDtypeStruct(shape, F32),
            jax.ShapeDtypeStruct(shape, F32),
            jax.ShapeDtypeStruct(emission.shape, F32),
        ),
        in_specs=[on_chip] * 3,
        out_specs=(hbm, hbm, hbm),
        scratch_shapes=[pltpu.SemaphoreType.DMA((3,))],
        compiler_params=pltpu.CompilerParams(vmem_limit_bytes=VMEM_BYTES),
        name="store",
    )(state.reshape(shape), adjoint.reshape(shape), gradient)


VMEM_BYTES = 32 * 1024 * 1024


def solution(mesh):
    nx, ny, ne = (mesh.shape[a] for a in ("gx", "gy", "ens"))
    field = P("ens", None, "gx", "gy")
    plane = P("gx", "gy")
    return jax.shard_map(
        functools.partial(per_device, nx, ny, ne),
        mesh=mesh,
        in_specs=(field, field, plane, plane, plane, plane, P(), P(), P()),
        out_specs=(field, field, P()),
        check_vma=False,
    )
```

```python
import functools

import jax
import jax.numpy as jnp
from jax import lax
from jax.experimental import pallas as pl
from jax.experimental.pallas import tpu as pltpu
from jax.sharding import PartitionSpec as P

MESH = pl.DeviceIdType.MESH
TR, ROWS, COLS, LANES, Q = 4, 32, 128, 128, 16
CELLS = TR * ROWS
F32, BF16 = jnp.float32, jnp.bfloat16
TILES = 8


def rolled(x, shift):
    n = x.shape[0]
    shift = shift % n
    if shift == 0:
        return x
    if shift % 8 == 0:
        return jnp.concatenate([x[n - shift :], x[: n - shift]], axis=0)
    return pltpu.roll(x, shift, 0)


def wrapped(i, n):
    return i & (n - 1) if n & (n - 1) == 0 else lax.rem(i, n)


def farthest_first(n):
    return sorted(range(1, n), key=lambda o: (-min(o, n - o), o))


def plane_order(n):
    far = (0, 1, 2, 1)
    return sorted(range(1, n), key=lambda o: -(far[o % 4] + far[o // 4 % 4]))


def pcr_factor(below, center, above, count, unit):
    steps, stride = [], 1
    while stride < count:
        k = stride * unit
        inverse = 1.0 / center
        alpha = -below * rolled(inverse, k)
        gamma = -above * rolled(inverse, -k)
        center = center + alpha * rolled(above, k) + gamma * rolled(below, -k)
        below, above = alpha * rolled(below, k), gamma * rolled(above, -k)
        steps.append((k, alpha, gamma))
        stride *= 2
    return steps, 1.0 / center


def pcr_apply(factors, side):
    steps, inverse = factors
    for k, alpha, gamma in steps:
        side = side + alpha * rolled(side, k) + gamma * rolled(side, -k)
    return side * inverse


class Line:
    def __init__(self, size):
        self.size = size
        sub = lax.broadcasted_iota(jnp.int32, (8, LANES), 0) % size
        self.first = sub == 0
        self.last = sub == size - 1

    def extended(self, cells):
        head = jnp.where(self.first, 0.0, rolled(cells[-1], 1))
        tail = jnp.where(self.last, 0.0, rolled(cells[0], -1))
        return [head] + cells + [tail]

    def bands(self, vel, disp, wet, half_decay):
        vel, disp, wet = (self.extended(cells) for cells in (vel, disp, wet))
        gate = [wet[k] * wet[k + 1] for k in range(Q + 1)]
        flux = [0.5 * (disp[k] + disp[k + 1]) * gate[k] for k in range(Q + 1)]
        plus = [jnp.maximum(v, 0.0) for v in vel]
        minus = [jnp.maximum(-v, 0.0) for v in vel]
        fwd_below = [-(flux[q] + plus[q + 1] * gate[q]) for q in range(Q)]
        fwd_above = [-(flux[q + 1] + minus[q + 1] * gate[q + 1]) for q in range(Q)]
        adj_below = [-(flux[q] + minus[q] * gate[q]) for q in range(Q)]
        adj_above = [-(flux[q + 1] + plus[q + 2] * gate[q + 1]) for q in range(Q)]
        center = [
            (1.0 + flux[q] + flux[q + 1] + plus[q + 1] * gate[q] + minus[q + 1] * gate[q + 1])
            + half_decay
            for q in range(Q)
        ]
        inverse = [1.0 / center[0]]
        for q in range(1, Q - 1):
            pivot = center[q] - fwd_below[q] * fwd_above[q - 1] * inverse[q - 1]
            inverse.append(1.0 / pivot)
        forward = self.factor(fwd_below, center, fwd_above, inverse)
        adjoint = self.factor(adj_below, center, adj_above, inverse)
        return forward, adjoint

    def factor(self, below, center, above, inverse):
        e = Q - 1
        fa = dict(inverse=inverse, below_end=below[e], above_end=above[e])
        fa["mult"] = mult = [None] + [below[q] * inverse[q - 1] for q in range(1, e)]
        fa["up"] = up = [above[q] * inverse[q] for q in range(e)]
        start = [-below[0]]
        for q in range(1, e):
            start.append(-mult[q] * start[q - 1])
        v, w = [None] * e, [None] * e
        v[e - 1] = start[e - 1] * inverse[e - 1]
        w[e - 1] = -up[e - 1]
        for q in range(e - 2, -1, -1):
            v[q] = start[q] * inverse[q] - up[q] * v[q + 1]
            w[q] = -up[q] * w[q + 1]
        fa["v"], fa["w"] = v, w
        fa["reduced"] = pcr_factor(
            below[e] * v[e - 1],
            center[e] + below[e] * w[e - 1] + above[e] * rolled(v[0], -1),
            above[e] * rolled(w[0], -1),
            self.size,
            1,
        )
        head = jnp.where(self.first, 1.0, 0.0)
        fa["from_first"] = self.solve(fa, [head] + [None] * e)
        fa["from_last"] = self.solve(fa, [None] * e + [jnp.where(self.last, 1.0, 0.0)])
        return fa

    def solve(self, fa, field):
        def plus(a, b):
            return b if a is None else a if b is None else a + b

        def times(a, b):
            return None if b is None else a * b

        e = Q - 1
        g = [field[0]]
        for q in range(1, e):
            g.append(plus(field[q], times(-fa["mult"][q], g[q - 1])))
        part = [None] * e
        part[e - 1] = times(fa["inverse"][e - 1], g[e - 1])
        for q in range(e - 2, -1, -1):
            part[q] = plus(times(fa["inverse"][q], g[q]), times(-fa["up"][q], part[q + 1]))
        side = plus(field[e], times(-fa["below_end"], part[e - 1]))
        if part[0] is not None:
            side = side - fa["above_end"] * rolled(part[0], -1)
        ends = pcr_apply(fa["reduced"], side)
        before = rolled(ends, 1)
        return [
            plus(part[q], fa["v"][q] * before + fa["w"][q] * ends) for q in range(e)
        ] + [ends]

    def finish(self, fa, part, head, tail):
        first, last = fa["from_first"], fa["from_last"]
        return [part[q] + first[q] * head + last[q] * tail for q in range(Q)]

    def edges(self, cells):
        return jnp.where(self.last, cells[Q - 1], cells[0])


def faces(plus_first, disp_first, minus_last, disp_last, index, count):
    disp_next = rolled(disp_first, -1)
    shut = (index == count - 1) | (disp_last <= 0.0) | (disp_next <= 0.0)
    flux = 0.5 * (disp_last + disp_next)
    return (
        jnp.where(shut, 0.0, flux + minus_last),
        jnp.where(shut, 0.0, flux + rolled(plus_first, -1)),
    )


def kernel(
    nx, ny, ne, nsrc,
    decay_in, conc, cot, vel_x, vel_y, disp, wet_cells, emission, cells,
    state_out, adjoint_out, grad_out,
    decay, f_vx, f_vy, f_disp, f_wet, f_conc, f_cot, f_emis, f_cells,
    vel_t, disp_t, wet_t, work, work_t, adjoint_v, mate_v, first_v, last_v,
    onehot, rows_v, cols_v, owner_v,
    y_send, y_recv, x_send, x_recv, xb_send, xb_recv, yb_send, yb_recv, ends_a, ends_b,
    z_send, z_recv, p_send, p_recv, g_send, g_recv, total,
    in_sem, mate_ssem, mate_rsem, ssem, rsem,
):
    gx, gy, en = lax.axis_index("gx"), lax.axis_index("gy"), lax.axis_index("ens")
    half = nsrc // ne
    chunk = half // nx
    tiles = chunk // LANES
    half_tiles = half // LANES
    mate = (gx, gy, wrapped(en + 1, ne))
    assert tiles == 2

    loads = [
        pltpu.make_async_copy(src, dst, in_sem.at[i])
        for i, (src, dst) in enumerate(
            [
                (vel_y, f_vy), (disp, f_disp), (wet_cells, f_wet), (cot.at[0], f_cot),
                (vel_x, f_vx), (cells, f_cells), (emission, f_emis), (conc.at[0], f_conc),
                (decay_in, decay),
            ]
        )
    ]

    def line_peer(o):
        return (gx, wrapped(gy + o, ny), en)

    def x_peer(o):
        return (gx ^ o, gy, en)

    def mate_peer(o):
        return (gx ^ o, gy, mate[2])

    barrier = pltpu.get_barrier_semaphore()
    greeted = [line_peer(o) for o in farthest_first(ny)]
    greeted += [peer(o) for o in plane_order(nx) for peer in (x_peer, mate_peer)] + [mate]
    for load in loads[:5]:
        load.start()
    for peer in greeted:
        pl.semaphore_signal(barrier, inc=1, device_id=peer, device_id_type=MESH)
    for load in loads[5:]:
        load.start()

    def to_line(send, recv, slot):
        for o in farthest_first(ny):
            pltpu.make_async_remote_copy(
                src_ref=send, dst_ref=recv.at[gy], send_sem=ssem.at[slot],
                recv_sem=rsem.at[slot], device_id=line_peer(o), device_id_type=MESH,
            ).start()
        recv[gy] = send[...]

    def to_x(send, recv, slot):
        for o in plane_order(nx):
            pltpu.make_async_remote_copy(
                src_ref=send, dst_ref=recv.at[gx], send_sem=ssem.at[slot],
                recv_sem=rsem.at[slot], device_id=x_peer(o), device_id_type=MESH,
            ).start()
        recv[gx] = send[...]

    def to_each_x(send, recv, slot):
        for o in plane_order(nx):
            peer = gx ^ o
            pltpu.make_async_remote_copy(
                src_ref=send.at[peer], dst_ref=recv.at[gx], send_sem=ssem.at[slot],
                recv_sem=rsem.at[slot], device_id=x_peer(o), device_id_type=MESH,
            ).start()
        recv[gx] = send[gx]

    def arrived(recv, count, slot):
        part = recv.at[pl.ds(0, count)]
        pltpu.make_async_copy(part, part, rsem.at[slot]).wait()

    def sent(recv, count, slot):
        part = recv.at[pl.ds(0, count)]
        pltpu.make_async_copy(part, part, ssem.at[slot]).wait()

    def strided(ref, q):
        return ref[pl.ds(q, 8, stride=Q), :]

    def column(ref):
        return [strided(ref, q) for q in range(Q)]

    def put(ref, cells_):
        for q in range(Q):
            ref[pl.ds(q, 8, stride=Q), :] = cells_[q]

    y_line, x_line = Line(8), Line(2)
    zero8 = jnp.zeros((8, LANES), F32)
    lane_tracer = lax.broadcasted_iota(jnp.int32, (8, LANES), 1) // ROWS
    sub_tracer = lax.broadcasted_iota(jnp.int32, (8, LANES), 0) // 2

    def half_decay(tracer):
        value = jnp.full((8, LANES), decay[TR - 1], F32)
        for t in range(TR - 1):
            value = jnp.where(tracer == t, decay[t], value)
        return 0.5 * value

    for i in (8, 0, 1, 2, 3):
        loads[i].wait()
    wet_f = f_wet[...].astype(F32)
    for field, ref in ((f_vy[...], vel_t), (f_disp[...], disp_t), (wet_f, wet_t)):
        ref[...] = jnp.transpose(jnp.concatenate([field] * TR, axis=0))
    work_t[...] = jnp.transpose(f_cot[...].reshape(CELLS, COLS))
    y_fwd, y_adj = y_line.bands(
        column(vel_t), column(disp_t), column(wet_t), half_decay(lane_tracer)
    )
    y_part = y_line.solve(y_adj, column(work_t))
    end = COLS - 1
    tracer_row = lane_tracer[0:1]
    packed = jnp.where(
        tracer_row == 0,
        jnp.maximum(vel_t[0:1, :], 0.0),
        jnp.where(
            tracer_row == 1,
            disp_t[0:1, :] * wet_t[0:1, :],
            jnp.where(
                tracer_row == 2,
                jnp.maximum(-vel_t[end : end + 1, :], 0.0),
                disp_t[end : end + 1, :] * wet_t[end : end + 1, :],
            ),
        ),
    )
    e = Q - 1
    for i, row in enumerate(
        (
            y_part[0][0:1], y_part[e][7:8], y_fwd["from_first"][0][0:1],
            y_fwd["from_last"][e][7:8], y_fwd["from_last"][0][0:1],
            y_fwd["from_first"][e][7:8], packed, zero8[0:1],
        )
    ):
        y_send[i : i + 1, :] = row

    loads[4].wait()

    def spread(ref, as_float):
        out = []
        for q in range(Q):
            value = jnp.where(x_line.first, ref[q : q + 1, :], ref[q + Q : q + Q + 1, :])
            out.append(value.astype(F32) if as_float else value)
        return out

    x_fwd, x_adj = x_line.bands(
        spread(f_vx, False), spread(f_disp, False), spread(f_wet, True), half_decay(sub_tracer)
    )
    put(first_v, x_adj["from_first"])
    put(last_v, x_adj["from_last"])

    loads[5].wait()
    shift = (ny * COLS).bit_length() - 1
    source = f_cells[...]
    row = lax.shift_right_logical(source, shift)
    owner_v[...] = lax.shift_right_logical(row, ROWS.bit_length() - 1)
    rows_v[...] = row - gx * ROWS
    cols_v[...] = (source & (ny * COLS - 1)) - gy * COLS
    row_iota = lax.broadcasted_iota(jnp.int32, (ROWS, LANES), 0)
    col_iota = lax.broadcasted_iota(jnp.int32, (COLS, LANES), 0)

    def lanes(tile, count):
        return pl.ds(pl.multiple_of(tile * LANES, LANES), count * LANES)

    loads[6].wait()

    def scatter(step, acc):
        base = pl.multiple_of(step * TILES, TILES)
        row_tile = rows_v[pl.ds(base, TILES), :]
        col_tile = cols_v[pl.ds(base, TILES), :]
        values = f_emis[:, lanes(base, TILES)]
        high = values.astype(BF16).astype(F32)
        low = values - high
        left, hots = [], []
        for i in range(TILES):
            mask = row_iota == row_tile[i : i + 1, :]
            part = slice(i * LANES, (i + 1) * LANES)
            left.append(
                jnp.concatenate(
                    [
                        jnp.where(mask, piece[t : t + 1, part], 0.0).astype(BF16)
                        for piece in (high, low)
                        for t in range(TR)
                    ],
                    axis=0,
                )
            )
            hots.append(jnp.where(col_iota == col_tile[i : i + 1, :], 1.0, 0.0).astype(BF16))
        hot = jnp.concatenate(hots, axis=1)
        onehot[:, lanes(base, TILES)] = hot
        return acc + lax.dot_general(
            jnp.concatenate(left, axis=1),
            hot,
            (((1,), (1,)), ((), ())),
            preferred_element_type=F32,
        )

    placed = lax.fori_loop(
        0, nsrc // LANES // TILES, scatter, jnp.zeros((2 * CELLS, COLS), F32)
    )
    loads[7].wait()
    work[...] = f_conc[...].reshape(CELLS, COLS) + (placed[:CELLS] + placed[CELLS:])
    fx_part = x_line.solve(x_fwd, column(work))
    x_send[0:8, :] = x_line.edges(fx_part)
    x_send[8:16, :] = jnp.where(x_line.last, x_fwd["from_last"][e], x_fwd["from_first"][0])
    x_send[16:24, :] = jnp.where(x_line.last, x_fwd["from_first"][e], x_fwd["from_last"][0])
    x_send[24:25, :] = jnp.maximum(f_vx[0:1, :], 0.0)
    x_send[25:26, :] = f_disp[0:1, :] * wet_f[0:1, :]
    x_send[26:27, :] = jnp.maximum(-f_vx[ROWS - 1 : ROWS, :], 0.0)
    x_send[27:28, :] = f_disp[ROWS - 1 : ROWS, :] * wet_f[ROWS - 1 : ROWS, :]
    x_send[28:32, :] = zero8[0:4]
    ends_a[0:8, :] = zero8
    ends_b[0:8, :] = zero8

    pl.semaphore_wait(barrier, len(greeted))
    to_line(y_send, y_recv, 0)
    to_x(x_send, x_recv, 1)

    def split_bf16(values):
        high = values.astype(BF16)
        return jnp.concatenate([high, (values - high.astype(F32)).astype(BF16)], axis=1)

    sub = lax.broadcasted_iota(jnp.int32, (8, LANES), 0)

    def folded(parts):
        for bit in (1, 2, 4):
            keep = (sub & bit) == 0
            parts = [
                jnp.where(keep, a, b) + pltpu.roll(jnp.where(keep, b, a), bit, 0)
                for a, b in zip(parts[0::2], parts[1::2])
            ]
        return parts[0]

    def pick(fields, send, at, unrolled):
        left = jnp.concatenate([split_bf16(field) for field in fields], axis=0)
        per_step = min(TILES, half_tiles)

        def go(step, _):
            base = pl.multiple_of(en * half_tiles + step * per_step, per_step)
            row_tile = rows_v[pl.ds(base, per_step), :]
            hot = onehot[:, lanes(base, per_step)]
            found = jnp.dot(left, jnp.concatenate([hot, hot], axis=0), preferred_element_type=F32)
            masks = [row_iota == row_tile[i : i + 1, :] for i in range(per_step)]
            for pair in range(per_step // 2):
                for k, first in enumerate(at):
                    parts = []
                    for t in range(TR):
                        for i in (2 * pair, 2 * pair + 1):
                            start = (k * TR + t) * ROWS
                            line = found[start : start + ROWS, i * LANES : (i + 1) * LANES]
                            line = jnp.where(masks[i], line, 0.0)
                            parts.append((line[0:8] + line[8:16]) + (line[16:24] + line[24:32]))
                    send[step * (per_step // 2) + pair, first : first + 8, :] = folded(parts)
            return 0

        if unrolled:
            for step in range(half_tiles // per_step):
                go(step, 0)
        else:
            lax.fori_loop(0, half_tiles // per_step, go, 0)

    pick((first_v[...], last_v[...]), z_send, (0, TR * tiles), False)
    to_each_x(z_send, z_recv, 2)

    def x_piece(ref, k):
        return jnp.concatenate([ref[d, 8 * k : 8 * k + 8, :] for d in range(nx)], axis=0)

    def single(ref, k, n):
        return jnp.concatenate([ref[d, k : k + 1, :] for d in range(n)], axis=0)

    def expanded(rows):
        return jnp.concatenate(
            [jnp.broadcast_to(rows[d : d + 1], (8, LANES)) for d in range(nx)], axis=0
        )

    def from_next(value):
        later = rolled(value, -8)
        return jnp.concatenate([rolled(later[8 * d : 8 * d + 8], 1) for d in range(nx)], axis=0)

    def own_x(ref, at):
        block = ref[pl.ds(pl.multiple_of(8 * at, 8), 8), :]
        return jnp.where(x_line.last, block, rolled(block, -1))

    arrived(x_recv, nx - 1, 1)
    index = lax.broadcasted_iota(jnp.int32, (nx, LANES), 0)
    x_before, x_after = (
        expanded(face) for face in faces(*[single(x_recv, 24 + k, nx) for k in range(4)], index, nx)
    )
    diagonal, corner = x_piece(x_recv, 1), x_piece(x_recv, 2)
    x_below = -corner * rolled(x_after, 8)
    x_center = 1.0 + diagonal * x_before + from_next(diagonal) * x_after
    block_index = lax.broadcasted_iota(jnp.int32, (8 * nx, LANES), 0) // 8
    x_above = jnp.where(
        block_index == nx - 1, 0.0, -from_next(corner) * rolled(x_before, -8)
    )
    terms = x_piece(x_recv, 0)
    jump = pcr_apply(pcr_factor(x_below, x_center, x_above, nx, 8), terms - from_next(terms))
    ends_a[8 : 8 + 8 * nx, :] = x_after * jump
    ends_b[8 : 8 + 8 * nx, :] = x_before * jump
    put(work, x_line.finish(x_fwd, fx_part, own_x(ends_a, gx), -own_x(ends_b, gx + 1)))
    work_t[...] = jnp.transpose(work[...])
    fy_part = y_line.solve(y_fwd, column(work_t))
    yb_send[0:1, :] = fy_part[0][0:1]
    yb_send[1:2, :] = fy_part[e][7:8]
    yb_send[2:8, :] = zero8[0:6]
    to_line(yb_send, yb_recv, 3)
    x_factors = pcr_factor(rolled(x_above, 8), x_center, rolled(x_below, -8), nx, 8)

    arrived(y_recv, ny - 1, 0)
    raw = single(y_recv, 6, ny)
    tracer_n = jnp.broadcast_to(tracer_row, (ny, LANES))
    quantities = []
    for k in range(4):
        value = jnp.where(tracer_n == k, raw, 0.0)
        value = value + pltpu.roll(value, ROWS, 1)
        quantities.append(value + pltpu.roll(value, 2 * ROWS, 1))
    index = lax.broadcasted_iota(jnp.int32, (ny, LANES), 0)
    y_before, y_after = faces(*quantities, index, ny)
    g00, gnn, g0n, gn0 = (single(y_recv, k, ny) for k in (2, 3, 4, 5))
    y_below = -gn0 * rolled(y_after, 1)
    y_center = 1.0 + gnn * y_before + rolled(g00, -1) * y_after
    y_above = jnp.where(index == ny - 1, 0.0, -rolled(g0n * y_before, -1))
    y_factors = pcr_factor(rolled(y_above, 1), y_center, rolled(y_below, -1), ny, 1)
    ends_a[8 : 8 + ny, :] = pcr_apply(
        y_factors, y_before * single(y_recv, 1, ny) - y_after * rolled(single(y_recv, 0, ny), -1)
    )
    head, tail = ends_a[pl.ds(7 + gy, 1), :], -ends_a[pl.ds(8 + gy, 1), :]
    put(work_t, y_line.finish(y_adj, y_part, head, tail))
    work[...] = jnp.transpose(work_t[...])
    ax_part = x_line.solve(x_adj, column(work))
    put(adjoint_v, ax_part)
    to_mate = pltpu.make_async_remote_copy(
        src_ref=adjoint_v, dst_ref=mate_v, send_sem=mate_ssem.at[0], recv_sem=mate_rsem.at[0],
        device_id=mate, device_id_type=MESH,
    )
    to_mate.start()
    xb_send[...] = x_line.edges(ax_part)
    to_x(xb_send, xb_recv, 4)

    to_mate.wait_recv()
    both = adjoint_v[...] + mate_v[...]
    work[...] = both
    both_edges = x_line.edges([strided(work, q) if q in (0, e) else None for q in range(Q)])
    for d in range(nx):
        p_send[d, 0:8, :] = both_edges
    pick((both,), p_send, (8,), True)
    to_each_x(p_send, p_recv, 5)

    y_fwd_factors = pcr_factor(y_below, y_center, y_above, ny, 1)
    arrived(z_recv, nx - 1, 2)

    def summed(ref, first, count, n):
        value = ref[0, first : first + count, :]
        for i in range(1, n):
            value = value + ref[i, first : first + count, :]
        return value

    width = TR * tiles
    z_first, z_last = summed(z_recv, 0, width, nx), summed(z_recv, width, width, nx)

    arrived(p_recv, nx - 1, 5)

    def flux_of(ref):
        terms = x_piece(ref, 0)
        return pcr_apply(x_factors, x_before * terms - x_after * from_next(terms))

    flux = flux_of(p_recv)
    mine = pl.multiple_of(en * half_tiles + gx * tiles, tiles)
    hot = onehot[:, lanes(mine, tiles)]
    found = jnp.dot(
        split_bf16(flux), jnp.concatenate([hot, hot], axis=0), preferred_element_type=F32
    )
    owner = owner_v[pl.ds(mine, tiles), :]
    for i in range(tiles):
        into, out = zero8, zero8
        for d in range(nx):
            value = found[8 * d : 8 * d + 8, i * LANES : (i + 1) * LANES]
            into = into + jnp.where(owner[i : i + 1, :] == d + 1, value, 0.0)
            out = out + jnp.where(owner[i : i + 1, :] == d, value, 0.0)
        for t in range(TR):
            spot = slice(tiles * t + i, tiles * t + i + 1)
            at = slice(2 * t + 1, 2 * t + 2)
            g_send[spot, :] = z_first[spot] * into[at] - z_last[spot] * out[at]
    g_send[...] = g_send[...] + summed(p_recv, 8, width, nx)
    to_line(g_send, g_recv, 6)

    arrived(xb_recv, nx - 1, 4)
    ends_a[8 : 8 + 8 * nx, :] = flux_of(xb_recv)
    put(
        adjoint_out,
        x_line.finish(x_adj, column(adjoint_v), own_x(ends_a, gx), -own_x(ends_a, gx + 1)),
    )

    arrived(yb_recv, ny - 1, 3)
    jump = pcr_apply(
        y_fwd_factors, single(yb_recv, 1, ny) - rolled(single(yb_recv, 0, ny), -1)
    )
    ends_a[8 : 8 + ny, :] = y_after * jump
    ends_b[8 : 8 + ny, :] = y_before * jump
    head, tail = ends_a[pl.ds(7 + gy, 1), :], -ends_b[pl.ds(8 + gy, 1), :]
    put(work_t, y_line.finish(y_fwd, fy_part, head, tail))
    state_out[...] = jnp.transpose(work_t[...])

    arrived(g_recv, ny - 1, 6)
    sums = summed(g_recv, 0, width, ny)
    for t in range(TR):
        for i in range(tiles):
            total[t : t + 1, i * LANES : (i + 1) * LANES] = sums[tiles * t + i : tiles * t + i + 1]

    here = grad_out.at[:, pl.ds(pl.multiple_of(en * half + gx * chunk, LANES), chunk)]
    peers = [peer(o) for o in plane_order(nx) for peer in (x_peer, mate_peer)] + [mate]
    for peer in peers:
        pltpu.make_async_remote_copy(
            src_ref=total, dst_ref=here, send_sem=ssem.at[7], recv_sem=rsem.at[7],
            device_id=peer, device_id_type=MESH,
        ).start()
    grad_out[:, pl.ds(pl.multiple_of(en * half + gx * chunk, LANES), chunk)] = total[...]

    sent(y_recv, ny - 1, 0)
    sent(x_recv, nx - 1, 1)
    sent(z_recv, nx - 1, 2)
    sent(yb_recv, ny - 1, 3)
    sent(xb_recv, nx - 1, 4)
    sent(p_recv, nx - 1, 5)
    sent(g_recv, ny - 1, 6)
    to_mate.wait_send()

    rest = grad_out.at[:, pl.ds(0, len(peers) * chunk)]
    pltpu.make_async_copy(rest, rest, ssem.at[7]).wait()
    pltpu.make_async_copy(rest, rest, rsem.at[7]).wait()


def store(state, adjoint, gradient, state_out, adjoint_out, grad_out, sem):
    moves = ((gradient, grad_out), (state, state_out), (adjoint, adjoint_out))
    copies = [pltpu.make_async_copy(m[0], m[1], sem.at[i]) for i, m in enumerate(moves)]
    for copy in copies:
        copy.start()
    for copy in copies:
        copy.wait()


def per_device(
    nx, ny, ne, concentration, cotangent, vel_x, vel_y, dispersion, wet_cells, decay_rate, emission,
    source_cell,
):
    nsrc = source_cell.shape[0]
    chunk = nsrc // (nx * ne)
    operands = [
        pltpu.with_memory_space_constraint(x, pltpu.HBM)
        for x in (
            decay_rate, concentration, cotangent, vel_x, vel_y, dispersion, wet_cells, emission,
            source_cell.reshape(nsrc // LANES, LANES),
        )
    ]
    width = TR * chunk // LANES
    square = pltpu.VMEM((CELLS, COLS), F32)
    block = pltpu.VMEM((ROWS, COLS), F32)

    def vmem(*shape, dtype=F32):
        return pltpu.VMEM(shape, dtype)

    index = vmem(nsrc // LANES, LANES, dtype=jnp.int32)
    ends = vmem(8 + 8 * max(nx, ny), LANES)
    scratch = [
        pltpu.SMEM((TR,), F32), block, block, block, vmem(ROWS, COLS, dtype=jnp.int32),
        vmem(TR, ROWS, COLS), vmem(TR, ROWS, COLS), vmem(TR, nsrc), index,
        square, square, square, square, square, square, square, square, square,
        vmem(COLS, nsrc, dtype=BF16), index, index, index,
        vmem(8, LANES), vmem(ny, 8, LANES), vmem(32, LANES), vmem(nx, 32, LANES),
        vmem(8, LANES), vmem(nx, 8, LANES), vmem(8, LANES), vmem(ny, 8, LANES), ends, ends,
        vmem(nx, 2 * width, LANES), vmem(nx, 2 * width, LANES),
        vmem(nx, 8 + width, LANES), vmem(nx, 8 + width, LANES),
        vmem(width, LANES), vmem(ny, width, LANES), vmem(TR, chunk),
        pltpu.SemaphoreType.DMA((9,)),
        pltpu.SemaphoreType.DMA((1,)), pltpu.SemaphoreType.DMA((1,)),
        pltpu.SemaphoreType.DMA((8,)), pltpu.SemaphoreType.DMA((8,)),
    ]
    hbm = pl.BlockSpec(memory_space=pl.ANY)
    on_chip = pl.BlockSpec(memory_space=pltpu.VMEM)
    state, adjoint, gradient = pl.pallas_call(
        functools.partial(kernel, nx, ny, ne, nsrc),
        out_shape=(
            jax.ShapeDtypeStruct((CELLS, COLS), F32),
            jax.ShapeDtypeStruct((CELLS, COLS), F32),
            jax.ShapeDtypeStruct(emission.shape, F32),
        ),
        in_specs=[hbm] * 9,
        out_specs=(on_chip, on_chip, on_chip),
        scratch_shapes=scratch,
        compiler_params=pltpu.CompilerParams(
            collective_id=0, has_side_effects=True, vmem_limit_bytes=VMEM_BYTES
        ),
        name="adi_step",
    )(*operands)
    shape = concentration.shape
    return pl.pallas_call(
        store,
        out_shape=(
            jax.ShapeDtypeStruct(shape, F32),
            jax.ShapeDtypeStruct(shape, F32),
            jax.ShapeDtypeStruct(emission.shape, F32),
        ),
        in_specs=[on_chip] * 3,
        out_specs=(hbm, hbm, hbm),
        scratch_shapes=[pltpu.SemaphoreType.DMA((3,))],
        compiler_params=pltpu.CompilerParams(vmem_limit_bytes=VMEM_BYTES),
        name="store",
    )(state.reshape(shape), adjoint.reshape(shape), gradient)


VMEM_BYTES = 32 * 1024 * 1024


def solution(mesh):
    nx, ny, ne = (mesh.shape[a] for a in ("gx", "gy", "ens"))
    field = P("ens", None, "gx", "gy")
    plane = P("gx", "gy")
    return jax.shard_map(
        functools.partial(per_device, nx, ny, ne),
        mesh=mesh,
        in_specs=(field, field, plane, plane, plane, plane, P(), P(), P()),
        out_specs=(field, field, P()),
        check_vma=False,
    )
```

```python
import functools

import jax
import jax.numpy as jnp
from jax import lax
from jax.experimental import pallas as pl
from jax.experimental.pallas import tpu as pltpu
from jax.sharding import PartitionSpec as P

MESH = pl.DeviceIdType.MESH
TR, ROWS, COLS, LANES, Q = 4, 32, 128, 128, 16
CELLS = TR * ROWS
F32, BF16 = jnp.float32, jnp.bfloat16
TILES = 8


def rolled(x, shift):
    n = x.shape[0]
    shift = shift % n
    if shift == 0:
        return x
    if shift % 8 == 0:
        return jnp.concatenate([x[n - shift :], x[: n - shift]], axis=0)
    return pltpu.roll(x, shift, 0)


def wrapped(i, n):
    return i & (n - 1) if n & (n - 1) == 0 else lax.rem(i, n)


def farthest_first(n):
    return sorted(range(1, n), key=lambda o: (-min(o, n - o), o))


def plane_order(n):
    far = (0, 1, 2, 1)
    return sorted(range(1, n), key=lambda o: -(far[o % 4] + far[o // 4 % 4]))


def pcr_factor(below, center, above, count, unit):
    steps, stride = [], 1
    while stride < count:
        k = stride * unit
        inverse = 1.0 / center
        alpha = -below * rolled(inverse, k)
        gamma = -above * rolled(inverse, -k)
        center = center + alpha * rolled(above, k) + gamma * rolled(below, -k)
        below, above = alpha * rolled(below, k), gamma * rolled(above, -k)
        steps.append((k, alpha, gamma))
        stride *= 2
    return steps, 1.0 / center


def pcr_apply(factors, side):
    steps, inverse = factors
    for k, alpha, gamma in steps:
        side = side + alpha * rolled(side, k) + gamma * rolled(side, -k)
    return side * inverse


class Line:
    def __init__(self, size):
        self.size = size
        sub = lax.broadcasted_iota(jnp.int32, (8, LANES), 0) % size
        self.first = sub == 0
        self.last = sub == size - 1

    def extended(self, cells):
        head = jnp.where(self.first, 0.0, rolled(cells[-1], 1))
        tail = jnp.where(self.last, 0.0, rolled(cells[0], -1))
        return [head] + cells + [tail]

    def bands(self, vel, disp, wet, half_decay):
        vel, disp, wet = (self.extended(cells) for cells in (vel, disp, wet))
        gate = [wet[k] * wet[k + 1] for k in range(Q + 1)]
        flux = [0.5 * (disp[k] + disp[k + 1]) * gate[k] for k in range(Q + 1)]
        plus = [jnp.maximum(v, 0.0) for v in vel]
        minus = [jnp.maximum(-v, 0.0) for v in vel]
        fwd_below = [-(flux[q] + plus[q + 1] * gate[q]) for q in range(Q)]
        fwd_above = [-(flux[q + 1] + minus[q + 1] * gate[q + 1]) for q in range(Q)]
        adj_below = [-(flux[q] + minus[q] * gate[q]) for q in range(Q)]
        adj_above = [-(flux[q + 1] + plus[q + 2] * gate[q + 1]) for q in range(Q)]
        center = [
            (1.0 + flux[q] + flux[q + 1] + plus[q + 1] * gate[q] + minus[q + 1] * gate[q + 1])
            + half_decay
            for q in range(Q)
        ]
        inverse = [1.0 / center[0]]
        for q in range(1, Q - 1):
            pivot = center[q] - fwd_below[q] * fwd_above[q - 1] * inverse[q - 1]
            inverse.append(1.0 / pivot)
        forward = self.factor(fwd_below, center, fwd_above, inverse)
        adjoint = self.factor(adj_below, center, adj_above, inverse)
        return forward, adjoint

    def factor(self, below, center, above, inverse):
        e = Q - 1
        fa = dict(inverse=inverse, below_end=below[e], above_end=above[e])
        fa["mult"] = mult = [None] + [below[q] * inverse[q - 1] for q in range(1, e)]
        fa["up"] = up = [above[q] * inverse[q] for q in range(e)]
        start = [-below[0]]
        for q in range(1, e):
            start.append(-mult[q] * start[q - 1])
        v, w = [None] * e, [None] * e
        v[e - 1] = start[e - 1] * inverse[e - 1]
        w[e - 1] = -up[e - 1]
        for q in range(e - 2, -1, -1):
            v[q] = start[q] * inverse[q] - up[q] * v[q + 1]
            w[q] = -up[q] * w[q + 1]
        fa["v"], fa["w"] = v, w
        fa["reduced"] = pcr_factor(
            below[e] * v[e - 1],
            center[e] + below[e] * w[e - 1] + above[e] * rolled(v[0], -1),
            above[e] * rolled(w[0], -1),
            self.size,
            1,
        )
        head = jnp.where(self.first, 1.0, 0.0)
        fa["from_first"] = self.solve(fa, [head] + [None] * e)
        fa["from_last"] = self.solve(fa, [None] * e + [jnp.where(self.last, 1.0, 0.0)])
        return fa

    def solve(self, fa, field):
        def plus(a, b):
            return b if a is None else a if b is None else a + b

        def times(a, b):
            return None if b is None else a * b

        e = Q - 1
        g = [field[0]]
        for q in range(1, e):
            g.append(plus(field[q], times(-fa["mult"][q], g[q - 1])))
        part = [None] * e
        part[e - 1] = times(fa["inverse"][e - 1], g[e - 1])
        for q in range(e - 2, -1, -1):
            part[q] = plus(times(fa["inverse"][q], g[q]), times(-fa["up"][q], part[q + 1]))
        side = plus(field[e], times(-fa["below_end"], part[e - 1]))
        if part[0] is not None:
            side = side - fa["above_end"] * rolled(part[0], -1)
        ends = pcr_apply(fa["reduced"], side)
        before = rolled(ends, 1)
        return [
            plus(part[q], fa["v"][q] * before + fa["w"][q] * ends) for q in range(e)
        ] + [ends]

    def finish(self, fa, part, head, tail):
        first, last = fa["from_first"], fa["from_last"]
        return [part[q] + first[q] * head + last[q] * tail for q in range(Q)]

    def edges(self, cells):
        return jnp.where(self.last, cells[Q - 1], cells[0])


def faces(plus_first, disp_first, minus_last, disp_last, index, count):
    disp_next = rolled(disp_first, -1)
    shut = (index == count - 1) | (disp_last <= 0.0) | (disp_next <= 0.0)
    flux = 0.5 * (disp_last + disp_next)
    return (
        jnp.where(shut, 0.0, flux + minus_last),
        jnp.where(shut, 0.0, flux + rolled(plus_first, -1)),
    )


def kernel(
    nx, ny, ne, nsrc,
    decay_in, conc, cot, vel_x, vel_y, disp, wet_cells, emission, cells,
    state_out, adjoint_out, grad_out,
    decay, f_vx, f_vy, f_disp, f_wet, f_conc, f_cot, f_emis, f_cells,
    vel_t, disp_t, wet_t, work, work_t, adjoint_v, mate_v, first_v, last_v,
    onehot, rows_v, cols_v, owner_v,
    y_send, y_recv, x_send, x_recv, xb_send, xb_recv, yb_send, yb_recv, ends_a, ends_b,
    z_send, z_recv, p_send, p_recv, g_send, g_recv, total,
    in_sem, mate_ssem, mate_rsem, ssem, rsem,
):
    gx, gy, en = lax.axis_index("gx"), lax.axis_index("gy"), lax.axis_index("ens")
    half = nsrc // ne
    chunk = half // nx
    tiles = chunk // LANES
    half_tiles = half // LANES
    mate = (gx, gy, wrapped(en + 1, ne))
    assert tiles == 2

    loads = [
        pltpu.make_async_copy(src, dst, in_sem.at[i])
        for i, (src, dst) in enumerate(
            [
                (vel_y, f_vy), (disp, f_disp), (wet_cells, f_wet), (cot.at[0], f_cot),
                (vel_x, f_vx), (cells, f_cells), (emission, f_emis), (conc.at[0], f_conc),
                (decay_in, decay),
            ]
        )
    ]

    def line_peer(o):
        return (gx, wrapped(gy + o, ny), en)

    def x_peer(o):
        return (gx ^ o, gy, en)

    def mate_peer(o):
        return (gx ^ o, gy, mate[2])

    barrier = pltpu.get_barrier_semaphore()
    greeted = [line_peer(o) for o in farthest_first(ny)]
    greeted += [peer(o) for o in plane_order(nx) for peer in (x_peer, mate_peer)] + [mate]
    for load in loads[:5]:
        load.start()
    for peer in greeted:
        pl.semaphore_signal(barrier, inc=1, device_id=peer, device_id_type=MESH)
    for load in loads[5:]:
        load.start()

    def to_line(send, recv, slot):
        for o in farthest_first(ny):
            pltpu.make_async_remote_copy(
                src_ref=send, dst_ref=recv.at[gy], send_sem=ssem.at[slot],
                recv_sem=rsem.at[slot], device_id=line_peer(o), device_id_type=MESH,
            ).start()
        recv[gy] = send[...]

    def to_x(send, recv, slot):
        for o in plane_order(nx):
            pltpu.make_async_remote_copy(
                src_ref=send, dst_ref=recv.at[gx], send_sem=ssem.at[slot],
                recv_sem=rsem.at[slot], device_id=x_peer(o), device_id_type=MESH,
            ).start()
        recv[gx] = send[...]

    def to_each_x(send, recv, slot):
        for o in plane_order(nx):
            peer = gx ^ o
            pltpu.make_async_remote_copy(
                src_ref=send.at[peer], dst_ref=recv.at[gx], send_sem=ssem.at[slot],
                recv_sem=rsem.at[slot], device_id=x_peer(o), device_id_type=MESH,
            ).start()
        recv[gx] = send[gx]

    def arrived(recv, count, slot):
        part = recv.at[pl.ds(0, count)]
        pltpu.make_async_copy(part, part, rsem.at[slot]).wait()

    def sent(recv, count, slot):
        part = recv.at[pl.ds(0, count)]
        pltpu.make_async_copy(part, part, ssem.at[slot]).wait()

    def strided(ref, q):
        return ref[pl.ds(q, 8, stride=Q), :]

    def column(ref):
        return [strided(ref, q) for q in range(Q)]

    def put(ref, cells_):
        for q in range(Q):
            ref[pl.ds(q, 8, stride=Q), :] = cells_[q]

    y_line, x_line = Line(8), Line(2)
    zero8 = jnp.zeros((8, LANES), F32)
    lane_tracer = lax.broadcasted_iota(jnp.int32, (8, LANES), 1) // ROWS
    sub_tracer = lax.broadcasted_iota(jnp.int32, (8, LANES), 0) // 2

    def half_decay(tracer):
        value = jnp.full((8, LANES), decay[TR - 1], F32)
        for t in range(TR - 1):
            value = jnp.where(tracer == t, decay[t], value)
        return 0.5 * value

    for i in (8, 0, 1, 2, 3):
        loads[i].wait()
    wet_f = f_wet[...].astype(F32)
    for field, ref in ((f_vy[...], vel_t), (f_disp[...], disp_t), (wet_f, wet_t)):
        ref[...] = jnp.transpose(jnp.concatenate([field] * TR, axis=0))
    work_t[...] = jnp.transpose(f_cot[...].reshape(CELLS, COLS))
    y_fwd, y_adj = y_line.bands(
        column(vel_t), column(disp_t), column(wet_t), half_decay(lane_tracer)
    )
    y_part = y_line.solve(y_adj, column(work_t))
    end = COLS - 1
    tracer_row = lane_tracer[0:1]
    packed = jnp.where(
        tracer_row == 0,
        jnp.maximum(vel_t[0:1, :], 0.0),
        jnp.where(
            tracer_row == 1,
            disp_t[0:1, :] * wet_t[0:1, :],
            jnp.where(
                tracer_row == 2,
                jnp.maximum(-vel_t[end : end + 1, :], 0.0),
                disp_t[end : end + 1, :] * wet_t[end : end + 1, :],
            ),
        ),
    )
    e = Q - 1
    for i, row in enumerate(
        (
            y_part[0][0:1], y_part[e][7:8], y_fwd["from_first"][0][0:1],
            y_fwd["from_last"][e][7:8], y_fwd["from_last"][0][0:1],
            y_fwd["from_first"][e][7:8], packed, zero8[0:1],
        )
    ):
        y_send[i : i + 1, :] = row

    loads[4].wait()

    def spread(ref, as_float):
        out = []
        for q in range(Q):
            value = jnp.where(x_line.first, ref[q : q + 1, :], ref[q + Q : q + Q + 1, :])
            out.append(value.astype(F32) if as_float else value)
        return out

    x_fwd, x_adj = x_line.bands(
        spread(f_vx, False), spread(f_disp, False), spread(f_wet, True), half_decay(sub_tracer)
    )
    put(first_v, x_adj["from_first"])
    put(last_v, x_adj["from_last"])

    loads[5].wait()
    shift = (ny * COLS).bit_length() - 1
    source = f_cells[...]
    row = lax.shift_right_logical(source, shift)
    owner_v[...] = lax.shift_right_logical(row, ROWS.bit_length() - 1)
    rows_v[...] = row - gx * ROWS
    cols_v[...] = (source & (ny * COLS - 1)) - gy * COLS
    row_iota = lax.broadcasted_iota(jnp.int32, (ROWS, LANES), 0)
    col_iota = lax.broadcasted_iota(jnp.int32, (COLS, LANES), 0)

    def lanes(tile, count):
        return pl.ds(pl.multiple_of(tile * LANES, LANES), count * LANES)

    loads[6].wait()

    def scatter(step, acc):
        base = pl.multiple_of(step * TILES, TILES)
        row_tile = rows_v[pl.ds(base, TILES), :]
        col_tile = cols_v[pl.ds(base, TILES), :]
        values = f_emis[:, lanes(base, TILES)]
        high = values.astype(BF16).astype(F32)
        low = values - high
        left, hots = [], []
        for i in range(TILES):
            mask = row_iota == row_tile[i : i + 1, :]
            part = slice(i * LANES, (i + 1) * LANES)
            left.append(
                jnp.concatenate(
                    [
                        jnp.where(mask, piece[t : t + 1, part], 0.0).astype(BF16)
                        for piece in (high, low)
                        for t in range(TR)
                    ],
                    axis=0,
                )
            )
            hots.append(jnp.where(col_iota == col_tile[i : i + 1, :], 1.0, 0.0).astype(BF16))
        hot = jnp.concatenate(hots, axis=1)
        onehot[:, lanes(base, TILES)] = hot
        return acc + lax.dot_general(
            jnp.concatenate(left, axis=1),
            hot,
            (((1,), (1,)), ((), ())),
            preferred_element_type=F32,
        )

    placed = lax.fori_loop(
        0, nsrc // LANES // TILES, scatter, jnp.zeros((2 * CELLS, COLS), F32)
    )
    loads[7].wait()
    work[...] = f_conc[...].reshape(CELLS, COLS) + (placed[:CELLS] + placed[CELLS:])
    fx_part = x_line.solve(x_fwd, column(work))
    x_send[0:8, :] = x_line.edges(fx_part)
    x_send[8:16, :] = jnp.where(x_line.last, x_fwd["from_last"][e], x_fwd["from_first"][0])
    x_send[16:24, :] = jnp.where(x_line.last, x_fwd["from_first"][e], x_fwd["from_last"][0])
    x_send[24:25, :] = jnp.maximum(f_vx[0:1, :], 0.0)
    x_send[25:26, :] = f_disp[0:1, :] * wet_f[0:1, :]
    x_send[26:27, :] = jnp.maximum(-f_vx[ROWS - 1 : ROWS, :], 0.0)
    x_send[27:28, :] = f_disp[ROWS - 1 : ROWS, :] * wet_f[ROWS - 1 : ROWS, :]
    x_send[28:32, :] = zero8[0:4]
    ends_a[0:8, :] = zero8
    ends_b[0:8, :] = zero8

    pl.semaphore_wait(barrier, len(greeted))
    to_line(y_send, y_recv, 0)
    to_x(x_send, x_recv, 1)

    def split_bf16(values):
        high = values.astype(BF16)
        return jnp.concatenate([high, (values - high.astype(F32)).astype(BF16)], axis=1)

    sub = lax.broadcasted_iota(jnp.int32, (8, LANES), 0)

    def folded(parts):
        for bit in (1, 2, 4):
            keep = (sub & bit) == 0
            parts = [
                jnp.where(keep, a, b) + pltpu.roll(jnp.where(keep, b, a), bit, 0)
                for a, b in zip(parts[0::2], parts[1::2])
            ]
        return parts[0]

    def pick(fields, send, at, unrolled):
        left = jnp.concatenate([split_bf16(field) for field in fields], axis=0)
        per_step = min(TILES, half_tiles)

        def go(step, _):
            base = pl.multiple_of(en * half_tiles + step * per_step, per_step)
            row_tile = rows_v[pl.ds(base, per_step), :]
            hot = onehot[:, lanes(base, per_step)]
            found = jnp.dot(left, jnp.concatenate([hot, hot], axis=0), preferred_element_type=F32)
            masks = [row_iota == row_tile[i : i + 1, :] for i in range(per_step)]
            for pair in range(per_step // 2):
                for k, first in enumerate(at):
                    parts = []
                    for t in range(TR):
                        for i in (2 * pair, 2 * pair + 1):
                            start = (k * TR + t) * ROWS
                            line = found[start : start + ROWS, i * LANES : (i + 1) * LANES]
                            line = jnp.where(masks[i], line, 0.0)
                            parts.append((line[0:8] + line[8:16]) + (line[16:24] + line[24:32]))
                    send[step * (per_step // 2) + pair, first : first + 8, :] = folded(parts)
            return 0

        if unrolled:
            for step in range(half_tiles // per_step):
                go(step, 0)
        else:
            lax.fori_loop(0, half_tiles // per_step, go, 0)

    pick((first_v[...], last_v[...]), z_send, (0, TR * tiles), False)
    to_each_x(z_send, z_recv, 2)

    def x_piece(ref, k):
        return jnp.concatenate([ref[d, 8 * k : 8 * k + 8, :] for d in range(nx)], axis=0)

    def single(ref, k, n):
        return jnp.concatenate([ref[d, k : k + 1, :] for d in range(n)], axis=0)

    def expanded(rows):
        return jnp.concatenate(
            [jnp.broadcast_to(rows[d : d + 1], (8, LANES)) for d in range(nx)], axis=0
        )

    def from_next(value):
        later = rolled(value, -8)
        return jnp.concatenate([rolled(later[8 * d : 8 * d + 8], 1) for d in range(nx)], axis=0)

    def own_x(ref, at):
        block = ref[pl.ds(pl.multiple_of(8 * at, 8), 8), :]
        return jnp.where(x_line.last, block, rolled(block, -1))

    arrived(y_recv, ny - 1, 0)
    raw = single(y_recv, 6, ny)
    tracer_n = jnp.broadcast_to(tracer_row, (ny, LANES))
    quantities = []
    for k in range(4):
        value = jnp.where(tracer_n == k, raw, 0.0)
        value = value + pltpu.roll(value, ROWS, 1)
        quantities.append(value + pltpu.roll(value, 2 * ROWS, 1))
    index = lax.broadcasted_iota(jnp.int32, (ny, LANES), 0)
    y_before, y_after = faces(*quantities, index, ny)
    g00, gnn, g0n, gn0 = (single(y_recv, k, ny) for k in (2, 3, 4, 5))
    y_below = -gn0 * rolled(y_after, 1)
    y_center = 1.0 + gnn * y_before + rolled(g00, -1) * y_after
    y_above = jnp.where(index == ny - 1, 0.0, -rolled(g0n * y_before, -1))
    y_factors = pcr_factor(rolled(y_above, 1), y_center, rolled(y_below, -1), ny, 1)
    ends_a[8 : 8 + ny, :] = pcr_apply(
        y_factors, y_before * single(y_recv, 1, ny) - y_after * rolled(single(y_recv, 0, ny), -1)
    )
    head, tail = ends_a[pl.ds(7 + gy, 1), :], -ends_a[pl.ds(8 + gy, 1), :]
    put(work_t, y_line.finish(y_adj, y_part, head, tail))
    work[...] = jnp.transpose(work_t[...])
    ax_part = x_line.solve(x_adj, column(work))
    put(adjoint_v, ax_part)
    to_mate = pltpu.make_async_remote_copy(
        src_ref=adjoint_v, dst_ref=mate_v, send_sem=mate_ssem.at[0], recv_sem=mate_rsem.at[0],
        device_id=mate, device_id_type=MESH,
    )
    to_mate.start()
    xb_send[...] = x_line.edges(ax_part)

    to_mate.wait_recv()
    both = adjoint_v[...] + mate_v[...]
    work[...] = both
    both_edges = x_line.edges([strided(work, q) if q in (0, e) else None for q in range(Q)])
    for d in range(nx):
        p_send[d, 0:8, :] = both_edges
    pick((both,), p_send, (8,), True)
    to_each_x(p_send, p_recv, 5)
    to_x(xb_send, xb_recv, 4)

    arrived(x_recv, nx - 1, 1)
    index = lax.broadcasted_iota(jnp.int32, (nx, LANES), 0)
    x_before, x_after = (
        expanded(face) for face in faces(*[single(x_recv, 24 + k, nx) for k in range(4)], index, nx)
    )
    diagonal, corner = x_piece(x_recv, 1), x_piece(x_recv, 2)
    x_below = -corner * rolled(x_after, 8)
    x_center = 1.0 + diagonal * x_before + from_next(diagonal) * x_after
    block_index = lax.broadcasted_iota(jnp.int32, (8 * nx, LANES), 0) // 8
    x_above = jnp.where(
        block_index == nx - 1, 0.0, -from_next(corner) * rolled(x_before, -8)
    )
    terms = x_piece(x_recv, 0)
    jump = pcr_apply(pcr_factor(x_below, x_center, x_above, nx, 8), terms - from_next(terms))
    ends_a[8 : 8 + 8 * nx, :] = x_after * jump
    ends_b[8 : 8 + 8 * nx, :] = x_before * jump
    put(work, x_line.finish(x_fwd, fx_part, own_x(ends_a, gx), -own_x(ends_b, gx + 1)))
    work_t[...] = jnp.transpose(work[...])
    fy_part = y_line.solve(y_fwd, column(work_t))
    yb_send[0:1, :] = fy_part[0][0:1]
    yb_send[1:2, :] = fy_part[e][7:8]
    yb_send[2:8, :] = zero8[0:6]
    to_line(yb_send, yb_recv, 3)
    x_factors = pcr_factor(rolled(x_above, 8), x_center, rolled(x_below, -8), nx, 8)

    y_fwd_factors = pcr_factor(y_below, y_center, y_above, ny, 1)
    arrived(z_recv, nx - 1, 2)

    def summed(ref, first, count, n):
        value = ref[0, first : first + count, :]
        for i in range(1, n):
            value = value + ref[i, first : first + count, :]
        return value

    width = TR * tiles
    z_first, z_last = summed(z_recv, 0, width, nx), summed(z_recv, width, width, nx)

    arrived(p_recv, nx - 1, 5)

    def flux_of(ref):
        terms = x_piece(ref, 0)
        return pcr_apply(x_factors, x_before * terms - x_after * from_next(terms))

    flux = flux_of(p_recv)
    mine = pl.multiple_of(en * half_tiles + gx * tiles, tiles)
    hot = onehot[:, lanes(mine, tiles)]
    found = jnp.dot(
        split_bf16(flux), jnp.concatenate([hot, hot], axis=0), preferred_element_type=F32
    )
    owner = owner_v[pl.ds(mine, tiles), :]
    for i in range(tiles):
        into, out = zero8, zero8
        for d in range(nx):
            value = found[8 * d : 8 * d + 8, i * LANES : (i + 1) * LANES]
            into = into + jnp.where(owner[i : i + 1, :] == d + 1, value, 0.0)
            out = out + jnp.where(owner[i : i + 1, :] == d, value, 0.0)
        for t in range(TR):
            spot = slice(tiles * t + i, tiles * t + i + 1)
            at = slice(2 * t + 1, 2 * t + 2)
            g_send[spot, :] = z_first[spot] * into[at] - z_last[spot] * out[at]
    g_send[...] = g_send[...] + summed(p_recv, 8, width, nx)
    to_line(g_send, g_recv, 6)

    arrived(xb_recv, nx - 1, 4)
    ends_a[8 : 8 + 8 * nx, :] = flux_of(xb_recv)
    put(
        adjoint_out,
        x_line.finish(x_adj, column(adjoint_v), own_x(ends_a, gx), -own_x(ends_a, gx + 1)),
    )

    arrived(yb_recv, ny - 1, 3)
    jump = pcr_apply(
        y_fwd_factors, single(yb_recv, 1, ny) - rolled(single(yb_recv, 0, ny), -1)
    )
    ends_a[8 : 8 + ny, :] = y_after * jump
    ends_b[8 : 8 + ny, :] = y_before * jump
    head, tail = ends_a[pl.ds(7 + gy, 1), :], -ends_b[pl.ds(8 + gy, 1), :]
    put(work_t, y_line.finish(y_fwd, fy_part, head, tail))
    state_out[...] = jnp.transpose(work_t[...])

    arrived(g_recv, ny - 1, 6)
    sums = summed(g_recv, 0, width, ny)
    for t in range(TR):
        for i in range(tiles):
            total[t : t + 1, i * LANES : (i + 1) * LANES] = sums[tiles * t + i : tiles * t + i + 1]

    here = grad_out.at[:, pl.ds(pl.multiple_of(en * half + gx * chunk, LANES), chunk)]
    peers = [peer(o) for o in plane_order(nx) for peer in (x_peer, mate_peer)] + [mate]
    for peer in peers:
        pltpu.make_async_remote_copy(
            src_ref=total, dst_ref=here, send_sem=ssem.at[7], recv_sem=rsem.at[7],
            device_id=peer, device_id_type=MESH,
        ).start()
    grad_out[:, pl.ds(pl.multiple_of(en * half + gx * chunk, LANES), chunk)] = total[...]

    sent(y_recv, ny - 1, 0)
    sent(x_recv, nx - 1, 1)
    sent(z_recv, nx - 1, 2)
    sent(yb_recv, ny - 1, 3)
    sent(xb_recv, nx - 1, 4)
    sent(p_recv, nx - 1, 5)
    sent(g_recv, ny - 1, 6)
    to_mate.wait_send()

    rest = grad_out.at[:, pl.ds(0, len(peers) * chunk)]
    pltpu.make_async_copy(rest, rest, ssem.at[7]).wait()
    pltpu.make_async_copy(rest, rest, rsem.at[7]).wait()


def store(state, adjoint, gradient, state_out, adjoint_out, grad_out, sem):
    moves = ((gradient, grad_out), (state, state_out), (adjoint, adjoint_out))
    copies = [pltpu.make_async_copy(m[0], m[1], sem.at[i]) for i, m in enumerate(moves)]
    for copy in copies:
        copy.start()
    for copy in copies:
        copy.wait()


def per_device(
    nx, ny, ne, concentration, cotangent, vel_x, vel_y, dispersion, wet_cells, decay_rate, emission,
    source_cell,
):
    nsrc = source_cell.shape[0]
    chunk = nsrc // (nx * ne)
    operands = [
        pltpu.with_memory_space_constraint(x, pltpu.HBM)
        for x in (
            decay_rate, concentration, cotangent, vel_x, vel_y, dispersion, wet_cells, emission,
            source_cell.reshape(nsrc // LANES, LANES),
        )
    ]
    width = TR * chunk // LANES
    square = pltpu.VMEM((CELLS, COLS), F32)
    block = pltpu.VMEM((ROWS, COLS), F32)

    def vmem(*shape, dtype=F32):
        return pltpu.VMEM(shape, dtype)

    index = vmem(nsrc // LANES, LANES, dtype=jnp.int32)
    ends = vmem(8 + 8 * max(nx, ny), LANES)
    scratch = [
        pltpu.SMEM((TR,), F32), block, block, block, vmem(ROWS, COLS, dtype=jnp.int32),
        vmem(TR, ROWS, COLS), vmem(TR, ROWS, COLS), vmem(TR, nsrc), index,
        square, square, square, square, square, square, square, square, square,
        vmem(COLS, nsrc, dtype=BF16), index, index, index,
        vmem(8, LANES), vmem(ny, 8, LANES), vmem(32, LANES), vmem(nx, 32, LANES),
        vmem(8, LANES), vmem(nx, 8, LANES), vmem(8, LANES), vmem(ny, 8, LANES), ends, ends,
        vmem(nx, 2 * width, LANES), vmem(nx, 2 * width, LANES),
        vmem(nx, 8 + width, LANES), vmem(nx, 8 + width, LANES),
        vmem(width, LANES), vmem(ny, width, LANES), vmem(TR, chunk),
        pltpu.SemaphoreType.DMA((9,)),
        pltpu.SemaphoreType.DMA((1,)), pltpu.SemaphoreType.DMA((1,)),
        pltpu.SemaphoreType.DMA((8,)), pltpu.SemaphoreType.DMA((8,)),
    ]
    hbm = pl.BlockSpec(memory_space=pl.ANY)
    on_chip = pl.BlockSpec(memory_space=pltpu.VMEM)
    state, adjoint, gradient = pl.pallas_call(
        functools.partial(kernel, nx, ny, ne, nsrc),
        out_shape=(
            jax.ShapeDtypeStruct((CELLS, COLS), F32),
            jax.ShapeDtypeStruct((CELLS, COLS), F32),
            jax.ShapeDtypeStruct(emission.shape, F32),
        ),
        in_specs=[hbm] * 9,
        out_specs=(on_chip, on_chip, on_chip),
        scratch_shapes=scratch,
        compiler_params=pltpu.CompilerParams(
            collective_id=0, has_side_effects=True, vmem_limit_bytes=VMEM_BYTES
        ),
        name="adi_step",
    )(*operands)
    shape = concentration.shape
    return pl.pallas_call(
        store,
        out_shape=(
            jax.ShapeDtypeStruct(shape, F32),
            jax.ShapeDtypeStruct(shape, F32),
            jax.ShapeDtypeStruct(emission.shape, F32),
        ),
        in_specs=[on_chip] * 3,
        out_specs=(hbm, hbm, hbm),
        scratch_shapes=[pltpu.SemaphoreType.DMA((3,))],
        compiler_params=pltpu.CompilerParams(vmem_limit_bytes=VMEM_BYTES),
        name="store",
    )(state.reshape(shape), adjoint.reshape(shape), gradient)


VMEM_BYTES = 32 * 1024 * 1024


def solution(mesh):
    nx, ny, ne = (mesh.shape[a] for a in ("gx", "gy", "ens"))
    field = P("ens", None, "gx", "gy")
    plane = P("gx", "gy")
    return jax.shard_map(
        functools.partial(per_device, nx, ny, ne),
        mesh=mesh,
        in_specs=(field, field, plane, plane, plane, plane, P(), P(), P()),
        out_specs=(field, field, P()),
        check_vma=False,
    )
```

```python
import functools

import jax
import jax.numpy as jnp
from jax import lax
from jax.experimental import pallas as pl
from jax.experimental.pallas import tpu as pltpu
from jax.sharding import PartitionSpec as P

MESH = pl.DeviceIdType.MESH
TR, ROWS, COLS, LANES, Q = 4, 32, 128, 128, 16
CELLS = TR * ROWS
F32, BF16 = jnp.float32, jnp.bfloat16
TILES = 8


def rolled(x, shift):
    n = x.shape[0]
    shift = shift % n
    if shift == 0:
        return x
    if shift % 8 == 0:
        return jnp.concatenate([x[n - shift :], x[: n - shift]], axis=0)
    return pltpu.roll(x, shift, 0)


def wrapped(i, n):
    return i & (n - 1) if n & (n - 1) == 0 else lax.rem(i, n)


def farthest_first(n):
    return sorted(range(1, n), key=lambda o: (-min(o, n - o), o))


def plane_order(n):
    far = (0, 1, 2, 1)
    return sorted(range(1, n), key=lambda o: -(far[o % 4] + far[o // 4 % 4]))


def pcr_factor(below, center, above, count, unit):
    steps, stride = [], 1
    while stride < count:
        k = stride * unit
        inverse = 1.0 / center
        alpha = -below * rolled(inverse, k)
        gamma = -above * rolled(inverse, -k)
        center = center + alpha * rolled(above, k) + gamma * rolled(below, -k)
        below, above = alpha * rolled(below, k), gamma * rolled(above, -k)
        steps.append((k, alpha, gamma))
        stride *= 2
    return steps, 1.0 / center


def pcr_apply(factors, side):
    steps, inverse = factors
    for k, alpha, gamma in steps:
        side = side + alpha * rolled(side, k) + gamma * rolled(side, -k)
    return side * inverse


class Line:
    def __init__(self, size):
        self.size = size
        sub = lax.broadcasted_iota(jnp.int32, (8, LANES), 0) % size
        self.first = sub == 0
        self.last = sub == size - 1

    def extended(self, cells):
        head = jnp.where(self.first, 0.0, rolled(cells[-1], 1))
        tail = jnp.where(self.last, 0.0, rolled(cells[0], -1))
        return [head] + cells + [tail]

    def bands(self, vel, disp, wet, half_decay):
        vel, disp, wet = (self.extended(cells) for cells in (vel, disp, wet))
        gate = [wet[k] * wet[k + 1] for k in range(Q + 1)]
        flux = [0.5 * (disp[k] + disp[k + 1]) * gate[k] for k in range(Q + 1)]
        plus = [jnp.maximum(v, 0.0) for v in vel]
        minus = [jnp.maximum(-v, 0.0) for v in vel]
        fwd_below = [-(flux[q] + plus[q + 1] * gate[q]) for q in range(Q)]
        fwd_above = [-(flux[q + 1] + minus[q + 1] * gate[q + 1]) for q in range(Q)]
        adj_below = [-(flux[q] + minus[q] * gate[q]) for q in range(Q)]
        adj_above = [-(flux[q + 1] + plus[q + 2] * gate[q + 1]) for q in range(Q)]
        center = [
            (1.0 + flux[q] + flux[q + 1] + plus[q + 1] * gate[q] + minus[q + 1] * gate[q + 1])
            + half_decay
            for q in range(Q)
        ]
        inverse = [1.0 / center[0]]
        for q in range(1, Q - 1):
            pivot = center[q] - fwd_below[q] * fwd_above[q - 1] * inverse[q - 1]
            inverse.append(1.0 / pivot)
        forward = self.factor(fwd_below, center, fwd_above, inverse)
        adjoint = self.factor(adj_below, center, adj_above, inverse)
        return forward, adjoint

    def factor(self, below, center, above, inverse):
        e = Q - 1
        fa = dict(inverse=inverse, below_end=below[e], above_end=above[e])
        fa["mult"] = mult = [None] + [below[q] * inverse[q - 1] for q in range(1, e)]
        fa["up"] = up = [above[q] * inverse[q] for q in range(e)]
        start = [-below[0]]
        for q in range(1, e):
            start.append(-mult[q] * start[q - 1])
        v, w = [None] * e, [None] * e
        v[e - 1] = start[e - 1] * inverse[e - 1]
        w[e - 1] = -up[e - 1]
        for q in range(e - 2, -1, -1):
            v[q] = start[q] * inverse[q] - up[q] * v[q + 1]
            w[q] = -up[q] * w[q + 1]
        fa["v"], fa["w"] = v, w
        fa["reduced"] = pcr_factor(
            below[e] * v[e - 1],
            center[e] + below[e] * w[e - 1] + above[e] * rolled(v[0], -1),
            above[e] * rolled(w[0], -1),
            self.size,
            1,
        )
        head = jnp.where(self.first, 1.0, 0.0)
        fa["from_first"] = self.solve(fa, [head] + [None] * e)
        fa["from_last"] = self.solve(fa, [None] * e + [jnp.where(self.last, 1.0, 0.0)])
        return fa

    def solve(self, fa, field):
        def plus(a, b):
            return b if a is None else a if b is None else a + b

        def times(a, b):
            return None if b is None else a * b

        e = Q - 1
        g = [field[0]]
        for q in range(1, e):
            g.append(plus(field[q], times(-fa["mult"][q], g[q - 1])))
        part = [None] * e
        part[e - 1] = times(fa["inverse"][e - 1], g[e - 1])
        for q in range(e - 2, -1, -1):
            part[q] = plus(times(fa["inverse"][q], g[q]), times(-fa["up"][q], part[q + 1]))
        side = plus(field[e], times(-fa["below_end"], part[e - 1]))
        if part[0] is not None:
            side = side - fa["above_end"] * rolled(part[0], -1)
        ends = pcr_apply(fa["reduced"], side)
        before = rolled(ends, 1)
        return [
            plus(part[q], fa["v"][q] * before + fa["w"][q] * ends) for q in range(e)
        ] + [ends]

    def finish(self, fa, part, head, tail):
        first, last = fa["from_first"], fa["from_last"]
        return [part[q] + first[q] * head + last[q] * tail for q in range(Q)]

    def edges(self, cells):
        return jnp.where(self.last, cells[Q - 1], cells[0])


def faces(plus_first, disp_first, minus_last, disp_last, index, count):
    disp_next = rolled(disp_first, -1)
    shut = (index == count - 1) | (disp_last <= 0.0) | (disp_next <= 0.0)
    flux = 0.5 * (disp_last + disp_next)
    return (
        jnp.where(shut, 0.0, flux + minus_last),
        jnp.where(shut, 0.0, flux + rolled(plus_first, -1)),
    )


def kernel(
    nx, ny, ne, nsrc,
    decay_in, conc, cot, vel_x, vel_y, disp, wet_cells, emission, cells,
    state_out, adjoint_out, grad_out,
    decay, f_vx, f_vy, f_disp, f_wet, f_conc, f_cot, f_emis, f_cells,
    vel_t, disp_t, wet_t, work, work_t, adjoint_v, mate_v, first_v, last_v,
    onehot, rows_v, cols_v, owner_v,
    y_send, y_recv, x_send, x_recv, xb_send, xb_recv, yb_send, yb_recv, ends_a, ends_b,
    z_send, z_recv, e_send, e_recv, p_send, p_recv, g_send, g_recv, total,
    in_sem, mate_ssem, mate_rsem, ssem, rsem,
):
    gx, gy, en = lax.axis_index("gx"), lax.axis_index("gy"), lax.axis_index("ens")
    half = nsrc // ne
    chunk = half // nx
    tiles = chunk // LANES
    half_tiles = half // LANES
    mate = (gx, gy, wrapped(en + 1, ne))
    assert tiles == 2

    loads = [
        pltpu.make_async_copy(src, dst, in_sem.at[i])
        for i, (src, dst) in enumerate(
            [
                (vel_y, f_vy), (disp, f_disp), (wet_cells, f_wet), (cot.at[0], f_cot),
                (vel_x, f_vx), (cells, f_cells), (emission, f_emis), (conc.at[0], f_conc),
                (decay_in, decay),
            ]
        )
    ]

    def line_peer(o):
        return (gx, wrapped(gy + o, ny), en)

    def x_peer(o):
        return (gx ^ o, gy, en)

    def mate_peer(o):
        return (gx ^ o, gy, mate[2])

    barrier = pltpu.get_barrier_semaphore()
    greeted = [line_peer(o) for o in farthest_first(ny)]
    greeted += [peer(o) for o in plane_order(nx) for peer in (x_peer, mate_peer)] + [mate]
    for i, peer in enumerate(greeted):
        pl.semaphore_signal(barrier, inc=1, device_id=peer, device_id_type=MESH)
        if i == 2:
            for load in loads[:5]:
                load.start()
    for load in loads[5:]:
        load.start()

    def to_line(send, recv, slot):
        for o in farthest_first(ny):
            pltpu.make_async_remote_copy(
                src_ref=send, dst_ref=recv.at[gy], send_sem=ssem.at[slot],
                recv_sem=rsem.at[slot], device_id=line_peer(o), device_id_type=MESH,
            ).start()
        recv[gy] = send[...]

    def to_x(send, recv, slot):
        for o in plane_order(nx):
            pltpu.make_async_remote_copy(
                src_ref=send, dst_ref=recv.at[gx], send_sem=ssem.at[slot],
                recv_sem=rsem.at[slot], device_id=x_peer(o), device_id_type=MESH,
            ).start()
        recv[gx] = send[...]

    def to_each_x(send, recv, slot):
        for o in plane_order(nx):
            peer = gx ^ o
            pltpu.make_async_remote_copy(
                src_ref=send.at[peer], dst_ref=recv.at[gx], send_sem=ssem.at[slot],
                recv_sem=rsem.at[slot], device_id=x_peer(o), device_id_type=MESH,
            ).start()
        recv[gx] = send[gx]

    def arrived(recv, count, slot):
        part = recv.at[pl.ds(0, count)]
        pltpu.make_async_copy(part, part, rsem.at[slot]).wait()

    def sent(recv, count, slot):
        part = recv.at[pl.ds(0, count)]
        pltpu.make_async_copy(part, part, ssem.at[slot]).wait()

    def strided(ref, q):
        return ref[pl.ds(q, 8, stride=Q), :]

    def column(ref):
        return [strided(ref, q) for q in range(Q)]

    def put(ref, cells_):
        for q in range(Q):
            ref[pl.ds(q, 8, stride=Q), :] = cells_[q]

    y_line, x_line = Line(8), Line(2)
    zero8 = jnp.zeros((8, LANES), F32)
    lane_tracer = lax.broadcasted_iota(jnp.int32, (8, LANES), 1) // ROWS
    sub_tracer = lax.broadcasted_iota(jnp.int32, (8, LANES), 0) // 2

    def half_decay(tracer):
        value = jnp.full((8, LANES), decay[TR - 1], F32)
        for t in range(TR - 1):
            value = jnp.where(tracer == t, decay[t], value)
        return 0.5 * value

    for i in (8, 0, 1, 2, 3):
        loads[i].wait()
    wet_f = f_wet[...].astype(F32)
    for field, ref in ((f_vy[...], vel_t), (f_disp[...], disp_t), (wet_f, wet_t)):
        ref[...] = jnp.transpose(jnp.concatenate([field] * TR, axis=0))
    work_t[...] = jnp.transpose(f_cot[...].reshape(CELLS, COLS))
    y_fwd, y_adj = y_line.bands(
        column(vel_t), column(disp_t), column(wet_t), half_decay(lane_tracer)
    )
    y_part = y_line.solve(y_adj, column(work_t))
    end = COLS - 1
    tracer_row = lane_tracer[0:1]
    packed = jnp.where(
        tracer_row == 0,
        jnp.maximum(vel_t[0:1, :], 0.0),
        jnp.where(
            tracer_row == 1,
            disp_t[0:1, :] * wet_t[0:1, :],
            jnp.where(
                tracer_row == 2,
                jnp.maximum(-vel_t[end : end + 1, :], 0.0),
                disp_t[end : end + 1, :] * wet_t[end : end + 1, :],
            ),
        ),
    )
    e = Q - 1
    for i, row in enumerate(
        (
            y_part[0][0:1], y_part[e][7:8], y_fwd["from_first"][0][0:1],
            y_fwd["from_last"][e][7:8], y_fwd["from_last"][0][0:1],
            y_fwd["from_first"][e][7:8], packed, zero8[0:1],
        )
    ):
        y_send[i : i + 1, :] = row

    loads[4].wait()

    def spread(ref, as_float):
        out = []
        for q in range(Q):
            value = jnp.where(x_line.first, ref[q : q + 1, :], ref[q + Q : q + Q + 1, :])
            out.append(value.astype(F32) if as_float else value)
        return out

    x_fwd, x_adj = x_line.bands(
        spread(f_vx, False), spread(f_disp, False), spread(f_wet, True), half_decay(sub_tracer)
    )
    put(first_v, x_adj["from_first"])
    put(last_v, x_adj["from_last"])

    loads[5].wait()
    shift = (ny * COLS).bit_length() - 1
    source = f_cells[...]
    row = lax.shift_right_logical(source, shift)
    owner_v[...] = lax.shift_right_logical(row, ROWS.bit_length() - 1)
    rows_v[...] = row - gx * ROWS
    cols_v[...] = (source & (ny * COLS - 1)) - gy * COLS
    row_iota = lax.broadcasted_iota(jnp.int32, (ROWS, LANES), 0)
    col_iota = lax.broadcasted_iota(jnp.int32, (COLS, LANES), 0)

    def lanes(tile, count):
        return pl.ds(pl.multiple_of(tile * LANES, LANES), count * LANES)

    loads[6].wait()

    def scatter(step, acc):
        base = pl.multiple_of(step * TILES, TILES)
        row_tile = rows_v[pl.ds(base, TILES), :]
        col_tile = cols_v[pl.ds(base, TILES), :]
        values = f_emis[:, lanes(base, TILES)]
        high = values.astype(BF16).astype(F32)
        low = values - high
        left, hots = [], []
        for i in range(TILES):
            mask = row_iota == row_tile[i : i + 1, :]
            part = slice(i * LANES, (i + 1) * LANES)
            left.append(
                jnp.concatenate(
                    [
                        jnp.where(mask, piece[t : t + 1, part], 0.0).astype(BF16)
                        for piece in (high, low)
                        for t in range(TR)
                    ],
                    axis=0,
                )
            )
            hots.append(jnp.where(col_iota == col_tile[i : i + 1, :], 1.0, 0.0).astype(BF16))
        hot = jnp.concatenate(hots, axis=1)
        onehot[:, lanes(base, TILES)] = hot
        return acc + lax.dot_general(
            jnp.concatenate(left, axis=1),
            hot,
            (((1,), (1,)), ((), ())),
            preferred_element_type=F32,
        )

    placed = lax.fori_loop(
        0, nsrc // LANES // TILES, scatter, jnp.zeros((2 * CELLS, COLS), F32)
    )
    loads[7].wait()
    work[...] = f_conc[...].reshape(CELLS, COLS) + (placed[:CELLS] + placed[CELLS:])
    fx_part = x_line.solve(x_fwd, column(work))
    x_send[0:8, :] = x_line.edges(fx_part)
    x_send[8:16, :] = jnp.where(x_line.last, x_fwd["from_last"][e], x_fwd["from_first"][0])
    x_send[16:24, :] = jnp.where(x_line.last, x_fwd["from_first"][e], x_fwd["from_last"][0])
    x_send[24:25, :] = jnp.maximum(f_vx[0:1, :], 0.0)
    x_send[25:26, :] = f_disp[0:1, :] * wet_f[0:1, :]
    x_send[26:27, :] = jnp.maximum(-f_vx[ROWS - 1 : ROWS, :], 0.0)
    x_send[27:28, :] = f_disp[ROWS - 1 : ROWS, :] * wet_f[ROWS - 1 : ROWS, :]
    x_send[28:32, :] = zero8[0:4]
    ends_a[0:8, :] = zero8
    ends_b[0:8, :] = zero8

    pl.semaphore_wait(barrier, len(greeted))
    to_line(y_send, y_recv, 0)
    to_x(x_send, x_recv, 1)

    def split_bf16(values):
        high = values.astype(BF16)
        return jnp.concatenate([high, (values - high.astype(F32)).astype(BF16)], axis=1)

    sub = lax.broadcasted_iota(jnp.int32, (8, LANES), 0)

    def folded(parts):
        for bit in (1, 2, 4):
            keep = (sub & bit) == 0
            parts = [
                jnp.where(keep, a, b) + pltpu.roll(jnp.where(keep, b, a), bit, 0)
                for a, b in zip(parts[0::2], parts[1::2])
            ]
        return parts[0]

    def pick(fields, send, at, unrolled):
        left = jnp.concatenate([split_bf16(field) for field in fields], axis=0)
        per_step = min(TILES, half_tiles)

        def go(step, _):
            base = pl.multiple_of(en * half_tiles + step * per_step, per_step)
            row_tile = rows_v[pl.ds(base, per_step), :]
            hot = onehot[:, lanes(base, per_step)]
            found = jnp.dot(left, jnp.concatenate([hot, hot], axis=0), preferred_element_type=F32)
            masks = [row_iota == row_tile[i : i + 1, :] for i in range(per_step)]
            for pair in range(per_step // 2):
                for k, first in enumerate(at):
                    parts = []
                    for t in range(TR):
                        for i in (2 * pair, 2 * pair + 1):
                            start = (k * TR + t) * ROWS
                            line = found[start : start + ROWS, i * LANES : (i + 1) * LANES]
                            line = jnp.where(masks[i], line, 0.0)
                            parts.append((line[0:8] + line[8:16]) + (line[16:24] + line[24:32]))
                    send[step * (per_step // 2) + pair, first : first + 8, :] = folded(parts)
            return 0

        if unrolled:
            for step in range(half_tiles // per_step):
                go(step, 0)
        else:
            lax.fori_loop(0, half_tiles // per_step, go, 0)

    pick((first_v[...], last_v[...]), z_send, (0, TR * tiles), False)
    to_each_x(z_send, z_recv, 2)

    def x_piece(ref, k):
        return jnp.concatenate([ref[d, 8 * k : 8 * k + 8, :] for d in range(nx)], axis=0)

    def single(ref, k, n):
        return jnp.concatenate([ref[d, k : k + 1, :] for d in range(n)], axis=0)

    def expanded(rows):
        return jnp.concatenate(
            [jnp.broadcast_to(rows[d : d + 1], (8, LANES)) for d in range(nx)], axis=0
        )

    def from_next(value):
        later = rolled(value, -8)
        return jnp.concatenate([rolled(later[8 * d : 8 * d + 8], 1) for d in range(nx)], axis=0)

    def own_x(ref, at):
        block = ref[pl.ds(pl.multiple_of(8 * at, 8), 8), :]
        return jnp.where(x_line.last, block, rolled(block, -1))

    arrived(y_recv, ny - 1, 0)
    raw = single(y_recv, 6, ny)
    tracer_n = jnp.broadcast_to(tracer_row, (ny, LANES))
    quantities = []
    for k in range(4):
        value = jnp.where(tracer_n == k, raw, 0.0)
        value = value + pltpu.roll(value, ROWS, 1)
        quantities.append(value + pltpu.roll(value, 2 * ROWS, 1))
    index = lax.broadcasted_iota(jnp.int32, (ny, LANES), 0)
    y_before, y_after = faces(*quantities, index, ny)
    g00, gnn, g0n, gn0 = (single(y_recv, k, ny) for k in (2, 3, 4, 5))
    y_below = -gn0 * rolled(y_after, 1)
    y_center = 1.0 + gnn * y_before + rolled(g00, -1) * y_after
    y_above = jnp.where(index == ny - 1, 0.0, -rolled(g0n * y_before, -1))
    y_factors = pcr_factor(rolled(y_above, 1), y_center, rolled(y_below, -1), ny, 1)
    ends_a[8 : 8 + ny, :] = pcr_apply(
        y_factors, y_before * single(y_recv, 1, ny) - y_after * rolled(single(y_recv, 0, ny), -1)
    )
    head, tail = ends_a[pl.ds(7 + gy, 1), :], -ends_a[pl.ds(8 + gy, 1), :]
    put(work_t, y_line.finish(y_adj, y_part, head, tail))
    work[...] = jnp.transpose(work_t[...])
    ax_part = x_line.solve(x_adj, column(work))
    put(adjoint_v, ax_part)
    to_mate = pltpu.make_async_remote_copy(
        src_ref=adjoint_v, dst_ref=mate_v, send_sem=mate_ssem.at[0], recv_sem=mate_rsem.at[0],
        device_id=mate, device_id_type=MESH,
    )
    to_mate.start()
    xb_send[...] = x_line.edges(ax_part)

    to_mate.wait_recv()
    both = adjoint_v[...] + mate_v[...]
    work[...] = both
    both_edges = x_line.edges([strided(work, q) if q in (0, e) else None for q in range(Q)])
    e_send[...] = both_edges
    to_x(e_send, e_recv, 8)
    pick((both,), p_send, (0,), True)
    to_each_x(p_send, p_recv, 5)
    to_x(xb_send, xb_recv, 4)

    arrived(x_recv, nx - 1, 1)
    index = lax.broadcasted_iota(jnp.int32, (nx, LANES), 0)
    x_before, x_after = (
        expanded(face) for face in faces(*[single(x_recv, 24 + k, nx) for k in range(4)], index, nx)
    )
    diagonal, corner = x_piece(x_recv, 1), x_piece(x_recv, 2)
    x_below = -corner * rolled(x_after, 8)
    x_center = 1.0 + diagonal * x_before + from_next(diagonal) * x_after
    block_index = lax.broadcasted_iota(jnp.int32, (8 * nx, LANES), 0) // 8
    x_above = jnp.where(
        block_index == nx - 1, 0.0, -from_next(corner) * rolled(x_before, -8)
    )
    terms = x_piece(x_recv, 0)
    jump = pcr_apply(pcr_factor(x_below, x_center, x_above, nx, 8), terms - from_next(terms))
    ends_a[8 : 8 + 8 * nx, :] = x_after * jump
    ends_b[8 : 8 + 8 * nx, :] = x_before * jump
    put(work, x_line.finish(x_fwd, fx_part, own_x(ends_a, gx), -own_x(ends_b, gx + 1)))
    work_t[...] = jnp.transpose(work[...])
    fy_part = y_line.solve(y_fwd, column(work_t))
    yb_send[0:1, :] = fy_part[0][0:1]
    yb_send[1:2, :] = fy_part[e][7:8]
    yb_send[2:8, :] = zero8[0:6]
    to_line(yb_send, yb_recv, 3)
    x_factors = pcr_factor(rolled(x_above, 8), x_center, rolled(x_below, -8), nx, 8)

    y_fwd_factors = pcr_factor(y_below, y_center, y_above, ny, 1)
    arrived(z_recv, nx - 1, 2)

    def summed(ref, first, count, n):
        value = ref[0, first : first + count, :]
        for i in range(1, n):
            value = value + ref[i, first : first + count, :]
        return value

    width = TR * tiles
    z_first, z_last = summed(z_recv, 0, width, nx), summed(z_recv, width, width, nx)

    arrived(e_recv, nx - 1, 8)

    def flux_of(ref):
        terms = x_piece(ref, 0)
        return pcr_apply(x_factors, x_before * terms - x_after * from_next(terms))

    flux = flux_of(e_recv)
    mine = pl.multiple_of(en * half_tiles + gx * tiles, tiles)
    hot = onehot[:, lanes(mine, tiles)]
    found = jnp.dot(
        split_bf16(flux), jnp.concatenate([hot, hot], axis=0), preferred_element_type=F32
    )
    owner = owner_v[pl.ds(mine, tiles), :]
    for i in range(tiles):
        into, out = zero8, zero8
        for d in range(nx):
            value = found[8 * d : 8 * d + 8, i * LANES : (i + 1) * LANES]
            into = into + jnp.where(owner[i : i + 1, :] == d + 1, value, 0.0)
            out = out + jnp.where(owner[i : i + 1, :] == d, value, 0.0)
        for t in range(TR):
            spot = slice(tiles * t + i, tiles * t + i + 1)
            at = slice(2 * t + 1, 2 * t + 2)
            g_send[spot, :] = z_first[spot] * into[at] - z_last[spot] * out[at]
    arrived(p_recv, nx - 1, 5)
    g_send[...] = g_send[...] + summed(p_recv, 0, width, nx)
    to_line(g_send, g_recv, 6)

    arrived(xb_recv, nx - 1, 4)
    ends_a[8 : 8 + 8 * nx, :] = flux_of(xb_recv)
    put(
        adjoint_out,
        x_line.finish(x_adj, column(adjoint_v), own_x(ends_a, gx), -own_x(ends_a, gx + 1)),
    )

    arrived(yb_recv, ny - 1, 3)
    jump = pcr_apply(
        y_fwd_factors, single(yb_recv, 1, ny) - rolled(single(yb_recv, 0, ny), -1)
    )
    ends_a[8 : 8 + ny, :] = y_after * jump
    ends_b[8 : 8 + ny, :] = y_before * jump
    head, tail = ends_a[pl.ds(7 + gy, 1), :], -ends_b[pl.ds(8 + gy, 1), :]
    put(work_t, y_line.finish(y_fwd, fy_part, head, tail))
    state_out[...] = jnp.transpose(work_t[...])

    arrived(g_recv, ny - 1, 6)
    sums = summed(g_recv, 0, width, ny)
    for t in range(TR):
        for i in range(tiles):
            total[t : t + 1, i * LANES : (i + 1) * LANES] = sums[tiles * t + i : tiles * t + i + 1]

    here = grad_out.at[:, pl.ds(pl.multiple_of(en * half + gx * chunk, LANES), chunk)]
    peers = [peer(o) for o in plane_order(nx) for peer in (x_peer, mate_peer)] + [mate]
    for peer in peers:
        pltpu.make_async_remote_copy(
            src_ref=total, dst_ref=here, send_sem=ssem.at[7], recv_sem=rsem.at[7],
            device_id=peer, device_id_type=MESH,
        ).start()
    grad_out[:, pl.ds(pl.multiple_of(en * half + gx * chunk, LANES), chunk)] = total[...]

    sent(y_recv, ny - 1, 0)
    sent(x_recv, nx - 1, 1)
    sent(z_recv, nx - 1, 2)
    sent(yb_recv, ny - 1, 3)
    sent(xb_recv, nx - 1, 4)
    sent(p_recv, nx - 1, 5)
    sent(e_recv, nx - 1, 8)
    sent(g_recv, ny - 1, 6)
    to_mate.wait_send()

    rest = grad_out.at[:, pl.ds(0, len(peers) * chunk)]
    pltpu.make_async_copy(rest, rest, ssem.at[7]).wait()
    pltpu.make_async_copy(rest, rest, rsem.at[7]).wait()


def store(state, adjoint, gradient, state_out, adjoint_out, grad_out, sem):
    moves = ((gradient, grad_out), (state, state_out), (adjoint, adjoint_out))
    copies = [pltpu.make_async_copy(m[0], m[1], sem.at[i]) for i, m in enumerate(moves)]
    for copy in copies:
        copy.start()
    for copy in copies:
        copy.wait()


def per_device(
    nx, ny, ne, concentration, cotangent, vel_x, vel_y, dispersion, wet_cells, decay_rate, emission,
    source_cell,
):
    nsrc = source_cell.shape[0]
    chunk = nsrc // (nx * ne)
    operands = [
        pltpu.with_memory_space_constraint(x, pltpu.HBM)
        for x in (
            decay_rate, concentration, cotangent, vel_x, vel_y, dispersion, wet_cells, emission,
            source_cell.reshape(nsrc // LANES, LANES),
        )
    ]
    width = TR * chunk // LANES
    square = pltpu.VMEM((CELLS, COLS), F32)
    block = pltpu.VMEM((ROWS, COLS), F32)

    def vmem(*shape, dtype=F32):
        return pltpu.VMEM(shape, dtype)

    index = vmem(nsrc // LANES, LANES, dtype=jnp.int32)
    ends = vmem(8 + 8 * max(nx, ny), LANES)
    scratch = [
        pltpu.SMEM((TR,), F32), block, block, block, vmem(ROWS, COLS, dtype=jnp.int32),
        vmem(TR, ROWS, COLS), vmem(TR, ROWS, COLS), vmem(TR, nsrc), index,
        square, square, square, square, square, square, square, square, square,
        vmem(COLS, nsrc, dtype=BF16), index, index, index,
        vmem(8, LANES), vmem(ny, 8, LANES), vmem(32, LANES), vmem(nx, 32, LANES),
        vmem(8, LANES), vmem(nx, 8, LANES), vmem(8, LANES), vmem(ny, 8, LANES), ends, ends,
        vmem(nx, 2 * width, LANES), vmem(nx, 2 * width, LANES),
        vmem(8, LANES), vmem(nx, 8, LANES), vmem(nx, width, LANES), vmem(nx, width, LANES),
        vmem(width, LANES), vmem(ny, width, LANES), vmem(TR, chunk),
        pltpu.SemaphoreType.DMA((9,)),
        pltpu.SemaphoreType.DMA((1,)), pltpu.SemaphoreType.DMA((1,)),
        pltpu.SemaphoreType.DMA((9,)), pltpu.SemaphoreType.DMA((9,)),
    ]
    hbm = pl.BlockSpec(memory_space=pl.ANY)
    on_chip = pl.BlockSpec(memory_space=pltpu.VMEM)
    state, adjoint, gradient = pl.pallas_call(
        functools.partial(kernel, nx, ny, ne, nsrc),
        out_shape=(
            jax.ShapeDtypeStruct((CELLS, COLS), F32),
            jax.ShapeDtypeStruct((CELLS, COLS), F32),
            jax.ShapeDtypeStruct(emission.shape, F32),
        ),
        in_specs=[hbm] * 9,
        out_specs=(on_chip, on_chip, on_chip),
        scratch_shapes=scratch,
        compiler_params=pltpu.CompilerParams(
            collective_id=0, has_side_effects=True, vmem_limit_bytes=VMEM_BYTES
        ),
        name="adi_step",
    )(*operands)
    shape = concentration.shape
    return pl.pallas_call(
        store,
        out_shape=(
            jax.ShapeDtypeStruct(shape, F32),
            jax.ShapeDtypeStruct(shape, F32),
            jax.ShapeDtypeStruct(emission.shape, F32),
        ),
        in_specs=[on_chip] * 3,
        out_specs=(hbm, hbm, hbm),
        scratch_shapes=[pltpu.SemaphoreType.DMA((3,))],
        compiler_params=pltpu.CompilerParams(vmem_limit_bytes=VMEM_BYTES),
        name="store",
    )(state.reshape(shape), adjoint.reshape(shape), gradient)


VMEM_BYTES = 32 * 1024 * 1024


def solution(mesh):
    nx, ny, ne = (mesh.shape[a] for a in ("gx", "gy", "ens"))
    field = P("ens", None, "gx", "gy")
    plane = P("gx", "gy")
    return jax.shard_map(
        functools.partial(per_device, nx, ny, ne),
        mesh=mesh,
        in_specs=(field, field, plane, plane, plane, plane, P(), P(), P()),
        out_specs=(field, field, P()),
        check_vma=False,
    )
```

```python
import functools

import jax
import jax.numpy as jnp
from jax import lax
from jax.experimental import pallas as pl
from jax.experimental.pallas import tpu as pltpu
from jax.sharding import PartitionSpec as P

MESH = pl.DeviceIdType.MESH
TR, ROWS, COLS, LANES, Q = 4, 32, 128, 128, 16
CELLS = TR * ROWS
F32, BF16 = jnp.float32, jnp.bfloat16
TILES = 8


def rolled(x, shift):
    n = x.shape[0]
    shift = shift % n
    if shift == 0:
        return x
    if shift % 8 == 0:
        return jnp.concatenate([x[n - shift :], x[: n - shift]], axis=0)
    return pltpu.roll(x, shift, 0)


def wrapped(i, n):
    return i & (n - 1) if n & (n - 1) == 0 else lax.rem(i, n)


def farthest_first(n):
    return sorted(range(1, n), key=lambda o: (-min(o, n - o), o))


def plane_order(n):
    far = (0, 1, 2, 1)
    return sorted(range(1, n), key=lambda o: -(far[o % 4] + far[o // 4 % 4]))


def pcr_factor(below, center, above, count, unit):
    steps, stride = [], 1
    while stride < count:
        k = stride * unit
        inverse = 1.0 / center
        alpha = -below * rolled(inverse, k)
        gamma = -above * rolled(inverse, -k)
        center = center + alpha * rolled(above, k) + gamma * rolled(below, -k)
        below, above = alpha * rolled(below, k), gamma * rolled(above, -k)
        steps.append((k, alpha, gamma))
        stride *= 2
    return steps, 1.0 / center


def pcr_apply(factors, side):
    steps, inverse = factors
    for k, alpha, gamma in steps:
        side = side + alpha * rolled(side, k) + gamma * rolled(side, -k)
    return side * inverse


class Line:
    def __init__(self, size):
        self.size = size
        sub = lax.broadcasted_iota(jnp.int32, (8, LANES), 0) % size
        self.first = sub == 0
        self.last = sub == size - 1

    def extended(self, cells):
        head = jnp.where(self.first, 0.0, rolled(cells[-1], 1))
        tail = jnp.where(self.last, 0.0, rolled(cells[0], -1))
        return [head] + cells + [tail]

    def bands(self, vel, disp, wet, half_decay):
        vel, disp, wet = (self.extended(cells) for cells in (vel, disp, wet))
        gate = [wet[k] * wet[k + 1] for k in range(Q + 1)]
        flux = [0.5 * (disp[k] + disp[k + 1]) * gate[k] for k in range(Q + 1)]
        plus = [jnp.maximum(v, 0.0) for v in vel]
        minus = [jnp.maximum(-v, 0.0) for v in vel]
        fwd_below = [-(flux[q] + plus[q + 1] * gate[q]) for q in range(Q)]
        fwd_above = [-(flux[q + 1] + minus[q + 1] * gate[q + 1]) for q in range(Q)]
        adj_below = [-(flux[q] + minus[q] * gate[q]) for q in range(Q)]
        adj_above = [-(flux[q + 1] + plus[q + 2] * gate[q + 1]) for q in range(Q)]
        center = [
            (1.0 + flux[q] + flux[q + 1] + plus[q + 1] * gate[q] + minus[q + 1] * gate[q + 1])
            + half_decay
            for q in range(Q)
        ]
        inverse = [1.0 / center[0]]
        for q in range(1, Q - 1):
            pivot = center[q] - fwd_below[q] * fwd_above[q - 1] * inverse[q - 1]
            inverse.append(1.0 / pivot)
        forward = self.factor(fwd_below, center, fwd_above, inverse)
        adjoint = self.factor(adj_below, center, adj_above, inverse)
        return forward, adjoint

    def factor(self, below, center, above, inverse):
        e = Q - 1
        fa = dict(inverse=inverse, below_end=below[e], above_end=above[e])
        fa["mult"] = mult = [None] + [below[q] * inverse[q - 1] for q in range(1, e)]
        fa["up"] = up = [above[q] * inverse[q] for q in range(e)]
        start = [-below[0]]
        for q in range(1, e):
            start.append(-mult[q] * start[q - 1])
        v, w = [None] * e, [None] * e
        v[e - 1] = start[e - 1] * inverse[e - 1]
        w[e - 1] = -up[e - 1]
        for q in range(e - 2, -1, -1):
            v[q] = start[q] * inverse[q] - up[q] * v[q + 1]
            w[q] = -up[q] * w[q + 1]
        fa["v"], fa["w"] = v, w
        fa["reduced"] = pcr_factor(
            below[e] * v[e - 1],
            center[e] + below[e] * w[e - 1] + above[e] * rolled(v[0], -1),
            above[e] * rolled(w[0], -1),
            self.size,
            1,
        )
        head = jnp.where(self.first, 1.0, 0.0)
        fa["from_first"] = self.solve(fa, [head] + [None] * e)
        fa["from_last"] = self.solve(fa, [None] * e + [jnp.where(self.last, 1.0, 0.0)])
        return fa

    def solve(self, fa, field):
        def plus(a, b):
            return b if a is None else a if b is None else a + b

        def times(a, b):
            return None if b is None else a * b

        e = Q - 1
        g = [field[0]]
        for q in range(1, e):
            g.append(plus(field[q], times(-fa["mult"][q], g[q - 1])))
        part = [None] * e
        part[e - 1] = times(fa["inverse"][e - 1], g[e - 1])
        for q in range(e - 2, -1, -1):
            part[q] = plus(times(fa["inverse"][q], g[q]), times(-fa["up"][q], part[q + 1]))
        side = plus(field[e], times(-fa["below_end"], part[e - 1]))
        if part[0] is not None:
            side = side - fa["above_end"] * rolled(part[0], -1)
        ends = pcr_apply(fa["reduced"], side)
        before = rolled(ends, 1)
        return [
            plus(part[q], fa["v"][q] * before + fa["w"][q] * ends) for q in range(e)
        ] + [ends]

    def finish(self, fa, part, head, tail):
        first, last = fa["from_first"], fa["from_last"]
        return [part[q] + first[q] * head + last[q] * tail for q in range(Q)]

    def edges(self, cells):
        return jnp.where(self.last, cells[Q - 1], cells[0])


def faces(plus_first, disp_first, minus_last, disp_last, index, count):
    disp_next = rolled(disp_first, -1)
    shut = (index == count - 1) | (disp_last <= 0.0) | (disp_next <= 0.0)
    flux = 0.5 * (disp_last + disp_next)
    return (
        jnp.where(shut, 0.0, flux + minus_last),
        jnp.where(shut, 0.0, flux + rolled(plus_first, -1)),
    )


def kernel(
    nx, ny, ne, nsrc,
    decay_in, conc, cot, vel_x, vel_y, disp, wet_cells, emission, cells,
    state_out, adjoint_out, grad_out,
    decay, f_vx, f_vy, f_disp, f_wet, f_conc, f_cot, f_emis, f_cells,
    vel_t, disp_t, wet_t, work, work_t, adjoint_v, mate_v, first_v, last_v,
    onehot, rows_v, cols_v, owner_v,
    y_send, y_recv, x_send, x_recv, xb_send, xb_recv, yb_send, yb_recv, ends_a, ends_b,
    z_send, z_recv, e_send, e_recv, p_send, p_recv, g_send, g_recv, total,
    in_sem, mate_ssem, mate_rsem, ssem, rsem,
):
    gx, gy, en = lax.axis_index("gx"), lax.axis_index("gy"), lax.axis_index("ens")
    half = nsrc // ne
    chunk = half // nx
    tiles = chunk // LANES
    half_tiles = half // LANES
    mate = (gx, gy, wrapped(en + 1, ne))
    assert tiles == 2

    loads = [
        pltpu.make_async_copy(src, dst, in_sem.at[i])
        for i, (src, dst) in enumerate(
            [
                (vel_y, f_vy), (disp, f_disp), (wet_cells, f_wet), (cot.at[0], f_cot),
                (vel_x, f_vx), (cells, f_cells), (emission, f_emis), (conc.at[0], f_conc),
                (decay_in, decay),
            ]
        )
    ]

    def line_peer(o):
        return (gx, wrapped(gy + o, ny), en)

    def x_peer(o):
        return (gx ^ o, gy, en)

    def mate_peer(o):
        return (gx ^ o, gy, mate[2])

    barrier = pltpu.get_barrier_semaphore()
    greeted = [line_peer(o) for o in farthest_first(ny)]
    greeted += [peer(o) for o in plane_order(nx) for peer in (x_peer, mate_peer)] + [mate]
    for i, peer in enumerate(greeted):
        pl.semaphore_signal(barrier, inc=1, device_id=peer, device_id_type=MESH)
        if i == 2:
            for load in loads[:5]:
                load.start()
    for load in loads[5:]:
        load.start()

    def to_line(send, recv, slot):
        for o in farthest_first(ny):
            pltpu.make_async_remote_copy(
                src_ref=send, dst_ref=recv.at[gy], send_sem=ssem.at[slot],
                recv_sem=rsem.at[slot], device_id=line_peer(o), device_id_type=MESH,
            ).start()
        recv[gy] = send[...]

    def to_x(send, recv, slot):
        for o in plane_order(nx):
            pltpu.make_async_remote_copy(
                src_ref=send, dst_ref=recv.at[gx], send_sem=ssem.at[slot],
                recv_sem=rsem.at[slot], device_id=x_peer(o), device_id_type=MESH,
            ).start()
        recv[gx] = send[...]

    def to_each_x(send, recv, slot):
        for o in plane_order(nx):
            peer = gx ^ o
            pltpu.make_async_remote_copy(
                src_ref=send.at[peer], dst_ref=recv.at[gx], send_sem=ssem.at[slot],
                recv_sem=rsem.at[slot], device_id=x_peer(o), device_id_type=MESH,
            ).start()
        recv[gx] = send[gx]

    def arrived(recv, count, slot):
        part = recv.at[pl.ds(0, count)]
        pltpu.make_async_copy(part, part, rsem.at[slot]).wait()

    def sent(recv, count, slot):
        part = recv.at[pl.ds(0, count)]
        pltpu.make_async_copy(part, part, ssem.at[slot]).wait()

    def strided(ref, q):
        return ref[pl.ds(q, 8, stride=Q), :]

    def column(ref):
        return [strided(ref, q) for q in range(Q)]

    def put(ref, cells_):
        for q in range(Q):
            ref[pl.ds(q, 8, stride=Q), :] = cells_[q]

    y_line, x_line = Line(8), Line(2)
    zero8 = jnp.zeros((8, LANES), F32)
    lane_tracer = lax.broadcasted_iota(jnp.int32, (8, LANES), 1) // ROWS
    sub_tracer = lax.broadcasted_iota(jnp.int32, (8, LANES), 0) // 2

    def half_decay(tracer):
        value = jnp.full((8, LANES), decay[TR - 1], F32)
        for t in range(TR - 1):
            value = jnp.where(tracer == t, decay[t], value)
        return 0.5 * value

    for i in (8, 0, 1, 2, 3):
        loads[i].wait()
    wet_f = f_wet[...].astype(F32)
    for field, ref in ((f_vy[...], vel_t), (f_disp[...], disp_t), (wet_f, wet_t)):
        ref[...] = jnp.transpose(jnp.concatenate([field] * TR, axis=0))
    work_t[...] = jnp.transpose(f_cot[...].reshape(CELLS, COLS))
    y_fwd, y_adj = y_line.bands(
        column(vel_t), column(disp_t), column(wet_t), half_decay(lane_tracer)
    )
    y_part = y_line.solve(y_adj, column(work_t))
    end = COLS - 1
    tracer_row = lane_tracer[0:1]
    packed = jnp.where(
        tracer_row == 0,
        jnp.maximum(vel_t[0:1, :], 0.0),
        jnp.where(
            tracer_row == 1,
            disp_t[0:1, :] * wet_t[0:1, :],
            jnp.where(
                tracer_row == 2,
                jnp.maximum(-vel_t[end : end + 1, :], 0.0),
                disp_t[end : end + 1, :] * wet_t[end : end + 1, :],
            ),
        ),
    )
    e = Q - 1
    for i, row in enumerate(
        (
            y_part[0][0:1], y_part[e][7:8], y_fwd["from_first"][0][0:1],
            y_fwd["from_last"][e][7:8], y_fwd["from_last"][0][0:1],
            y_fwd["from_first"][e][7:8], packed, zero8[0:1],
        )
    ):
        y_send[i : i + 1, :] = row

    loads[4].wait()

    def spread(ref, as_float):
        out = []
        for q in range(Q):
            value = jnp.where(x_line.first, ref[q : q + 1, :], ref[q + Q : q + Q + 1, :])
            out.append(value.astype(F32) if as_float else value)
        return out

    x_fwd, x_adj = x_line.bands(
        spread(f_vx, False), spread(f_disp, False), spread(f_wet, True), half_decay(sub_tracer)
    )
    put(first_v, x_adj["from_first"])
    put(last_v, x_adj["from_last"])

    loads[5].wait()
    shift = (ny * COLS).bit_length() - 1
    source = f_cells[...]
    row = lax.shift_right_logical(source, shift)
    owner_v[...] = lax.shift_right_logical(row, ROWS.bit_length() - 1)
    rows_v[...] = row - gx * ROWS
    cols_v[...] = (source & (ny * COLS - 1)) - gy * COLS
    row_iota = lax.broadcasted_iota(jnp.int32, (ROWS, LANES), 0)
    col_iota = lax.broadcasted_iota(jnp.int32, (COLS, LANES), 0)

    def lanes(tile, count):
        return pl.ds(pl.multiple_of(tile * LANES, LANES), count * LANES)

    loads[6].wait()

    def scatter(step, acc):
        base = pl.multiple_of(step * TILES, TILES)
        row_tile = rows_v[pl.ds(base, TILES), :]
        col_tile = cols_v[pl.ds(base, TILES), :]
        values = f_emis[:, lanes(base, TILES)]
        high = values.astype(BF16).astype(F32)
        low = values - high
        left, hots = [], []
        for i in range(TILES):
            mask = row_iota == row_tile[i : i + 1, :]
            part = slice(i * LANES, (i + 1) * LANES)
            left.append(
                jnp.concatenate(
                    [
                        jnp.where(mask, piece[t : t + 1, part], 0.0).astype(BF16)
                        for piece in (high, low)
                        for t in range(TR)
                    ],
                    axis=0,
                )
            )
            hots.append(jnp.where(col_iota == col_tile[i : i + 1, :], 1.0, 0.0).astype(BF16))
        hot = jnp.concatenate(hots, axis=1)
        onehot[:, lanes(base, TILES)] = hot
        return acc + lax.dot_general(
            jnp.concatenate(left, axis=1),
            hot,
            (((1,), (1,)), ((), ())),
            preferred_element_type=F32,
        )

    placed = lax.fori_loop(
        0, nsrc // LANES // TILES, scatter, jnp.zeros((2 * CELLS, COLS), F32)
    )
    loads[7].wait()
    work[...] = f_conc[...].reshape(CELLS, COLS) + (placed[:CELLS] + placed[CELLS:])
    fx_part = x_line.solve(x_fwd, column(work))
    x_send[0:8, :] = x_line.edges(fx_part)
    x_send[8:16, :] = jnp.where(x_line.last, x_fwd["from_last"][e], x_fwd["from_first"][0])
    x_send[16:24, :] = jnp.where(x_line.last, x_fwd["from_first"][e], x_fwd["from_last"][0])
    x_send[24:25, :] = jnp.maximum(f_vx[0:1, :], 0.0)
    x_send[25:26, :] = f_disp[0:1, :] * wet_f[0:1, :]
    x_send[26:27, :] = jnp.maximum(-f_vx[ROWS - 1 : ROWS, :], 0.0)
    x_send[27:28, :] = f_disp[ROWS - 1 : ROWS, :] * wet_f[ROWS - 1 : ROWS, :]
    x_send[28:32, :] = zero8[0:4]
    ends_a[0:8, :] = zero8
    ends_b[0:8, :] = zero8

    pl.semaphore_wait(barrier, len(greeted))
    to_line(y_send, y_recv, 0)
    to_x(x_send, x_recv, 1)

    def split_bf16(values):
        high = values.astype(BF16)
        return jnp.concatenate([high, (values - high.astype(F32)).astype(BF16)], axis=1)

    sub = lax.broadcasted_iota(jnp.int32, (8, LANES), 0)

    def folded(parts):
        for bit in (1, 2, 4):
            keep = (sub & bit) == 0
            parts = [
                jnp.where(keep, a, b) + pltpu.roll(jnp.where(keep, b, a), bit, 0)
                for a, b in zip(parts[0::2], parts[1::2])
            ]
        return parts[0]

    def pick(fields, send, at, unrolled):
        left = jnp.concatenate([split_bf16(field) for field in fields], axis=0)
        per_step = min(TILES, half_tiles)

        def go(step, _):
            base = pl.multiple_of(en * half_tiles + step * per_step, per_step)
            row_tile = rows_v[pl.ds(base, per_step), :]
            hot = onehot[:, lanes(base, per_step)]
            found = jnp.dot(left, jnp.concatenate([hot, hot], axis=0), preferred_element_type=F32)
            masks = [row_iota == row_tile[i : i + 1, :] for i in range(per_step)]
            for pair in range(per_step // 2):
                for k, first in enumerate(at):
                    parts = []
                    for t in range(TR):
                        for i in (2 * pair, 2 * pair + 1):
                            start = (k * TR + t) * ROWS
                            line = found[start : start + ROWS, i * LANES : (i + 1) * LANES]
                            line = jnp.where(masks[i], line, 0.0)
                            parts.append((line[0:8] + line[8:16]) + (line[16:24] + line[24:32]))
                    send[step * (per_step // 2) + pair, first : first + 8, :] = folded(parts)
            return 0

        if unrolled:
            steps, blocks = half_tiles // per_step, per_step // tiles
            order = plane_order(steps) + [0]
            middle = steps // 2
            for group in (order[:middle], order[middle:]):
                for far in group:
                    go((gx // blocks) ^ far, 0)
                for near in plane_order(blocks) + [0]:
                    for o in [far * blocks + near for far in group]:
                        if o:
                            pltpu.make_async_remote_copy(
                                src_ref=p_send.at[gx ^ o], dst_ref=p_recv.at[gx],
                                send_sem=ssem.at[5], recv_sem=rsem.at[5],
                                device_id=x_peer(o), device_id_type=MESH,
                            ).start()
            p_recv[gx] = p_send[gx]
        else:
            lax.fori_loop(0, half_tiles // per_step, go, 0)

    pick((first_v[...], last_v[...]), z_send, (0, TR * tiles), False)
    to_each_x(z_send, z_recv, 2)

    def x_piece(ref, k):
        return jnp.concatenate([ref[d, 8 * k : 8 * k + 8, :] for d in range(nx)], axis=0)

    def single(ref, k, n):
        return jnp.concatenate([ref[d, k : k + 1, :] for d in range(n)], axis=0)

    def expanded(rows):
        return jnp.concatenate(
            [jnp.broadcast_to(rows[d : d + 1], (8, LANES)) for d in range(nx)], axis=0
        )

    def from_next(value):
        later = rolled(value, -8)
        return jnp.concatenate([rolled(later[8 * d : 8 * d + 8], 1) for d in range(nx)], axis=0)

    def own_x(ref, at):
        block = ref[pl.ds(pl.multiple_of(8 * at, 8), 8), :]
        return jnp.where(x_line.last, block, rolled(block, -1))

    arrived(y_recv, ny - 1, 0)
    raw = single(y_recv, 6, ny)
    tracer_n = jnp.broadcast_to(tracer_row, (ny, LANES))
    quantities = []
    for k in range(4):
        value = jnp.where(tracer_n == k, raw, 0.0)
        value = value + pltpu.roll(value, ROWS, 1)
        quantities.append(value + pltpu.roll(value, 2 * ROWS, 1))
    index = lax.broadcasted_iota(jnp.int32, (ny, LANES), 0)
    y_before, y_after = faces(*quantities, index, ny)
    g00, gnn, g0n, gn0 = (single(y_recv, k, ny) for k in (2, 3, 4, 5))
    y_below = -gn0 * rolled(y_after, 1)
    y_center = 1.0 + gnn * y_before + rolled(g00, -1) * y_after
    y_above = jnp.where(index == ny - 1, 0.0, -rolled(g0n * y_before, -1))
    y_factors = pcr_factor(rolled(y_above, 1), y_center, rolled(y_below, -1), ny, 1)
    ends_a[8 : 8 + ny, :] = pcr_apply(
        y_factors, y_before * single(y_recv, 1, ny) - y_after * rolled(single(y_recv, 0, ny), -1)
    )
    head, tail = ends_a[pl.ds(7 + gy, 1), :], -ends_a[pl.ds(8 + gy, 1), :]
    put(work_t, y_line.finish(y_adj, y_part, head, tail))
    work[...] = jnp.transpose(work_t[...])
    ax_part = x_line.solve(x_adj, column(work))
    put(adjoint_v, ax_part)
    to_mate = pltpu.make_async_remote_copy(
        src_ref=adjoint_v, dst_ref=mate_v, send_sem=mate_ssem.at[0], recv_sem=mate_rsem.at[0],
        device_id=mate, device_id_type=MESH,
    )
    to_mate.start()
    xb_send[...] = x_line.edges(ax_part)

    to_mate.wait_recv()
    both = adjoint_v[...] + mate_v[...]
    work[...] = both
    both_edges = x_line.edges([strided(work, q) if q in (0, e) else None for q in range(Q)])
    e_send[...] = both_edges
    to_x(e_send, e_recv, 8)
    pick((both,), p_send, (0,), True)
    to_x(xb_send, xb_recv, 4)

    arrived(x_recv, nx - 1, 1)
    index = lax.broadcasted_iota(jnp.int32, (nx, LANES), 0)
    x_before, x_after = (
        expanded(face) for face in faces(*[single(x_recv, 24 + k, nx) for k in range(4)], index, nx)
    )
    diagonal, corner = x_piece(x_recv, 1), x_piece(x_recv, 2)
    x_below = -corner * rolled(x_after, 8)
    x_center = 1.0 + diagonal * x_before + from_next(diagonal) * x_after
    block_index = lax.broadcasted_iota(jnp.int32, (8 * nx, LANES), 0) // 8
    x_above = jnp.where(
        block_index == nx - 1, 0.0, -from_next(corner) * rolled(x_before, -8)
    )
    terms = x_piece(x_recv, 0)
    jump = pcr_apply(pcr_factor(x_below, x_center, x_above, nx, 8), terms - from_next(terms))
    ends_a[8 : 8 + 8 * nx, :] = x_after * jump
    ends_b[8 : 8 + 8 * nx, :] = x_before * jump
    put(work, x_line.finish(x_fwd, fx_part, own_x(ends_a, gx), -own_x(ends_b, gx + 1)))
    work_t[...] = jnp.transpose(work[...])
    fy_part = y_line.solve(y_fwd, column(work_t))
    yb_send[0:1, :] = fy_part[0][0:1]
    yb_send[1:2, :] = fy_part[e][7:8]
    yb_send[2:8, :] = zero8[0:6]
    to_line(yb_send, yb_recv, 3)
    x_factors = pcr_factor(rolled(x_above, 8), x_center, rolled(x_below, -8), nx, 8)

    y_fwd_factors = pcr_factor(y_below, y_center, y_above, ny, 1)
    arrived(z_recv, nx - 1, 2)

    def summed(ref, first, count, n):
        value = ref[0, first : first + count, :]
        for i in range(1, n):
            value = value + ref[i, first : first + count, :]
        return value

    width = TR * tiles
    z_first, z_last = summed(z_recv, 0, width, nx), summed(z_recv, width, width, nx)

    arrived(e_recv, nx - 1, 8)

    def flux_of(ref):
        terms = x_piece(ref, 0)
        return pcr_apply(x_factors, x_before * terms - x_after * from_next(terms))

    flux = flux_of(e_recv)
    mine = pl.multiple_of(en * half_tiles + gx * tiles, tiles)
    hot = onehot[:, lanes(mine, tiles)]
    found = jnp.dot(
        split_bf16(flux), jnp.concatenate([hot, hot], axis=0), preferred_element_type=F32
    )
    owner = owner_v[pl.ds(mine, tiles), :]
    for i in range(tiles):
        into, out = zero8, zero8
        for d in range(nx):
            value = found[8 * d : 8 * d + 8, i * LANES : (i + 1) * LANES]
            into = into + jnp.where(owner[i : i + 1, :] == d + 1, value, 0.0)
            out = out + jnp.where(owner[i : i + 1, :] == d, value, 0.0)
        for t in range(TR):
            spot = slice(tiles * t + i, tiles * t + i + 1)
            at = slice(2 * t + 1, 2 * t + 2)
            g_send[spot, :] = z_first[spot] * into[at] - z_last[spot] * out[at]
    arrived(p_recv, nx - 1, 5)
    g_send[...] = g_send[...] + summed(p_recv, 0, width, nx)
    to_line(g_send, g_recv, 6)

    arrived(xb_recv, nx - 1, 4)
    ends_a[8 : 8 + 8 * nx, :] = flux_of(xb_recv)
    put(
        adjoint_out,
        x_line.finish(x_adj, column(adjoint_v), own_x(ends_a, gx), -own_x(ends_a, gx + 1)),
    )

    arrived(yb_recv, ny - 1, 3)
    jump = pcr_apply(
        y_fwd_factors, single(yb_recv, 1, ny) - rolled(single(yb_recv, 0, ny), -1)
    )
    ends_a[8 : 8 + ny, :] = y_after * jump
    ends_b[8 : 8 + ny, :] = y_before * jump
    head, tail = ends_a[pl.ds(7 + gy, 1), :], -ends_b[pl.ds(8 + gy, 1), :]
    put(work_t, y_line.finish(y_fwd, fy_part, head, tail))
    state_out[...] = jnp.transpose(work_t[...])

    arrived(g_recv, ny - 1, 6)
    sums = summed(g_recv, 0, width, ny)
    for t in range(TR):
        for i in range(tiles):
            total[t : t + 1, i * LANES : (i + 1) * LANES] = sums[tiles * t + i : tiles * t + i + 1]

    here = grad_out.at[:, pl.ds(pl.multiple_of(en * half + gx * chunk, LANES), chunk)]
    peers = [peer(o) for o in plane_order(nx) for peer in (x_peer, mate_peer)] + [mate]
    for peer in peers:
        pltpu.make_async_remote_copy(
            src_ref=total, dst_ref=here, send_sem=ssem.at[7], recv_sem=rsem.at[7],
            device_id=peer, device_id_type=MESH,
        ).start()
    grad_out[:, pl.ds(pl.multiple_of(en * half + gx * chunk, LANES), chunk)] = total[...]

    sent(y_recv, ny - 1, 0)
    sent(x_recv, nx - 1, 1)
    sent(z_recv, nx - 1, 2)
    sent(yb_recv, ny - 1, 3)
    sent(xb_recv, nx - 1, 4)
    sent(p_recv, nx - 1, 5)
    sent(e_recv, nx - 1, 8)
    sent(g_recv, ny - 1, 6)
    to_mate.wait_send()

    rest = grad_out.at[:, pl.ds(0, len(peers) * chunk)]
    pltpu.make_async_copy(rest, rest, ssem.at[7]).wait()
    pltpu.make_async_copy(rest, rest, rsem.at[7]).wait()


def store(state, adjoint, gradient, state_out, adjoint_out, grad_out, sem):
    moves = ((gradient, grad_out), (state, state_out), (adjoint, adjoint_out))
    copies = [pltpu.make_async_copy(m[0], m[1], sem.at[i]) for i, m in enumerate(moves)]
    for copy in copies:
        copy.start()
    for copy in copies:
        copy.wait()


def per_device(
    nx, ny, ne, concentration, cotangent, vel_x, vel_y, dispersion, wet_cells, decay_rate, emission,
    source_cell,
):
    nsrc = source_cell.shape[0]
    chunk = nsrc // (nx * ne)
    operands = [
        pltpu.with_memory_space_constraint(x, pltpu.HBM)
        for x in (
            decay_rate, concentration, cotangent, vel_x, vel_y, dispersion, wet_cells, emission,
            source_cell.reshape(nsrc // LANES, LANES),
        )
    ]
    width = TR * chunk // LANES
    square = pltpu.VMEM((CELLS, COLS), F32)
    block = pltpu.VMEM((ROWS, COLS), F32)

    def vmem(*shape, dtype=F32):
        return pltpu.VMEM(shape, dtype)

    index = vmem(nsrc // LANES, LANES, dtype=jnp.int32)
    ends = vmem(8 + 8 * max(nx, ny), LANES)
    scratch = [
        pltpu.SMEM((TR,), F32), block, block, block, vmem(ROWS, COLS, dtype=jnp.int32),
        vmem(TR, ROWS, COLS), vmem(TR, ROWS, COLS), vmem(TR, nsrc), index,
        square, square, square, square, square, square, square, square, square,
        vmem(COLS, nsrc, dtype=BF16), index, index, index,
        vmem(8, LANES), vmem(ny, 8, LANES), vmem(32, LANES), vmem(nx, 32, LANES),
        vmem(8, LANES), vmem(nx, 8, LANES), vmem(8, LANES), vmem(ny, 8, LANES), ends, ends,
        vmem(nx, 2 * width, LANES), vmem(nx, 2 * width, LANES),
        vmem(8, LANES), vmem(nx, 8, LANES), vmem(nx, width, LANES), vmem(nx, width, LANES),
        vmem(width, LANES), vmem(ny, width, LANES), vmem(TR, chunk),
        pltpu.SemaphoreType.DMA((9,)),
        pltpu.SemaphoreType.DMA((1,)), pltpu.SemaphoreType.DMA((1,)),
        pltpu.SemaphoreType.DMA((9,)), pltpu.SemaphoreType.DMA((9,)),
    ]
    hbm = pl.BlockSpec(memory_space=pl.ANY)
    on_chip = pl.BlockSpec(memory_space=pltpu.VMEM)
    state, adjoint, gradient = pl.pallas_call(
        functools.partial(kernel, nx, ny, ne, nsrc),
        out_shape=(
            jax.ShapeDtypeStruct((CELLS, COLS), F32),
            jax.ShapeDtypeStruct((CELLS, COLS), F32),
            jax.ShapeDtypeStruct(emission.shape, F32),
        ),
        in_specs=[hbm] * 9,
        out_specs=(on_chip, on_chip, on_chip),
        scratch_shapes=scratch,
        compiler_params=pltpu.CompilerParams(
            collective_id=0, has_side_effects=True, vmem_limit_bytes=VMEM_BYTES
        ),
        name="adi_step",
    )(*operands)
    shape = concentration.shape
    return pl.pallas_call(
        store,
        out_shape=(
            jax.ShapeDtypeStruct(shape, F32),
            jax.ShapeDtypeStruct(shape, F32),
            jax.ShapeDtypeStruct(emission.shape, F32),
        ),
        in_specs=[on_chip] * 3,
        out_specs=(hbm, hbm, hbm),
        scratch_shapes=[pltpu.SemaphoreType.DMA((3,))],
        compiler_params=pltpu.CompilerParams(vmem_limit_bytes=VMEM_BYTES),
        name="store",
    )(state.reshape(shape), adjoint.reshape(shape), gradient)


VMEM_BYTES = 32 * 1024 * 1024


def solution(mesh):
    nx, ny, ne = (mesh.shape[a] for a in ("gx", "gy", "ens"))
    field = P("ens", None, "gx", "gy")
    plane = P("gx", "gy")
    return jax.shard_map(
        functools.partial(per_device, nx, ny, ne),
        mesh=mesh,
        in_specs=(field, field, plane, plane, plane, plane, P(), P(), P()),
        out_specs=(field, field, P()),
        check_vma=False,
    )
```

```python
import functools

import jax
import jax.numpy as jnp
from jax import lax
from jax.experimental import pallas as pl
from jax.experimental.pallas import tpu as pltpu
from jax.sharding import PartitionSpec as P

MESH = pl.DeviceIdType.MESH
TR, ROWS, COLS, LANES, Q = 4, 32, 128, 128, 16
CELLS = TR * ROWS
F32, BF16 = jnp.float32, jnp.bfloat16
TILES = 8


def rolled(x, shift):
    n = x.shape[0]
    shift = shift % n
    if shift == 0:
        return x
    if shift % 8 == 0:
        return jnp.concatenate([x[n - shift :], x[: n - shift]], axis=0)
    return pltpu.roll(x, shift, 0)


def wrapped(i, n):
    return i & (n - 1) if n & (n - 1) == 0 else lax.rem(i, n)


def farthest_first(n):
    return sorted(range(1, n), key=lambda o: (-min(o, n - o), o))


def plane_order(n):
    far = (0, 1, 2, 1)
    return sorted(range(1, n), key=lambda o: -(far[o % 4] + far[o // 4 % 4]))


def pcr_factor(below, center, above, count, unit):
    steps, stride = [], 1
    while stride < count:
        k = stride * unit
        inverse = 1.0 / center
        alpha = -below * rolled(inverse, k)
        gamma = -above * rolled(inverse, -k)
        center = center + alpha * rolled(above, k) + gamma * rolled(below, -k)
        below, above = alpha * rolled(below, k), gamma * rolled(above, -k)
        steps.append((k, alpha, gamma))
        stride *= 2
    return steps, 1.0 / center


def pcr_apply(factors, side):
    steps, inverse = factors
    for k, alpha, gamma in steps:
        side = side + alpha * rolled(side, k) + gamma * rolled(side, -k)
    return side * inverse


class Line:
    def __init__(self, size):
        self.size = size
        sub = lax.broadcasted_iota(jnp.int32, (8, LANES), 0) % size
        self.first = sub == 0
        self.last = sub == size - 1

    def extended(self, cells):
        head = jnp.where(self.first, 0.0, rolled(cells[-1], 1))
        tail = jnp.where(self.last, 0.0, rolled(cells[0], -1))
        return [head] + cells + [tail]

    def bands(self, vel, disp, wet, half_decay):
        vel, disp, wet = (self.extended(cells) for cells in (vel, disp, wet))
        gate = [wet[k] * wet[k + 1] for k in range(Q + 1)]
        flux = [0.5 * (disp[k] + disp[k + 1]) * gate[k] for k in range(Q + 1)]
        plus = [jnp.maximum(v, 0.0) for v in vel]
        minus = [jnp.maximum(-v, 0.0) for v in vel]
        fwd_below = [-(flux[q] + plus[q + 1] * gate[q]) for q in range(Q)]
        fwd_above = [-(flux[q + 1] + minus[q + 1] * gate[q + 1]) for q in range(Q)]
        adj_below = [-(flux[q] + minus[q] * gate[q]) for q in range(Q)]
        adj_above = [-(flux[q + 1] + plus[q + 2] * gate[q + 1]) for q in range(Q)]
        center = [
            (1.0 + flux[q] + flux[q + 1] + plus[q + 1] * gate[q] + minus[q + 1] * gate[q + 1])
            + half_decay
            for q in range(Q)
        ]
        inverse = [1.0 / center[0]]
        for q in range(1, Q - 1):
            pivot = center[q] - fwd_below[q] * fwd_above[q - 1] * inverse[q - 1]
            inverse.append(1.0 / pivot)
        forward = self.factor(fwd_below, center, fwd_above, inverse)
        adjoint = self.factor(adj_below, center, adj_above, inverse)
        return forward, adjoint

    def factor(self, below, center, above, inverse):
        e = Q - 1
        fa = dict(inverse=inverse, below_end=below[e], above_end=above[e])
        fa["mult"] = mult = [None] + [below[q] * inverse[q - 1] for q in range(1, e)]
        fa["up"] = up = [above[q] * inverse[q] for q in range(e)]
        start = [-below[0]]
        for q in range(1, e):
            start.append(-mult[q] * start[q - 1])
        v, w = [None] * e, [None] * e
        v[e - 1] = start[e - 1] * inverse[e - 1]
        w[e - 1] = -up[e - 1]
        for q in range(e - 2, -1, -1):
            v[q] = start[q] * inverse[q] - up[q] * v[q + 1]
            w[q] = -up[q] * w[q + 1]
        fa["v"], fa["w"] = v, w
        fa["reduced"] = pcr_factor(
            below[e] * v[e - 1],
            center[e] + below[e] * w[e - 1] + above[e] * rolled(v[0], -1),
            above[e] * rolled(w[0], -1),
            self.size,
            1,
        )
        head = jnp.where(self.first, 1.0, 0.0)
        fa["from_first"] = self.solve(fa, [head] + [None] * e)
        fa["from_last"] = self.solve(fa, [None] * e + [jnp.where(self.last, 1.0, 0.0)])
        return fa

    def solve(self, fa, field):
        def plus(a, b):
            return b if a is None else a if b is None else a + b

        def times(a, b):
            return None if b is None else a * b

        e = Q - 1
        g = [field[0]]
        for q in range(1, e):
            g.append(plus(field[q], times(-fa["mult"][q], g[q - 1])))
        part = [None] * e
        part[e - 1] = times(fa["inverse"][e - 1], g[e - 1])
        for q in range(e - 2, -1, -1):
            part[q] = plus(times(fa["inverse"][q], g[q]), times(-fa["up"][q], part[q + 1]))
        side = plus(field[e], times(-fa["below_end"], part[e - 1]))
        if part[0] is not None:
            side = side - fa["above_end"] * rolled(part[0], -1)
        ends = pcr_apply(fa["reduced"], side)
        before = rolled(ends, 1)
        return [
            plus(part[q], fa["v"][q] * before + fa["w"][q] * ends) for q in range(e)
        ] + [ends]

    def finish(self, fa, part, head, tail):
        first, last = fa["from_first"], fa["from_last"]
        return [part[q] + first[q] * head + last[q] * tail for q in range(Q)]

    def edges(self, cells):
        return jnp.where(self.last, cells[Q - 1], cells[0])


def faces(plus_first, disp_first, minus_last, disp_last, index, count):
    disp_next = rolled(disp_first, -1)
    shut = (index == count - 1) | (disp_last <= 0.0) | (disp_next <= 0.0)
    flux = 0.5 * (disp_last + disp_next)
    return (
        jnp.where(shut, 0.0, flux + minus_last),
        jnp.where(shut, 0.0, flux + rolled(plus_first, -1)),
    )


def kernel(
    nx, ny, ne, nsrc,
    decay_in, conc, cot, vel_x, vel_y, disp, wet_cells, emission, cells,
    state_out, adjoint_out, grad_out,
    decay, f_vx, f_vy, f_disp, f_wet, f_conc, f_cot, f_emis, f_cells,
    vel_t, disp_t, wet_t, work, work_t, adjoint_v, mate_v, first_v, last_v,
    onehot, rows_v, cols_v, owner_v,
    y_send, y_recv, x_send, x_recv, xb_send, xb_recv, yb_send, yb_recv, ends_a, ends_b,
    z_send, z_recv, e_send, e_recv, p_send, p_recv, g_send, g_recv, total,
    in_sem, mate_ssem, mate_rsem, ssem, rsem,
):
    gx, gy, en = lax.axis_index("gx"), lax.axis_index("gy"), lax.axis_index("ens")
    half = nsrc // ne
    chunk = half // nx
    tiles = chunk // LANES
    half_tiles = half // LANES
    mate = (gx, gy, wrapped(en + 1, ne))
    assert tiles == 2

    loads = [
        pltpu.make_async_copy(src, dst, in_sem.at[i])
        for i, (src, dst) in enumerate(
            [
                (vel_y, f_vy), (disp, f_disp), (wet_cells, f_wet), (cot.at[0], f_cot),
                (vel_x, f_vx), (cells, f_cells), (emission, f_emis), (conc.at[0], f_conc),
                (decay_in, decay),
            ]
        )
    ]

    def line_peer(o):
        return (gx, wrapped(gy + o, ny), en)

    def x_peer(o):
        return (gx ^ o, gy, en)

    def mate_peer(o):
        return (gx ^ o, gy, mate[2])

    barrier = pltpu.get_barrier_semaphore()
    greeted = [line_peer(o) for o in farthest_first(ny)]
    greeted += [peer(o) for o in plane_order(nx) for peer in (x_peer, mate_peer)] + [mate]
    for i, peer in enumerate(greeted):
        pl.semaphore_signal(barrier, inc=1, device_id=peer, device_id_type=MESH)
        if i == 2:
            for load in loads[:5]:
                load.start()
    for load in loads[5:]:
        load.start()

    def to_line(send, recv, slot):
        for o in farthest_first(ny):
            pltpu.make_async_remote_copy(
                src_ref=send, dst_ref=recv.at[gy], send_sem=ssem.at[slot],
                recv_sem=rsem.at[slot], device_id=line_peer(o), device_id_type=MESH,
            ).start()
        recv[gy] = send[...]

    def to_x(send, recv, slot):
        for o in plane_order(nx):
            pltpu.make_async_remote_copy(
                src_ref=send, dst_ref=recv.at[gx], send_sem=ssem.at[slot],
                recv_sem=rsem.at[slot], device_id=x_peer(o), device_id_type=MESH,
            ).start()
        recv[gx] = send[...]

    def to_each_x(send, recv, slot):
        for o in plane_order(nx):
            peer = gx ^ o
            pltpu.make_async_remote_copy(
                src_ref=send.at[peer], dst_ref=recv.at[gx], send_sem=ssem.at[slot],
                recv_sem=rsem.at[slot], device_id=x_peer(o), device_id_type=MESH,
            ).start()
        recv[gx] = send[gx]

    def arrived(recv, count, slot):
        part = recv.at[pl.ds(0, count)]
        pltpu.make_async_copy(part, part, rsem.at[slot]).wait()

    def sent(recv, count, slot):
        part = recv.at[pl.ds(0, count)]
        pltpu.make_async_copy(part, part, ssem.at[slot]).wait()

    def strided(ref, q):
        return ref[pl.ds(q, 8, stride=Q), :]

    def column(ref):
        return [strided(ref, q) for q in range(Q)]

    def put(ref, cells_):
        for q in range(Q):
            ref[pl.ds(q, 8, stride=Q), :] = cells_[q]

    y_line, x_line = Line(8), Line(2)
    zero8 = jnp.zeros((8, LANES), F32)
    lane_tracer = lax.broadcasted_iota(jnp.int32, (8, LANES), 1) // ROWS
    sub_tracer = lax.broadcasted_iota(jnp.int32, (8, LANES), 0) // 2

    def half_decay(tracer):
        value = jnp.full((8, LANES), decay[TR - 1], F32)
        for t in range(TR - 1):
            value = jnp.where(tracer == t, decay[t], value)
        return 0.5 * value

    for i in (8, 0, 1, 2, 3):
        loads[i].wait()
    wet_f = f_wet[...].astype(F32)
    for field, ref in ((f_vy[...], vel_t), (f_disp[...], disp_t), (wet_f, wet_t)):
        ref[...] = jnp.transpose(jnp.concatenate([field] * TR, axis=0))
    work_t[...] = jnp.transpose(f_cot[...].reshape(CELLS, COLS))
    y_fwd, y_adj = y_line.bands(
        column(vel_t), column(disp_t), column(wet_t), half_decay(lane_tracer)
    )
    y_part = y_line.solve(y_adj, column(work_t))
    end = COLS - 1
    tracer_row = lane_tracer[0:1]
    packed = jnp.where(
        tracer_row == 0,
        jnp.maximum(vel_t[0:1, :], 0.0),
        jnp.where(
            tracer_row == 1,
            disp_t[0:1, :] * wet_t[0:1, :],
            jnp.where(
                tracer_row == 2,
                jnp.maximum(-vel_t[end : end + 1, :], 0.0),
                disp_t[end : end + 1, :] * wet_t[end : end + 1, :],
            ),
        ),
    )
    e = Q - 1
    for i, row in enumerate(
        (
            y_part[0][0:1], y_part[e][7:8], y_fwd["from_first"][0][0:1],
            y_fwd["from_last"][e][7:8], y_fwd["from_last"][0][0:1],
            y_fwd["from_first"][e][7:8], packed, zero8[0:1],
        )
    ):
        y_send[i : i + 1, :] = row

    loads[4].wait()

    def spread(ref, as_float):
        out = []
        for q in range(Q):
            value = jnp.where(x_line.first, ref[q : q + 1, :], ref[q + Q : q + Q + 1, :])
            out.append(value.astype(F32) if as_float else value)
        return out

    x_fwd, x_adj = x_line.bands(
        spread(f_vx, False), spread(f_disp, False), spread(f_wet, True), half_decay(sub_tracer)
    )
    put(first_v, x_adj["from_first"])
    put(last_v, x_adj["from_last"])

    loads[5].wait()
    shift = (ny * COLS).bit_length() - 1
    source = f_cells[...]
    row = lax.shift_right_logical(source, shift)
    owner_v[...] = lax.shift_right_logical(row, ROWS.bit_length() - 1)
    rows_v[...] = row - gx * ROWS
    cols_v[...] = (source & (ny * COLS - 1)) - gy * COLS
    row_iota = lax.broadcasted_iota(jnp.int32, (ROWS, LANES), 0)
    col_iota = lax.broadcasted_iota(jnp.int32, (COLS, LANES), 0)

    def lanes(tile, count):
        return pl.ds(pl.multiple_of(tile * LANES, LANES), count * LANES)

    loads[6].wait()

    def scatter(step, acc):
        base = pl.multiple_of(step * TILES, TILES)
        row_tile = rows_v[pl.ds(base, TILES), :]
        col_tile = cols_v[pl.ds(base, TILES), :]
        values = f_emis[:, lanes(base, TILES)]
        high = values.astype(BF16).astype(F32)
        low = values - high
        left, hots = [], []
        for i in range(TILES):
            mask = row_iota == row_tile[i : i + 1, :]
            part = slice(i * LANES, (i + 1) * LANES)
            left.append(
                jnp.concatenate(
                    [
                        jnp.where(mask, piece[t : t + 1, part], 0.0).astype(BF16)
                        for piece in (high, low)
                        for t in range(TR)
                    ],
                    axis=0,
                )
            )
            hots.append(jnp.where(col_iota == col_tile[i : i + 1, :], 1.0, 0.0).astype(BF16))
        hot = jnp.concatenate(hots, axis=1)
        onehot[:, lanes(base, TILES)] = hot
        return acc + lax.dot_general(
            jnp.concatenate(left, axis=1),
            hot,
            (((1,), (1,)), ((), ())),
            preferred_element_type=F32,
        )

    placed = lax.fori_loop(
        0, nsrc // LANES // TILES, scatter, jnp.zeros((2 * CELLS, COLS), F32)
    )
    loads[7].wait()
    work[...] = f_conc[...].reshape(CELLS, COLS) + (placed[:CELLS] + placed[CELLS:])
    fx_part = x_line.solve(x_fwd, column(work))
    x_send[0:8, :] = x_line.edges(fx_part)
    x_send[8:16, :] = jnp.where(x_line.last, x_fwd["from_last"][e], x_fwd["from_first"][0])
    x_send[16:24, :] = jnp.where(x_line.last, x_fwd["from_first"][e], x_fwd["from_last"][0])
    x_send[24:25, :] = jnp.maximum(f_vx[0:1, :], 0.0)
    x_send[25:26, :] = f_disp[0:1, :] * wet_f[0:1, :]
    x_send[26:27, :] = jnp.maximum(-f_vx[ROWS - 1 : ROWS, :], 0.0)
    x_send[27:28, :] = f_disp[ROWS - 1 : ROWS, :] * wet_f[ROWS - 1 : ROWS, :]
    x_send[28:32, :] = zero8[0:4]
    ends_a[0:8, :] = zero8
    ends_b[0:8, :] = zero8

    pl.semaphore_wait(barrier, len(greeted))
    to_line(y_send, y_recv, 0)
    to_x(x_send, x_recv, 1)

    def split_bf16(values):
        high = values.astype(BF16)
        return jnp.concatenate([high, (values - high.astype(F32)).astype(BF16)], axis=1)

    sub = lax.broadcasted_iota(jnp.int32, (8, LANES), 0)

    def folded(parts):
        for bit in (1, 2, 4):
            keep = (sub & bit) == 0
            parts = [
                jnp.where(keep, a, b) + pltpu.roll(jnp.where(keep, b, a), bit, 0)
                for a, b in zip(parts[0::2], parts[1::2])
            ]
        return parts[0]

    def pick(fields, send, at, unrolled):
        left = jnp.concatenate([split_bf16(field) for field in fields], axis=0)
        per_step = min(TILES, half_tiles)

        def go(step, _):
            base = pl.multiple_of(en * half_tiles + step * per_step, per_step)
            row_tile = rows_v[pl.ds(base, per_step), :]
            hot = onehot[:, lanes(base, per_step)]
            found = jnp.dot(left, jnp.concatenate([hot, hot], axis=0), preferred_element_type=F32)
            masks = [row_iota == row_tile[i : i + 1, :] for i in range(per_step)]
            for pair in range(per_step // 2):
                for k, first in enumerate(at):
                    parts = []
                    for t in range(TR):
                        for i in (2 * pair, 2 * pair + 1):
                            start = (k * TR + t) * ROWS
                            line = found[start : start + ROWS, i * LANES : (i + 1) * LANES]
                            line = jnp.where(masks[i], line, 0.0)
                            parts.append((line[0:8] + line[8:16]) + (line[16:24] + line[24:32]))
                    send[step * (per_step // 2) + pair, first : first + 8, :] = folded(parts)
            return 0

        if unrolled:
            steps, blocks = half_tiles // per_step, per_step // tiles
            order = plane_order(steps) + [0]
            middle = steps // 2
            for group in (order[:middle], order[middle:]):
                for far in group:
                    go((gx // blocks) ^ far, 0)
                for near in plane_order(blocks) + [0]:
                    for o in [far * blocks + near for far in group]:
                        if o:
                            pltpu.make_async_remote_copy(
                                src_ref=p_send.at[gx ^ o], dst_ref=p_recv.at[gx],
                                send_sem=ssem.at[5], recv_sem=rsem.at[5],
                                device_id=x_peer(o), device_id_type=MESH,
                            ).start()
            p_recv[gx] = p_send[gx]
        else:
            lax.fori_loop(0, half_tiles // per_step, go, 0)

    pick((first_v[...], last_v[...]), z_send, (0, TR * tiles), False)
    to_each_x(z_send, z_recv, 2)

    def x_piece(ref, k):
        return jnp.concatenate([ref[d, 8 * k : 8 * k + 8, :] for d in range(nx)], axis=0)

    def single(ref, k, n):
        return jnp.concatenate([ref[d, k : k + 1, :] for d in range(n)], axis=0)

    def expanded(rows):
        return jnp.concatenate(
            [jnp.broadcast_to(rows[d : d + 1], (8, LANES)) for d in range(nx)], axis=0
        )

    def from_next(value):
        later = rolled(value, -8)
        return jnp.concatenate([rolled(later[8 * d : 8 * d + 8], 1) for d in range(nx)], axis=0)

    def own_x(ref, at):
        block = ref[pl.ds(pl.multiple_of(8 * at, 8), 8), :]
        return jnp.where(x_line.last, block, rolled(block, -1))

    arrived(y_recv, ny - 1, 0)
    raw = single(y_recv, 6, ny)
    tracer_n = jnp.broadcast_to(tracer_row, (ny, LANES))
    quantities = []
    for k in range(4):
        value = jnp.where(tracer_n == k, raw, 0.0)
        value = value + pltpu.roll(value, ROWS, 1)
        quantities.append(value + pltpu.roll(value, 2 * ROWS, 1))
    index = lax.broadcasted_iota(jnp.int32, (ny, LANES), 0)
    y_before, y_after = faces(*quantities, index, ny)
    g00, gnn, g0n, gn0 = (single(y_recv, k, ny) for k in (2, 3, 4, 5))
    y_below = -gn0 * rolled(y_after, 1)
    y_center = 1.0 + gnn * y_before + rolled(g00, -1) * y_after
    y_above = jnp.where(index == ny - 1, 0.0, -rolled(g0n * y_before, -1))
    y_factors = pcr_factor(rolled(y_above, 1), y_center, rolled(y_below, -1), ny, 1)
    ends_a[8 : 8 + ny, :] = pcr_apply(
        y_factors, y_before * single(y_recv, 1, ny) - y_after * rolled(single(y_recv, 0, ny), -1)
    )
    head, tail = ends_a[pl.ds(7 + gy, 1), :], -ends_a[pl.ds(8 + gy, 1), :]
    put(work_t, y_line.finish(y_adj, y_part, head, tail))
    work[...] = jnp.transpose(work_t[...])
    ax_part = x_line.solve(x_adj, column(work))
    put(adjoint_v, ax_part)
    to_mate = pltpu.make_async_remote_copy(
        src_ref=adjoint_v, dst_ref=mate_v, send_sem=mate_ssem.at[0], recv_sem=mate_rsem.at[0],
        device_id=mate, device_id_type=MESH,
    )
    to_mate.start()
    xb_send[...] = x_line.edges(ax_part)

    to_mate.wait_recv()
    first_sum, last_sum = (strided(adjoint_v, q) + strided(mate_v, q) for q in (0, e))
    e_send[...] = jnp.where(x_line.last, last_sum, first_sum)
    to_x(e_send, e_recv, 8)
    both = adjoint_v[...] + mate_v[...]
    pick((both,), p_send, (0,), True)
    to_x(xb_send, xb_recv, 4)

    arrived(x_recv, nx - 1, 1)
    index = lax.broadcasted_iota(jnp.int32, (nx, LANES), 0)
    x_before, x_after = (
        expanded(face) for face in faces(*[single(x_recv, 24 + k, nx) for k in range(4)], index, nx)
    )
    diagonal, corner = x_piece(x_recv, 1), x_piece(x_recv, 2)
    x_below = -corner * rolled(x_after, 8)
    x_center = 1.0 + diagonal * x_before + from_next(diagonal) * x_after
    block_index = lax.broadcasted_iota(jnp.int32, (8 * nx, LANES), 0) // 8
    x_above = jnp.where(
        block_index == nx - 1, 0.0, -from_next(corner) * rolled(x_before, -8)
    )
    terms = x_piece(x_recv, 0)
    jump = pcr_apply(pcr_factor(x_below, x_center, x_above, nx, 8), terms - from_next(terms))
    ends_a[8 : 8 + 8 * nx, :] = x_after * jump
    ends_b[8 : 8 + 8 * nx, :] = x_before * jump
    put(work, x_line.finish(x_fwd, fx_part, own_x(ends_a, gx), -own_x(ends_b, gx + 1)))
    work_t[...] = jnp.transpose(work[...])
    fy_part = y_line.solve(y_fwd, column(work_t))
    yb_send[0:1, :] = fy_part[0][0:1]
    yb_send[1:2, :] = fy_part[e][7:8]
    yb_send[2:8, :] = zero8[0:6]
    to_line(yb_send, yb_recv, 3)
    x_factors = pcr_factor(rolled(x_above, 8), x_center, rolled(x_below, -8), nx, 8)

    y_fwd_factors = pcr_factor(y_below, y_center, y_above, ny, 1)
    arrived(z_recv, nx - 1, 2)

    def summed(ref, first, count, n):
        value = ref[0, first : first + count, :]
        for i in range(1, n):
            value = value + ref[i, first : first + count, :]
        return value

    width = TR * tiles
    z_first, z_last = summed(z_recv, 0, width, nx), summed(z_recv, width, width, nx)

    arrived(e_recv, nx - 1, 8)

    def flux_of(ref):
        terms = x_piece(ref, 0)
        return pcr_apply(x_factors, x_before * terms - x_after * from_next(terms))

    flux = flux_of(e_recv)
    mine = pl.multiple_of(en * half_tiles + gx * tiles, tiles)
    hot = onehot[:, lanes(mine, tiles)]
    found = jnp.dot(
        split_bf16(flux), jnp.concatenate([hot, hot], axis=0), preferred_element_type=F32
    )
    owner = owner_v[pl.ds(mine, tiles), :]
    for i in range(tiles):
        into, out = zero8, zero8
        for d in range(nx):
            value = found[8 * d : 8 * d + 8, i * LANES : (i + 1) * LANES]
            into = into + jnp.where(owner[i : i + 1, :] == d + 1, value, 0.0)
            out = out + jnp.where(owner[i : i + 1, :] == d, value, 0.0)
        for t in range(TR):
            spot = slice(tiles * t + i, tiles * t + i + 1)
            at = slice(2 * t + 1, 2 * t + 2)
            g_send[spot, :] = z_first[spot] * into[at] - z_last[spot] * out[at]
    arrived(p_recv, nx - 1, 5)
    g_send[...] = g_send[...] + summed(p_recv, 0, width, nx)
    to_line(g_send, g_recv, 6)

    arrived(xb_recv, nx - 1, 4)
    ends_a[8 : 8 + 8 * nx, :] = flux_of(xb_recv)
    put(
        adjoint_out,
        x_line.finish(x_adj, column(adjoint_v), own_x(ends_a, gx), -own_x(ends_a, gx + 1)),
    )

    arrived(yb_recv, ny - 1, 3)
    jump = pcr_apply(
        y_fwd_factors, single(yb_recv, 1, ny) - rolled(single(yb_recv, 0, ny), -1)
    )
    ends_a[8 : 8 + ny, :] = y_after * jump
    ends_b[8 : 8 + ny, :] = y_before * jump
    head, tail = ends_a[pl.ds(7 + gy, 1), :], -ends_b[pl.ds(8 + gy, 1), :]
    put(work_t, y_line.finish(y_fwd, fy_part, head, tail))
    state_out[...] = jnp.transpose(work_t[...])

    arrived(g_recv, ny - 1, 6)
    sums = summed(g_recv, 0, width, ny)
    for t in range(TR):
        for i in range(tiles):
            total[t : t + 1, i * LANES : (i + 1) * LANES] = sums[tiles * t + i : tiles * t + i + 1]

    here = grad_out.at[:, pl.ds(pl.multiple_of(en * half + gx * chunk, LANES), chunk)]
    peers = [peer(o) for o in plane_order(nx) for peer in (x_peer, mate_peer)] + [mate]
    for peer in peers:
        pltpu.make_async_remote_copy(
            src_ref=total, dst_ref=here, send_sem=ssem.at[7], recv_sem=rsem.at[7],
            device_id=peer, device_id_type=MESH,
        ).start()
    grad_out[:, pl.ds(pl.multiple_of(en * half + gx * chunk, LANES), chunk)] = total[...]

    sent(y_recv, ny - 1, 0)
    sent(x_recv, nx - 1, 1)
    sent(z_recv, nx - 1, 2)
    sent(yb_recv, ny - 1, 3)
    sent(xb_recv, nx - 1, 4)
    sent(p_recv, nx - 1, 5)
    sent(e_recv, nx - 1, 8)
    sent(g_recv, ny - 1, 6)
    to_mate.wait_send()

    rest = grad_out.at[:, pl.ds(0, len(peers) * chunk)]
    pltpu.make_async_copy(rest, rest, ssem.at[7]).wait()
    pltpu.make_async_copy(rest, rest, rsem.at[7]).wait()


def store(state, adjoint, gradient, state_out, adjoint_out, grad_out, sem):
    moves = ((gradient, grad_out), (state, state_out), (adjoint, adjoint_out))
    copies = [pltpu.make_async_copy(m[0], m[1], sem.at[i]) for i, m in enumerate(moves)]
    for copy in copies:
        copy.start()
    for copy in copies:
        copy.wait()


def per_device(
    nx, ny, ne, concentration, cotangent, vel_x, vel_y, dispersion, wet_cells, decay_rate, emission,
    source_cell,
):
    nsrc = source_cell.shape[0]
    chunk = nsrc // (nx * ne)
    operands = [
        pltpu.with_memory_space_constraint(x, pltpu.HBM)
        for x in (
            decay_rate, concentration, cotangent, vel_x, vel_y, dispersion, wet_cells, emission,
            source_cell.reshape(nsrc // LANES, LANES),
        )
    ]
    width = TR * chunk // LANES
    square = pltpu.VMEM((CELLS, COLS), F32)
    block = pltpu.VMEM((ROWS, COLS), F32)

    def vmem(*shape, dtype=F32):
        return pltpu.VMEM(shape, dtype)

    index = vmem(nsrc // LANES, LANES, dtype=jnp.int32)
    ends = vmem(8 + 8 * max(nx, ny), LANES)
    scratch = [
        pltpu.SMEM((TR,), F32), block, block, block, vmem(ROWS, COLS, dtype=jnp.int32),
        vmem(TR, ROWS, COLS), vmem(TR, ROWS, COLS), vmem(TR, nsrc), index,
        square, square, square, square, square, square, square, square, square,
        vmem(COLS, nsrc, dtype=BF16), index, index, index,
        vmem(8, LANES), vmem(ny, 8, LANES), vmem(32, LANES), vmem(nx, 32, LANES),
        vmem(8, LANES), vmem(nx, 8, LANES), vmem(8, LANES), vmem(ny, 8, LANES), ends, ends,
        vmem(nx, 2 * width, LANES), vmem(nx, 2 * width, LANES),
        vmem(8, LANES), vmem(nx, 8, LANES), vmem(nx, width, LANES), vmem(nx, width, LANES),
        vmem(width, LANES), vmem(ny, width, LANES), vmem(TR, chunk),
        pltpu.SemaphoreType.DMA((9,)),
        pltpu.SemaphoreType.DMA((1,)), pltpu.SemaphoreType.DMA((1,)),
        pltpu.SemaphoreType.DMA((9,)), pltpu.SemaphoreType.DMA((9,)),
    ]
    hbm = pl.BlockSpec(memory_space=pl.ANY)
    on_chip = pl.BlockSpec(memory_space=pltpu.VMEM)
    state, adjoint, gradient = pl.pallas_call(
        functools.partial(kernel, nx, ny, ne, nsrc),
        out_shape=(
            jax.ShapeDtypeStruct((CELLS, COLS), F32),
            jax.ShapeDtypeStruct((CELLS, COLS), F32),
            jax.ShapeDtypeStruct(emission.shape, F32),
        ),
        in_specs=[hbm] * 9,
        out_specs=(on_chip, on_chip, on_chip),
        scratch_shapes=scratch,
        compiler_params=pltpu.CompilerParams(
            collective_id=0, has_side_effects=True, vmem_limit_bytes=VMEM_BYTES
        ),
        name="adi_step",
    )(*operands)
    shape = concentration.shape
    return pl.pallas_call(
        store,
        out_shape=(
            jax.ShapeDtypeStruct(shape, F32),
            jax.ShapeDtypeStruct(shape, F32),
            jax.ShapeDtypeStruct(emission.shape, F32),
        ),
        in_specs=[on_chip] * 3,
        out_specs=(hbm, hbm, hbm),
        scratch_shapes=[pltpu.SemaphoreType.DMA((3,))],
        compiler_params=pltpu.CompilerParams(vmem_limit_bytes=VMEM_BYTES),
        name="store",
    )(state.reshape(shape), adjoint.reshape(shape), gradient)


VMEM_BYTES = 32 * 1024 * 1024


def solution(mesh):
    nx, ny, ne = (mesh.shape[a] for a in ("gx", "gy", "ens"))
    field = P("ens", None, "gx", "gy")
    plane = P("gx", "gy")
    return jax.shard_map(
        functools.partial(per_device, nx, ny, ne),
        mesh=mesh,
        in_specs=(field, field, plane, plane, plane, plane, P(), P(), P()),
        out_specs=(field, field, P()),
        check_vma=False,
    )
```
